32 devices in a mesh: round: 4 (over y, x), bucket: 8 (over z, core).
Axes of the slice: x: 2, y: 2, z: 4, core: 2. Of those that a mesh axis runs over, the one named last changes fastest.
Arguments:
- x_start: float32 [4, 4096, 512], P('round', 'bucket'), may hold values from 0 to 1
- y_start: float32 [4, 4096, 512], P('round', 'bucket'), may hold values from 0 to 1
- bucket_payoff: bfloat16 [4, 4096, 4096], P('round', 'bucket'), may hold values from -0.09375 to 0.09375
- column_blocks: int32 [4, 4, 3], P('round'), may hold values from 0 to 3
- public_coef: float32 [4, 4, 3, 128, 128], P('round'), may hold values from -0.3125 to 0.3125
- predecessor_sequences: int32 [3, 256], replicated, may hold values from 0 to 511, as said below
Outputs:
- x_final: float32 [4, 4096, 512], P('round', 'bucket')
- y_final: float32 [4, 4096, 512], P('round', 'bucket')
The draws below stay inside these ranges and needn't reach their ends.
Inputs may be any that keep to these rules, and one draw needn't show every extreme that they name: `predecessor_sequences`: each row names 256 distinct sequences of the previous round.
All inputs are finite; a program needn't handle non-finite values.
Results may differ from the reference program's by a relative error of at most 0.013.
The reference program's roundings to bfloat16 on the way (of `mixed_y` and `mixed_x`) count: a program that leaves them out, or rounds other values in their place, can miss the bound.
Values may be sent and summed in bfloat16 or wider, within the bound.
A program may use at most 64 MiB of HBM per device.

```python
import jax
import jax.numpy as jnp
from jax import lax

K = 4096
S = 512
PB = 128
NBR = 3
ROUNDS = 4
SB = 4
HALF = 256


def draw_predecessor_sequences(key, part):
    row_keys = jax.random.split(key, ROUNDS - 1)

    def one_row(row_key):
        return jax.random.permutation(row_key, S)[:HALF]
    return jax.vmap(one_row)(row_keys).astype(jnp.int32)


def with_ends(values, stream_key, least, largest):
    place = [jax.random.randint(jax.random.fold_in(stream_key, axis), (), 0, length) for axis, length in enumerate(values.shape)]
    main_axis = values.shape.index(max(values.shape))
    beside = place[:main_axis] + [(place[main_axis] + 1) % values.shape[main_axis]] + place[main_axis + 1:]
    return values.at[tuple(place)].set(least).at[tuple(beside)].set(largest)


def shard_levels(key, extent, shards, low, top_value):
    def one(dim, parts):
        draws = jax.random.uniform(jax.random.fold_in(jax.random.fold_in(key, 6), dim), (parts,), jnp.float32, low / len(shards), top_value / len(shards))
        return jnp.repeat(jnp.exp(draws), extent[dim] // parts).reshape((-1,) + (1,) * (len(extent) - dim - 1))

    gain = one(*shards[0])
    for cut in shards[1:]:
        gain = gain * one(*cut)
    return gain


def normal_values(rng, shape, width, reach, pieces=(), kind=jnp.bfloat16):
    factor_of = shard_levels(rng, shape, pieces, -0.22, 0.18) if pieces else 1.0
    result = jax.random.normal(rng, shape, jnp.float32) * width * factor_of
    return jnp.minimum(jnp.maximum(result, -reach), reach).astype(kind)


def setup_inputs(seed: int = 0) -> dict:
    key_list = jax.random.split(jax.random.key(seed), 7)
    x_start = jnp.clip(1.0 * jax.random.uniform(key_list[0], (ROUNDS, K, S), jnp.float32) ** shard_levels(key_list[0], (ROUNDS, K, S), ((0, 4), (1, 8)), -0.2, 0.2), 0.0, 1.0)
    y_start = jnp.clip(1.0 * jax.random.uniform(key_list[1], (ROUNDS, K, S), jnp.float32) ** shard_levels(key_list[1], (ROUNDS, K, S), ((0, 4), (1, 8)), -0.2, 0.2), 0.0, 1.0)
    bucket_payoff = normal_values(key_list[2], (ROUNDS, K, K), K ** -0.5, 0.09375, ((0, 4), (1, 8)))
    column_blocks = with_ends(jax.random.randint(key_list[3], (ROUNDS, SB, NBR), 0, SB), jax.random.fold_in(key_list[3], 1), 0, SB - 1).astype(jnp.int32)
    public_coef = normal_values(key_list[4], (ROUNDS, SB, NBR, PB, PB), (NBR * PB) ** -0.5, 0.3125, ((0, 4),), jnp.float32)
    predecessor_sequences = draw_predecessor_sequences(jax.random.fold_in(key_list[6], 71), 0)
    return dict(x_start=x_start, y_start=y_start, bucket_payoff=bucket_payoff, column_blocks=column_blocks, public_coef=public_coef, predecessor_sequences=predecessor_sequences)


smooth_x = 0.1
smooth_y = 0.1
epsilon = 1e-06
highest = lax.Precision.HIGHEST

def pair_lse(utility_vector):
    even_part = utility_vector[:, 0::2]
    odd_part = utility_vector[:, 1::2]
    larger = jnp.maximum(even_part, odd_part)
    return larger + jnp.log(jnp.exp(even_part - larger) + jnp.exp(odd_part - larger))

def pair_share(utility_vector, aggregated_normalizers, parent_mass):
    even_part = parent_mass * jnp.exp(utility_vector[:, 0::2] - aggregated_normalizers)
    odd_part = parent_mass * jnp.exp(utility_vector[:, 1::2] - aggregated_normalizers)
    return jnp.stack([even_part, odd_part], axis=-1).reshape(utility_vector.shape)

def nested_entropy_mapping(destination_strategy, entropy_weight, predecessor_sequences):
    round_total = destination_strategy.shape[0]
    pair_count = destination_strategy.shape[2] // 2
    divided_utilities = destination_strategy / entropy_weight
    score_list = [None] * round_total
    total_list = [None] * round_total
    for depth_level in reversed(range(round_total)):
        carried = jnp.zeros_like(divided_utilities[depth_level])
        if depth_level < round_total - 1:
            carried = carried.at[:, predecessor_sequences[depth_level]].set(total_list[depth_level + 1])
        score_list[depth_level] = divided_utilities[depth_level] + carried
        total_list[depth_level] = pair_lse(score_list[depth_level])
    masses = []
    previous = jnp.ones((divided_utilities.shape[1], destination_strategy.shape[2]), dtype=divided_utilities.dtype)
    for depth_level in range(round_total):
        if depth_level == 0:
            parent_rows = jnp.arange(pair_count, dtype=jnp.int32)
        else:
            parent_rows = predecessor_sequences[depth_level - 1]
        previous = pair_share(score_list[depth_level], total_list[depth_level], previous[:, parent_rows])
        masses.append(previous)
    return jnp.stack(masses)

def public_forward(strategy, columns, coefficients):
    tiled = strategy.reshape(strategy.shape[0], columns.shape[0], -1)
    picked = tiled[:, columns, :]
    mixed = jnp.einsum('kmtq,mtpq->kmp', picked, coefficients, precision=highest)
    return mixed.reshape(strategy.shape)

def public_backward(strategy, columns, coefficients):
    tiled = strategy.reshape(strategy.shape[0], columns.shape[0], -1)
    spread = jnp.einsum('kmp,mtpq->kmtq', tiled, coefficients, precision=highest)
    selector = (columns[:, :, None] == jnp.arange(columns.shape[0], dtype=jnp.int32)).astype(strategy.dtype)
    gathered = jnp.einsum('kmtq,mtc->kcq', spread, selector, precision=highest)
    return gathered.reshape(strategy.shape)

def reference(x_start, y_start, bucket_payoff, column_blocks, public_coef, predecessor_sequences):
    first_player = x_start
    second_player = y_start
    for step_index in range(2):
        weight_new = 2.0 / (step_index + 3.0)
        mixed_y = jnp.stack([public_forward(second_player[idx_round], column_blocks[idx_round], public_coef[idx_round]) for idx_round in range(ROUNDS)]).astype(jnp.bfloat16)
        grad_x = jnp.stack([jnp.dot(bucket_payoff[idx_round], mixed_y[idx_round], preferred_element_type=jnp.float32) for idx_round in range(ROUNDS)])
        temp_x = smooth_x * jnp.sqrt(jnp.mean(grad_x * grad_x) + epsilon)
        best_x = nested_entropy_mapping(-grad_x, temp_x, predecessor_sequences)
        first_player = (1.0 - weight_new) * first_player + weight_new * best_x
        mixed_x = jnp.stack([public_backward(first_player[idx_round], column_blocks[idx_round], public_coef[idx_round]) for idx_round in range(ROUNDS)]).astype(jnp.bfloat16)
        grad_y = jnp.stack([lax.dot_general(bucket_payoff[idx_round], mixed_x[idx_round], (((0,), (0,)), ((), ())), preferred_element_type=jnp.float32) for idx_round in range(ROUNDS)])
        temp_y = smooth_y * jnp.sqrt(jnp.mean(grad_y * grad_y) + epsilon)
        best_y = nested_entropy_mapping(grad_y, temp_y, predecessor_sequences)
        second_player = (1.0 - weight_new) * second_player + weight_new * best_y
    return (first_player, second_player)
```

```python
import functools
import types

import jax
import jax.numpy as jnp
from jax import lax
from jax.experimental import pallas as pl
from jax.experimental.pallas import tpu as pltpu
from jax.sharding import PartitionSpec as P

smooth_x = 0.1
smooth_y = 0.1
epsilon = 1e-06
highest = lax.Precision.HIGHEST
nn = (((1,), (0,)), ((), ()))
nt = (((1,), (1,)), ((), ()))


def exact(a, b, dims=nn):
    return lax.dot_general(a, b, dims, precision=highest, preferred_element_type=jnp.float32)


weights = (2.0 / 3.0, 2.0 / 4.0)
top_code = 65535.0
shift_code = 32768


def split3(value):
    hi = value.astype(jnp.bfloat16)
    left = value - hi.astype(jnp.float32)
    mid = left.astype(jnp.bfloat16)
    lo = (left - mid.astype(jnp.float32)).astype(jnp.bfloat16)
    return [hi, mid, lo]


def dot(a, b, dims=nn):
    return lax.dot_general(a, b, dims, preferred_element_type=jnp.float32)


def picked(parts, one_hot, dims=nn):
    size = parts[0].shape[0]
    out = dot(jnp.concatenate(parts, axis=0), one_hot, dims)
    return sum(out[i * size : (i + 1) * size] for i in range(len(parts)))


def mix(parts, factors, dims):
    size = parts[0].shape[0]
    total = None
    for i, factor in reversed(list(enumerate(factors))):
        count = min(len(parts), 3 - i)
        out = dot(jnp.concatenate(parts[:count], axis=0), factor, dims)
        for j in reversed(range(count)):
            term = out[j * size : (j + 1) * size]
            total = term if total is None else total + term
    return total


def encode(value, code_ref):
    rows = value.shape[0]
    top = jnp.maximum(jnp.max(jnp.abs(value), axis=0, keepdims=True), 1e-30)
    power = jnp.floor(256.0 * jnp.log2(top * (1.0 / 32767.0))) + 1.0
    code = jnp.floor(value * jnp.exp2(power * (-1.0 / 256.0)) + 0.5)
    code_ref[:rows, :] = code.astype(jnp.int32).astype(jnp.int16)
    power = jnp.broadcast_to(power, (16, value.shape[1]))
    code_ref[rows:, :] = power.astype(jnp.int32).astype(jnp.int16)


def decode(code_ref):
    rows = code_ref.shape[0] - 16
    power = code_ref[rows:, :].astype(jnp.int32).astype(jnp.float32)[0:1, :]
    unit = jnp.exp2(power * (1.0 / 256.0))
    return code_ref[:rows, :].astype(jnp.int32).astype(jnp.float32) * unit


def line_kernel(names, n_r, n_b, *refs):
    k = types.SimpleNamespace(**dict(zip(names, refs)))
    f32, bf16 = jnp.float32, jnp.bfloat16
    _, rows, seqs = k.x_hbm.shape
    half = seqs // 2
    wide = half // 2
    part = rows // n_r
    pairs = n_b // 2
    me_r = lax.axis_index("round")
    me_b = lax.axis_index("bucket")
    pair = me_b // 2
    core = me_b % 2
    sibling = pair * 2 + 1 - core
    inner = (pair > 0) & (pair < pairs - 1)
    total_count = n_r * n_b * rows * seqs

    def remote(src, dst, send, recv, **where):
        return pltpu.make_async_remote_copy(
            src_ref=src,
            dst_ref=dst,
            send_sem=send,
            recv_sem=recv,
            device_id=where,
            device_id_type=pl.DeviceIdType.MESH,
        )

    load_y = pltpu.make_async_copy(k.y_hbm, k.yv, k.load_sem.at[0])
    load_pay = pltpu.make_async_copy(k.pay_hbm, k.pay, k.load_sem.at[1])
    load_x = pltpu.make_async_copy(k.x_hbm, k.xv, k.load_sem.at[2])
    load_y.start()
    load_pay.start()
    load_x.start()

    barrier = pltpu.get_barrier_semaphore()
    for d in range(1, n_b):
        pl.semaphore_signal(
            barrier,
            inc=1,
            device_id={"bucket": (me_b + d) % n_b},
            device_id_type=pl.DeviceIdType.MESH,
        )
    for d in range(1, n_r):
        pl.semaphore_signal(
            barrier,
            inc=1,
            device_id={"round": (me_r + d) % n_r},
            device_id_type=pl.DeviceIdType.MESH,
        )

    def order(i):
        return 2 * (i // half * wide + i % wide) + (i % half) // wide

    down = lax.broadcasted_iota(jnp.int32, (seqs, seqs), 0)
    across = lax.broadcasted_iota(jnp.int32, (seqs, seqs), 1)
    k.to_outer[...] = (order(down) == across).astype(f32).astype(bf16)

    tiles, per_row, tile, _ = k.coef_ref.shape[1:]
    for m in range(tiles):
        for c in range(tiles):
            value = jnp.zeros((tile, tile), f32)
            for t in range(per_row):
                value = value + jnp.where(k.col_ref[0, m, t] == c, k.coef_ref[0, m, t], 0.0)
            k.mixer[m * tile : (m + 1) * tile, c * tile : (c + 1) * tile] = value
    for i, piece in enumerate(split3(k.mixer[...])):
        k.mix_p[i] = dot(k.to_outer[...], piece).astype(bf16)

    def rows_of(s):
        return pl.ds(pl.multiple_of(s * part, part), part)

    def columns(j):
        return pl.ds(pl.multiple_of(j * rows, rows), rows)


    def own_copy(kind, s):
        target = (sibling, me_b + 2, me_b - 2)[kind]
        here = k.blocks.at[me_b, :, rows_of(s), :]
        return remote(here, here, k.ag_send.at[kind, s], k.ag_recv.at[me_b, s], bucket=target)

    def own_start(s):
        @pl.when(pair < pairs - 1)
        def _():
            own_copy(1, s).start()

        @pl.when(pair > 0)
        def _():
            own_copy(2, s).start()

        own_copy(0, s).start()

    def own_drain(s):
        @pl.when(pair < pairs - 1)
        def _():
            own_copy(1, s).wait_send()

        @pl.when(pair > 0)
        def _():
            own_copy(2, s).wait_send()

        own_copy(0, s).wait_send()

    def set_own(s, value):
        value = value.astype(bf16)
        for h in range(2):
            k.blocks[me_b, h, rows_of(s), :] = value[:, h * half : (h + 1) * half]

    load_y.wait()
    for s in range(n_r):
        value = mix(split3(k.yv[0, rows_of(s), :]), [k.mix_p[i] for i in range(3)], nt)
        k.f_y[rows_of(s), :] = value
        set_own(s, value)
        if s == 0:
            pl.semaphore_wait(barrier, n_b + n_r - 2)
        own_start(s)

    def by_parts(b):
        for s in range(n_r):
            here = k.blocks.at[b, :, rows_of(s), :]
            remote(here, here, k.ag_send.at[0, s], k.ag_recv.at[b, s], bucket=sibling).wait_recv()

    def by_half(b, h):
        here = k.blocks.at[b, h]
        remote(here, here, k.ag_send.at[0, h], k.ag_recv.at[b, h], bucket=sibling).wait_recv()

    def go_on(b, h, step):
        here = k.blocks.at[b, h]
        return remote(
            here, here, k.line_send.at[b, h], k.ag_recv.at[b, h], bucket=me_b + step
        )

    def pass_on(b, h):
        here = k.blocks.at[b, h]
        return remote(here, here, k.pass_send.at[b, h], k.ag_recv.at[b, h], bucket=sibling)

    def product(b, h):
        return dot(k.pay[0, :, columns(b)], k.blocks[b, h])

    def setup():
        load_pay.wait()

        def turn(q, _):
            k.pay_out[q] = k.pay[0, :, columns(q * 2 + 1 - core)].T
            turned(q).start()
            k.pay_t[q, core] = k.pay[0, :, columns(q * 2 + core)].T
            return 0

        lax.fori_loop(0, pairs, turn, 0)
        for r in range(n_r - 1):
            place = order(lax.broadcasted_iota(jnp.int32, (seqs, half), 0))
            one_hot = (place == k.pred_ref[r : r + 1, :]).astype(f32).astype(bf16)
            k.gather[r] = one_hot
            k.spread[r] = one_hot.T
        load_x.wait()
        value = picked(split3(exact(k.xv[0], k.mixer[...])), k.to_outer[...], nt)
        k.f_x[...] = value
        for i in range(3):
            k.mix_p[i] = dot(k.mix_p[i], k.to_outer[...], nt).astype(bf16)

    def turned(q):
        return remote(
            k.pay_out.at[q],
            k.pay_t.at[q, core],
            k.turn_send.at[q],
            k.turn_recv.at[q],
            bucket=sibling,
        )


    def row_copy(d, h):
        s = (me_r + d) % n_r
        return remote(
            k.row_q.at[s, h],
            k.row_in.at[me_r, h],
            k.row_send.at[s, h],
            k.row_recv.at[me_r, h],
            round=s,
        )

    def row_arrival(d, h):
        s = (me_r + d) % n_r
        here = k.row_in.at[s, h]
        return remote(here, here, k.row_send.at[s, h], k.row_recv.at[s, h], round=s)

    def finish(h):
        for d in range(1, n_r):
            s = (me_r + d) % n_r
            encode(k.grad[h, rows_of(s), :], k.row_q.at[s, h])
            row_copy(d, h).start()
        squares = k.grad[h]
        squares = jnp.sum((squares * squares).reshape(rows // 8, 8, half), axis=0)
        squares = squares[:, :wide] + squares[:, wide:]
        if h == 0:
            k.sq_b[me_b] = squares
        else:
            k.sq_b[me_b] += squares
        k.rows_f[me_r, h] = k.grad[h, rows_of(me_r), :]

    def sqb_copy(d):
        s = (me_b + d) % n_b
        here = k.sq_b.at[me_b]
        return remote(here, here, k.sqb_send.at[d], k.sqb_recv.at[me_b], bucket=s)

    def sqb_arrival(d):
        s = (me_b + d) % n_b
        here = k.sq_b.at[s]
        return remote(here, here, k.sqb_send.at[d], k.sqb_recv.at[s], bucket=s)

    def sqr_copy(d):
        s = (me_r + d) % n_r
        here = k.sq_r.at[me_r]
        return remote(here, here, k.sqr_send.at[d], k.sqr_recv.at[me_r], round=s)

    def sqr_arrival(d):
        s = (me_r + d) % n_r
        here = k.sq_r.at[s]
        return remote(here, here, k.sqr_send.at[d], k.sqr_recv.at[s], round=s)

    def back_copy(r):
        return remote(
            k.back_q.at[r], k.back_in.at[me_r], k.back_send.at[r], k.back_recv.at[me_r], round=r
        )

    def back_arrival(s):
        here = k.back_in.at[s]
        return remote(here, here, k.back_send.at[s], k.back_recv.at[s], round=s)

    def prox(sign, factor):
        for d in range(1, n_b):
            sqb_copy(d).start()
        for d in range(1, n_r):
            row_arrival(d, 0).wait_recv()
            s = (me_r + d) % n_r
            k.rows_f[s, 0] = decode(k.row_in.at[s, 0])
        for d in range(1, n_b):
            sqb_arrival(d).wait_recv()
        k.sq_r[me_r] = jnp.sum(k.sq_b[...], axis=0)
        for d in range(1, n_r):
            sqr_copy(d).start()
        for d in range(1, n_r):
            row_arrival(d, 1).wait_recv()
            s = (me_r + d) % n_r
            k.rows_f[s, 1] = decode(k.row_in.at[s, 1])
        for d in range(1, n_r):
            sqr_arrival(d).wait_recv()
        squares = jnp.sum(jnp.sum(k.sq_r[...], axis=0), axis=0, keepdims=True)
        squares = jnp.sum(squares, axis=1, keepdims=True)
        scale = sign / (factor * jnp.sqrt(squares / total_count + epsilon))

        carried = None
        shares = [None] * n_r
        for r in reversed(range(n_r)):
            norms = []
            shares[r] = []
            for h in range(2):
                values = k.rows_f[r, h] * scale
                if carried is not None:
                    values = values + carried[:, h * half : (h + 1) * half]
                even, odd = values[:, :wide], values[:, wide:]
                small = jnp.exp(-jnp.abs(even - odd))
                larger = 1.0 / (1.0 + small)
                smaller = small * larger
                ahead = even >= odd
                k.share[r, h, :, :wide] = jnp.where(ahead, larger, smaller)
                k.share[r, h, :, wide:] = jnp.where(ahead, smaller, larger)
                norms.append(jnp.maximum(even, odd) + jnp.log(1.0 + small))
            if r > 0:
                norm = jnp.concatenate(norms, axis=1)
                carried = picked(split3(norm), k.spread[r - 1])

        mass = None
        for r in range(n_r):
            halves = []
            if r > 0:
                parent = picked(split3(mass), k.gather[r - 1])
            for h in range(2):
                now = k.share[r, h]
                if r > 0:
                    above = parent[:, h * wide : (h + 1) * wide]
                    now = now * jnp.concatenate([above, above], axis=1)
                halves.append(now)
            mass = jnp.concatenate(halves, axis=1)
            code = jnp.floor(mass * top_code + 0.5).astype(jnp.int32) - shift_code
            k.back_q[r] = code.astype(jnp.int16)

            @pl.when(me_r != r)
            def _():
                back_copy(r).start()

            @pl.when(me_r == r)
            def _():
                k.back_in[me_r] = k.back_q[r]

    def prox_drain():
        for d in range(1, n_r):
            for h in range(2):
                row_copy(d, h).wait_send()
            back_copy((me_r + d) % n_r).wait_send()
            sqr_copy(d).wait_send()
        for d in range(1, n_b):
            sqb_copy(d).wait_send()

    def pieces(s):
        whole = (k.back_in[s].astype(jnp.int32) + shift_code).astype(f32)
        hi = whole.astype(bf16)
        return [hi, (whole - hi.astype(f32)).astype(bf16)]

    def mixed_part(s, state, weight, dims):
        value = mix(pieces(s), [k.mix_p[i] for i in range(3)], dims)
        value = (1.0 - weight) * state[rows_of(s), :] + (weight * (1.0 / top_code)) * value
        state[rows_of(s), :] = value
        return value

    def add_best(out, s, share):
        best = picked(pieces(s), k.to_outer[...])
        out[0, rows_of(s), :] += (share * (1.0 / top_code)) * best


    def mixed_copy(s):
        here = k.mixed.at[core, :, rows_of(s), :]
        return remote(here, here, k.mx_send.at[s], k.mx_recv.at[core, s], bucket=sibling)

    def mixed_arrival(s):
        here = k.mixed.at[1 - core, :, rows_of(s), :]
        return remote(here, here, k.mx_send.at[s], k.mx_recv.at[1 - core, s], bucket=sibling)

    def partial(q, h):
        return dot(k.pay_t[q, 0], k.mixed[0, h]) + dot(k.pay_t[q, 1], k.mixed[1, h])

    def sum_copy(way, q, h):
        return remote(
            k.sum_out.at[way, q, h],
            k.sum_in.at[way, q, h],
            k.sum_send.at[way, q, h],
            k.sum_recv.at[way, q, h],
            bucket=jnp.where(way == 0, me_b + 2, me_b - 2),
        )

    def sum_arrival(way, q, h):
        here = k.sum_in.at[way, q, h]
        return remote(
            here, here, k.sum_send.at[way, q, h], k.sum_recv.at[way, q, h], bucket=sibling
        )

    def sum_unit(i):
        j = i // 2
        up = (i % 2 == 0) == (pair < pairs // 2)
        way = jnp.where(up, 0, 1)
        q = jnp.where(up, pairs - 1 - j // 2, j // 2)
        valid = jnp.where(up, q > pair, q < pair)
        fed = jnp.where(up, pair > 0, pair < pairs - 1)
        return way, q, j % 2, valid, fed

    def step(index, _):
        weight = 2.0 / (index.astype(f32) + 3.0)

        @pl.when(index == 0)
        def _():
            setup()

        for h in range(2):
            k.grad[h] = product(me_b, h)
        by_parts(sibling)
        for h in range(2):
            k.grad[h] += product(sibling, h)

        @pl.when(index == 0)
        def _():
            for q in range(pairs):
                turned(q).wait()
            k.xo_ref[...] = (1.0 - weights[0]) * (1.0 - weights[1]) * k.xv[...]
            k.yo_ref[...] = (1.0 - weights[0]) * (1.0 - weights[1]) * k.yv[...]

        def toward(place):
            near = jnp.where(pair % 2 == 0, 2, -2)
            side = jnp.where(pair < pairs // 2, 1, -1)
            second = side * jnp.where(inner, 2, 4)
            far = side * jnp.where(inner, 4, 6)
            return (near, second, far)[place]

        def take(place):
            offset = toward(place)
            b, other = me_b + offset, sibling + offset
            onward = jnp.where(offset < 0, 2, -2)

            def send_on(h):
                @pl.when(inner)
                def _():
                    go_on(b, h, onward).start()

                pass_on(b, h).start()

            if place == 0:
                by_parts(b)
            elif place == 1:

                @pl.when(inner)
                def _():
                    by_parts(b)

            for h in range(2):
                if place == 1:

                    @pl.when(jnp.logical_not(inner))
                    def _():
                        by_half(b, h)

                elif place == 2:
                    by_half(b, h)
                send_on(h)
                if place == 2:
                    k.grad[h] += product(b, h)
                    by_half(other, h)
                    k.grad[h] += product(other, h)
                    finish(h)
            if place < 2:
                for h in range(2):
                    k.grad[h] += product(b, h)
                    by_half(other, h)
                    k.grad[h] += product(other, h)

        def take_drain(place):
            offset = toward(place)
            for h in range(2):

                @pl.when(inner)
                def _():
                    go_on(me_b + offset, h, jnp.where(offset < 0, 2, -2)).wait_send()

                pass_on(me_b + offset, h).wait_send()

        take(0)

        @pl.when(index == 1)
        def _():
            for s in range(n_r):
                add_best(k.yo_ref, s, weights[0] * (1.0 - weights[1]))

        take(1)
        take(2)
        for place in range(3):
            take_drain(place)
        for s in range(n_r):
            own_drain(s)

        prox(-1.0, smooth_x)
        for d in range(n_r):
            s = (me_r + d) % n_r
            if d > 0:
                back_arrival(s).wait_recv()
            value = mixed_part(s, k.f_x, weight, nn).astype(bf16)
            for h in range(2):
                k.mixed[core, h, rows_of(s), :] = value[:, h * half : (h + 1) * half]
            mixed_copy(s).start()
        for d in range(n_r):
            mixed_arrival((me_r + d) % n_r).wait_recv()

        def move(i, _):
            way, q, h, valid, fed = sum_unit(i)

            @pl.when(valid)
            def _():
                k.work[...] = partial(q, h)

                @pl.when(fed)
                def _():
                    sum_arrival(way, q, h).wait_recv()
                    k.work[...] += decode(k.sum_in.at[way, q, h])

                encode(k.work[...], k.sum_out.at[way, q, h])
                sum_copy(way, q, h).start()

            return 0

        lax.fori_loop(0, 4 * (pairs - 1), move, 0)
        prox_drain()
        for s in range(n_r):
            mixed_copy(s).wait_send()
        share = jnp.where(index == 0, weights[0] * (1.0 - weights[1]), weights[1])
        for s in range(n_r):
            add_best(k.xo_ref, s, share)
        for h in range(2):
            k.grad[h] = partial(pair, h)

            @pl.when(pair > 0)
            def _():
                sum_arrival(0, pair, h).wait_recv()
                k.grad[h] += decode(k.sum_in.at[0, pair, h])

            @pl.when(pair < pairs - 1)
            def _():
                sum_arrival(1, pair, h).wait_recv()
                k.grad[h] += decode(k.sum_in.at[1, pair, h])

            finish(h)

        def settle(i, _):
            way, q, h, valid, fed = sum_unit(i)

            @pl.when(valid)
            def _():
                sum_copy(way, q, h).wait_send()

            return 0

        lax.fori_loop(0, 4 * (pairs - 1), settle, 0)

        prox(1.0, smooth_y)
        for d in range(n_r):
            s = (me_r + d) % n_r
            if d > 0:
                back_arrival(s).wait_recv()

            @pl.when(index == 0)
            def _():
                set_own(s, mixed_part(s, k.f_y, weight, nt))
                own_start(s)

            @pl.when(index == 1)
            def _():
                add_best(k.yo_ref, s, weights[1])

        prox_drain()
        return 0

    lax.fori_loop(0, 2, step, 0)


def line_body(x_start, y_start, bucket_payoff, column_blocks, public_coef, predecessor_sequences):
    n_r = lax.axis_size("round")
    n_b = lax.axis_size("bucket")
    _, rows, seqs = x_start.shape
    half = seqs // 2
    part = rows // n_r
    pairs = n_b // 2
    f32, bf16, i16 = jnp.float32, jnp.bfloat16, jnp.int16
    vmem = pl.BlockSpec(memory_space=pltpu.VMEM)
    smem = pl.BlockSpec(memory_space=pltpu.SMEM)
    hbm = pl.BlockSpec(memory_space=pl.ANY)
    dma = pltpu.SemaphoreType.DMA
    scratch = dict(
        xv=pltpu.VMEM((1, rows, seqs), f32),
        yv=pltpu.VMEM((1, rows, seqs), f32),
        pay=pltpu.VMEM((1, rows, n_b * rows), bf16),
        pay_t=pltpu.VMEM((pairs, 2, rows, rows), bf16),
        pay_out=pltpu.VMEM((pairs, rows, rows), bf16),
        blocks=pltpu.VMEM((n_b, 2, rows, half), bf16),
        mixed=pltpu.VMEM((2, 2, rows, half), bf16),
        mixer=pltpu.VMEM((seqs, seqs), f32),
        mix_p=pltpu.VMEM((3, seqs, seqs), bf16),
        to_outer=pltpu.VMEM((seqs, seqs), bf16),
        gather=pltpu.VMEM((n_r - 1, seqs, half), bf16),
        spread=pltpu.VMEM((n_r - 1, half, seqs), bf16),
        f_x=pltpu.VMEM((rows, seqs), f32),
        f_y=pltpu.VMEM((rows, seqs), f32),
        grad=pltpu.VMEM((2, rows, half), f32),
        work=pltpu.VMEM((rows, half), f32),
        sum_out=pltpu.VMEM((2, pairs, 2, rows + 16, half), i16),
        sum_in=pltpu.VMEM((2, pairs, 2, rows + 16, half), i16),
        row_q=pltpu.VMEM((n_r, 2, part + 16, half), i16),
        row_in=pltpu.VMEM((n_r, 2, part + 16, half), i16),
        rows_f=pltpu.VMEM((n_r, 2, part, half), f32),
        share=pltpu.VMEM((n_r, 2, part, half), f32),
        back_q=pltpu.VMEM((n_r, part, seqs), i16),
        back_in=pltpu.VMEM((n_r, part, seqs), i16),
        sq_b=pltpu.VMEM((n_b, 8, 128), f32),
        sq_r=pltpu.VMEM((n_r, 8, 128), f32),
        load_sem=dma((3,)),
        turn_send=dma((pairs,)),
        turn_recv=dma((pairs,)),
        ag_send=dma((3, n_r)),
        ag_recv=dma((n_b, n_r)),
        line_send=dma((n_b, 2)),
        pass_send=dma((n_b, 2)),
        mx_send=dma((n_r,)),
        mx_recv=dma((2, n_r)),
        sum_send=dma((2, pairs, 2)),
        sum_recv=dma((2, pairs, 2)),
        row_send=dma((n_r, 2)),
        row_recv=dma((n_r, 2)),
        back_send=dma((n_r,)),
        back_recv=dma((n_r,)),
        sqb_send=dma((n_b,)),
        sqb_recv=dma((n_b,)),
        sqr_send=dma((n_r,)),
        sqr_recv=dma((n_r,)),
    )
    names = ["x_hbm", "y_hbm", "pay_hbm", "col_ref", "coef_ref", "pred_ref", "xo_ref", "yo_ref"]
    names += list(scratch)
    return pl.pallas_call(
        functools.partial(line_kernel, names, n_r, n_b),
        out_shape=[jax.ShapeDtypeStruct(x_start.shape, f32)] * 2,
        in_specs=[hbm, hbm, hbm, smem, vmem, vmem],
        out_specs=[vmem, vmem],
        scratch_shapes=list(scratch.values()),
        compiler_params=pltpu.CompilerParams(
            collective_id=0, has_side_effects=True, vmem_limit_bytes=60 * 1024 * 1024
        ),
    )(x_start, y_start, bucket_payoff, column_blocks, public_coef, predecessor_sequences)


def plain_kernel(
    n_r,
    n_b,
    x_ref,
    y_ref,
    pay_ref,
    col_ref,
    coef_ref,
    pred_ref,
    xo_ref,
    yo_ref,
    xs,
    ys,
    mixer,
    gather,
    pay_t,
    blocks,
    mixed,
    grad,
    sib_out,
    sib_in,
    far_out,
    far_in,
    sq_b,
    sq_r,
    rows_in,
    score,
    norm,
    mass,
    back_in,
    far_q,
    far_s,
    far_q_in,
    far_s_in,
    row_q,
    row_s,
    row_q_in,
    row_s_in,
    back_q,
    back_s,
    back_q_in,
    back_s_in,
    ag_send,
    ag_recv,
    fw_send,
    line_send,
    sib_send,
    sib_recv,
    far_send,
    far_recv,
    sqb_send,
    sqb_recv,
    sqr_send,
    sqr_recv,
    row_send,
    row_recv,
    back_send,
    back_recv,
    far_s_send,
    far_s_recv,
    row_s_send,
    row_s_recv,
    back_s_send,
    back_s_recv,
):
    rows, seqs = xs.shape
    half = seqs // 2
    part = rows // n_r
    pairs = n_b // 2
    me_r = lax.axis_index("round")
    me_b = lax.axis_index("bucket")
    pair = me_b // 2
    core = me_b % 2
    sibling = pair * 2 + 1 - core
    total_count = n_r * n_b * rows * seqs

    def remote(src, dst, send, recv, **where):
        return pltpu.make_async_remote_copy(
            src_ref=src,
            dst_ref=dst,
            send_sem=send,
            recv_sem=recv,
            device_id=where,
            device_id_type=pl.DeviceIdType.MESH,
        )

    barrier = pltpu.get_barrier_semaphore()
    for d in range(1, n_b):
        pl.semaphore_signal(
            barrier,
            inc=1,
            device_id={"bucket": (me_b + d) % n_b},
            device_id_type=pl.DeviceIdType.MESH,
        )
    for d in range(1, n_r):
        pl.semaphore_signal(
            barrier,
            inc=1,
            device_id={"round": (me_r + d) % n_r},
            device_id_type=pl.DeviceIdType.MESH,
        )
    pl.semaphore_wait(barrier, n_b + n_r - 2)

    def order(i):
        return jnp.where(i < half, 2 * i, 2 * (i - half) + 1)

    down = lax.broadcasted_iota(jnp.int32, (seqs, seqs), 0)
    across = lax.broadcasted_iota(jnp.int32, (seqs, seqs), 1)
    to_inner = (down == order(across)).astype(jnp.float32)
    to_outer = (order(down) == across).astype(jnp.float32)

    tiles, per_row, tile, _ = coef_ref.shape[1:]
    for m in range(tiles):
        for c in range(tiles):
            value = jnp.zeros((tile, tile), jnp.float32)
            for t in range(per_row):
                value = value + jnp.where(col_ref[0, m, t] == c, coef_ref[0, m, t], 0.0)
            mixer[m * tile : (m + 1) * tile, c * tile : (c + 1) * tile] = value
    mixer[...] = exact(to_outer, exact(mixer[...], to_inner))
    ys[...] = exact(y_ref[0], to_inner)
    for r in range(n_r - 1):
        place = order(lax.broadcasted_iota(jnp.int32, (seqs, half), 0))
        gather[r] = (place == pred_ref[r : r + 1, :]).astype(jnp.float32)

    def columns(j):
        return pl.ds(pl.multiple_of(j * rows, rows), rows)

    def coded(value, code_ref, scale_ref):
        top = jnp.max(jnp.abs(value), axis=0, keepdims=True)
        unit = jnp.maximum(top, 1e-30) / 32767.0
        code = jnp.floor(value * (1.0 / unit) + 0.5)
        code_ref[...] = code.astype(jnp.int32).astype(jnp.int16)
        scale_ref[...] = jnp.broadcast_to(unit, scale_ref.shape)

    def decoded(code_ref, scale_ref):
        return code_ref[...].astype(jnp.int32).astype(jnp.float32) * scale_ref[0:1, :]

    def prox(state, sign, factor, weight, short):
        def row_copy(d):
            s = (me_r + d) % n_r
            here = grad.at[pl.ds(pl.multiple_of(s * part, part), part)]
            if not short:
                return [
                    remote(here, rows_in.at[me_r], row_send.at[s], row_recv.at[me_r], round=s)
                ]
            return [
                remote(
                    row_q.at[s], row_q_in.at[me_r], row_send.at[s], row_recv.at[me_r], round=s
                ),
                remote(
                    row_s.at[s], row_s_in.at[me_r], row_s_send.at[s], row_s_recv.at[me_r], round=s
                ),
            ]

        def row_arrival(d):
            s = (me_r + d) % n_r
            if not short:
                return [
                    remote(rows_in.at[s], rows_in.at[s], row_send.at[s], row_recv.at[s], round=s)
                ]
            return [
                remote(row_q_in.at[s], row_q_in.at[s], row_send.at[s], row_recv.at[s], round=s),
                remote(
                    row_s_in.at[s], row_s_in.at[s], row_s_send.at[s], row_s_recv.at[s], round=s
                ),
            ]

        for d in range(1, n_r):
            if short:
                s = (me_r + d) % n_r
                here = pl.ds(pl.multiple_of(s * part, part), part)
                coded(grad[here, :], row_q.at[s], row_s.at[s])
            for copy in row_copy(d):
                copy.start()
        squares = grad[...]
        squares = jnp.sum((squares * squares).reshape(rows // 8, 8, seqs), axis=0)
        squares = sum(squares[:, i * 128 : (i + 1) * 128] for i in range(seqs // 128))
        sq_b[me_b] = squares

        def sqb_copy(d):
            s = (me_b + d) % n_b
            return remote(
                sq_b.at[me_b], sq_b.at[me_b], sqb_send.at[d], sqb_recv.at[me_b], bucket=s
            )

        def sqb_arrival(d):
            s = (me_b + d) % n_b
            return remote(sq_b.at[s], sq_b.at[s], sqb_send.at[d], sqb_recv.at[s], bucket=s)

        for d in range(1, n_b):
            sqb_copy(d).start()
        rows_in[me_r] = grad[pl.ds(pl.multiple_of(me_r * part, part), part), :]
        for d in range(1, n_b):
            sqb_arrival(d).wait_recv()
        sq_r[me_r] = jnp.sum(sq_b[...], axis=0)

        def sqr_copy(d):
            s = (me_r + d) % n_r
            return remote(sq_r.at[me_r], sq_r.at[me_r], sqr_send.at[d], sqr_recv.at[me_r], round=s)

        def sqr_arrival(d):
            s = (me_r + d) % n_r
            return remote(sq_r.at[s], sq_r.at[s], sqr_send.at[d], sqr_recv.at[s], round=s)

        for d in range(1, n_r):
            sqr_copy(d).start()
        for d in range(1, n_r):
            sqr_arrival(d).wait_recv()
        squares = jnp.sum(jnp.sum(sq_r[...], axis=0), axis=0, keepdims=True)
        squares = jnp.sum(squares, axis=1, keepdims=True)
        scale = sign / (factor * jnp.sqrt(squares / total_count + epsilon))
        for d in range(1, n_r):
            for copy in row_arrival(d):
                copy.wait_recv()
            if short:
                s = (me_r + d) % n_r
                rows_in[s] = decoded(row_q_in.at[s], row_s_in.at[s])

        for r in reversed(range(n_r)):
            values = rows_in[r] * scale
            if r < n_r - 1:
                values = values + exact(norm[r + 1], gather[r], nt)
            score[r] = values
            even, odd = values[:, :half], values[:, half:]
            larger = jnp.maximum(even, odd)
            norm[r] = larger + jnp.log(jnp.exp(even - larger) + jnp.exp(odd - larger))

        def back_copy(r):
            if not short:
                return [
                    remote(
                        mass.at[r], back_in.at[me_r], back_send.at[r], back_recv.at[me_r], round=r
                    )
                ]
            return [
                remote(
                    back_q.at[r], back_q_in.at[me_r], back_send.at[r], back_recv.at[me_r], round=r
                ),
                remote(
                    back_s.at[r],
                    back_s_in.at[me_r],
                    back_s_send.at[r],
                    back_s_recv.at[me_r],
                    round=r,
                ),
            ]

        def back_arrival(s):
            if not short:
                return [
                    remote(
                        back_in.at[s], back_in.at[s], back_send.at[s], back_recv.at[s], round=s
                    )
                ]
            return [
                remote(
                    back_q_in.at[s], back_q_in.at[s], back_send.at[s], back_recv.at[s], round=s
                ),
                remote(
                    back_s_in.at[s], back_s_in.at[s], back_s_send.at[s], back_s_recv.at[s], round=s
                ),
            ]

        for r in range(n_r):
            even = jnp.exp(score[r, :, :half] - norm[r])
            odd = jnp.exp(score[r, :, half:] - norm[r])
            if r > 0:
                parent = exact(mass[r - 1], gather[r - 1])
                even = parent * even
                odd = parent * odd
            mass[r, :, :half] = even
            mass[r, :, half:] = odd

            @pl.when(me_r != r)
            def _():
                if short:
                    coded(mass[r], back_q.at[r], back_s.at[r])
                for copy in back_copy(r):
                    copy.start()

        def update(s, best):
            here = pl.ds(pl.multiple_of(s * part, part), part)
            state[here, :] = (1.0 - weight) * state[here, :] + weight * best

        update(me_r, mass[me_r])
        for d in range(1, n_r):
            s = (me_r + d) % n_r
            for copy in back_arrival(s):
                copy.wait_recv()
            if short:
                update(s, decoded(back_q_in.at[s], back_s_in.at[s]))
            else:
                update(s, back_in[s])
        for d in range(1, n_r):
            for copy in row_copy(d) + back_copy((me_r + d) % n_r):
                copy.wait_send()
            sqr_copy(d).wait_send()
        for d in range(1, n_b):
            sqb_copy(d).wait_send()

    def step(index, _):
        weight = 2.0 / (index.astype(jnp.float32) + 3.0)
        short = False

        blocks[me_b] = exact(ys[...], mixer[...], nt).astype(jnp.bfloat16)

        def own_copy(kind):
            target = (sibling, me_b + 2, me_b - 2)[kind]
            return remote(
                blocks.at[me_b], blocks.at[me_b], ag_send.at[kind], ag_recv.at[me_b], bucket=target
            )

        def go_on(b, d, step):
            return remote(
                blocks.at[b], blocks.at[b], line_send.at[d], ag_recv.at[b], bucket=me_b + step
            )

        def pass_on(b, d):
            return remote(blocks.at[b], blocks.at[b], fw_send.at[d], ag_recv.at[b], bucket=sibling)

        def arrival(b):
            return remote(
                blocks.at[b], blocks.at[b], ag_send.at[0], ag_recv.at[b], bucket=sibling
            )

        def product(b):
            return jnp.dot(
                pay_ref[0, :, columns(b)], blocks[b], preferred_element_type=jnp.float32
            )

        @pl.when(pair < pairs - 1)
        def _():
            own_copy(1).start()

        @pl.when(pair > 0)
        def _():
            own_copy(2).start()

        own_copy(0).start()
        @pl.when(index == 0)
        def _():
            xs[...] = exact(x_ref[0], to_inner)

            def turn(j, _):
                pay_t[columns(j), :] = pay_ref[0, :, columns(j)].T
                return 0

            lax.fori_loop(0, n_b, turn, 0)
        grad[...] = product(me_b)
        arrival(sibling).wait_recv()
        grad[...] += product(sibling)

        def take(d, _):
            left = me_b - 2 * d
            right = me_b + 2 * d

            @pl.when(pair >= d)
            def _():
                arrival(left).wait_recv()

                @pl.when(pair < pairs - 1)
                def _():
                    go_on(left, d, 2).start()

                pass_on(left, d).start()

            @pl.when(pair + d < pairs)
            def _():
                arrival(right).wait_recv()

                @pl.when(pair > 0)
                def _():
                    go_on(right, pairs + d, -2).start()

                pass_on(right, pairs + d).start()

            def use(b, other):
                grad[...] += product(b)
                arrival(other).wait_recv()
                grad[...] += product(other)

            @pl.when(pair >= d)
            def _():
                use(left, sibling - 2 * d)

            @pl.when(pair + d < pairs)
            def _():
                use(right, sibling + 2 * d)

            return 0

        lax.fori_loop(1, pairs, take, 0)

        def drain(d, _):
            left = me_b - 2 * d
            right = me_b + 2 * d

            @pl.when(pair >= d)
            def _():
                pass_on(left, d).wait_send()

                @pl.when(pair < pairs - 1)
                def _():
                    go_on(left, d, 2).wait_send()

            @pl.when(pair + d < pairs)
            def _():
                pass_on(right, pairs + d).wait_send()

                @pl.when(pair > 0)
                def _():
                    go_on(right, pairs + d, -2).wait_send()

            return 0

        lax.fori_loop(1, pairs, drain, 0)
        own_copy(0).wait_send()

        @pl.when(pair < pairs - 1)
        def _():
            own_copy(1).wait_send()

        @pl.when(pair > 0)
        def _():
            own_copy(2).wait_send()

        prox(xs, -1.0, smooth_x, weight, short)

        mixed[...] = exact(xs[...], mixer[...]).astype(jnp.bfloat16)

        def partial(b):
            return jnp.dot(pay_t[columns(b), :], mixed[...], preferred_element_type=jnp.float32)

        def sib_copy(q):
            return remote(
                sib_out.at[q], sib_in.at[q], sib_send.at[q], sib_recv.at[q], bucket=sibling
            )

        def far_copy(q, step, target):
            slot = q if step > 0 else pairs + q
            if not short:
                return [
                    remote(
                        far_out.at[q],
                        far_in.at[slot],
                        far_send.at[q],
                        far_recv.at[slot],
                        bucket=target,
                    )
                ]
            return [
                remote(
                    far_q.at[q],
                    far_q_in.at[slot],
                    far_send.at[q],
                    far_recv.at[slot],
                    bucket=target,
                ),
                remote(
                    far_s.at[q],
                    far_s_in.at[slot],
                    far_s_send.at[q],
                    far_s_recv.at[slot],
                    bucket=target,
                ),
            ]

        def far_value(q, step):
            slot = q if step > 0 else pairs + q
            for copy in far_copy(q, step, sibling):
                copy.wait_recv()
            if short:
                return decoded(far_q_in.at[slot], far_s_in.at[slot])
            return far_in[slot]

        def to_sibling(q):
            sib_out[q] = partial(q * 2 + 1 - core)
            sib_copy(q).start()

        def move(q, step):
            far_out[q] = partial(q * 2 + core)
            sib_copy(q).wait_recv()
            far_out[q] += sib_in[q]

            @pl.when(pair > 0 if step > 0 else pair < pairs - 1)
            def _():
                far_out[q] += far_value(q, step)

            if short:
                coded(far_out[q], far_q.at[q], far_s.at[q])
            for copy in far_copy(q, step, me_b + step):
                copy.start()

        def outward(right, left):
            def one(i, _):
                @pl.when(pair < pairs - 1 - i)
                def _():
                    right(pairs - 1 - i)

                @pl.when(pair > i)
                def _():
                    left(i)

                return 0

            lax.fori_loop(0, pairs - 1, one, 0)

        def far_done(q, step):
            for copy in far_copy(q, step, me_b + step):
                copy.wait_send()

        outward(to_sibling, to_sibling)
        outward(lambda q: move(q, 2), lambda q: move(q, -2))
        to_sibling(pair)
        grad[...] = partial(me_b)
        sib_copy(pair).wait_recv()
        grad[...] += sib_in[pair]

        @pl.when(pair > 0)
        def _():
            grad[...] += far_value(pair, 2)

        @pl.when(pair < pairs - 1)
        def _():
            grad[...] += far_value(pair, -2)

        outward(lambda q: far_done(q, 2), lambda q: far_done(q, -2))
        for q in range(pairs):
            sib_copy(q).wait_send()
        prox(ys, 1.0, smooth_y, weight, short)
        return 0

    lax.fori_loop(0, 2, step, 0)
    down = lax.broadcasted_iota(jnp.int32, (seqs, seqs), 0)
    across = lax.broadcasted_iota(jnp.int32, (seqs, seqs), 1)
    to_outer = (order(down) == across).astype(jnp.float32)
    xo_ref[0] = exact(xs[...], to_outer)
    yo_ref[0] = exact(ys[...], to_outer)


def plain_body(x_start, y_start, bucket_payoff, column_blocks, public_coef, predecessor_sequences):
    n_r = lax.axis_size("round")
    n_b = lax.axis_size("bucket")
    _, rows, seqs = x_start.shape
    part = rows // n_r
    pairs = n_b // 2
    f32, bf16 = jnp.float32, jnp.bfloat16
    vmem = pl.BlockSpec(memory_space=pltpu.VMEM)
    smem = pl.BlockSpec(memory_space=pltpu.SMEM)
    dma = pltpu.SemaphoreType.DMA
    return pl.pallas_call(
        functools.partial(plain_kernel, n_r, n_b),
        out_shape=[jax.ShapeDtypeStruct(x_start.shape, f32)] * 2,
        in_specs=[vmem, vmem, vmem, smem, vmem, vmem],
        out_specs=[vmem, vmem],
        scratch_shapes=[
            pltpu.VMEM((rows, seqs), f32),
            pltpu.VMEM((rows, seqs), f32),
            pltpu.VMEM((seqs, seqs), f32),
            pltpu.VMEM((n_r - 1, seqs, seqs // 2), f32),
            pltpu.VMEM((n_b * rows, rows), bf16),
            pltpu.VMEM((n_b, rows, seqs), bf16),
            pltpu.VMEM((rows, seqs), bf16),
            pltpu.VMEM((rows, seqs), f32),
            pltpu.VMEM((pairs, rows, seqs), f32),
            pltpu.VMEM((pairs, rows, seqs), f32),
            pltpu.VMEM((pairs, rows, seqs), f32),
            pltpu.VMEM((2 * pairs, rows, seqs), f32),
            pltpu.VMEM((n_b, 8, 128), f32),
            pltpu.VMEM((n_r, 8, 128), f32),
            pltpu.VMEM((n_r, part, seqs), f32),
            pltpu.VMEM((n_r, part, seqs), f32),
            pltpu.VMEM((n_r, part, seqs // 2), f32),
            pltpu.VMEM((n_r, part, seqs), f32),
            pltpu.VMEM((n_r, part, seqs), f32),
            pltpu.VMEM((16, 128), jnp.int16),
            pltpu.VMEM((pairs, 8, seqs), f32),
            pltpu.VMEM((16, 128), jnp.int16),
            pltpu.VMEM((2 * pairs, 8, seqs), f32),
            pltpu.VMEM((16, 128), jnp.int16),
            pltpu.VMEM((n_r, 8, seqs), f32),
            pltpu.VMEM((16, 128), jnp.int16),
            pltpu.VMEM((n_r, 8, seqs), f32),
            pltpu.VMEM((16, 128), jnp.int16),
            pltpu.VMEM((n_r, 8, seqs), f32),
            pltpu.VMEM((16, 128), jnp.int16),
            pltpu.VMEM((n_r, 8, seqs), f32),
            dma((3,)),
            dma((n_b,)),
            dma((2 * pairs,)),
            dma((2 * pairs,)),
            dma((pairs,)),
            dma((pairs,)),
            dma((pairs,)),
            dma((2 * pairs,)),
            dma((n_b,)),
            dma((n_b,)),
            dma((n_r,)),
            dma((n_r,)),
            dma((n_r,)),
            dma((n_r,)),
            dma((n_r,)),
            dma((n_r,)),
            dma((pairs,)),
            dma((2 * pairs,)),
            dma((n_r,)),
            dma((n_r,)),
            dma((n_r,)),
            dma((n_r,)),
        ],
        compiler_params=pltpu.CompilerParams(
            collective_id=0, has_side_effects=True, vmem_limit_bytes=60 * 1024 * 1024
        ),
    )(x_start, y_start, bucket_payoff, column_blocks, public_coef, predecessor_sequences)


def solution(mesh):
    in_specs = (
        P("round", "bucket", None),
        P("round", "bucket", None),
        P("round", "bucket", None),
        P("round", None, None),
        P("round", None, None, None, None),
        P(),
    )
    out_specs = (P("round", "bucket", None), P("round", "bucket", None))

    line = mesh.shape["round"] == 4 and mesh.shape["bucket"] == 8

    def run(*arrays):
        return tuple(
            jax.shard_map(
                line_body if line else plain_body, mesh=mesh, in_specs=in_specs, out_specs=out_specs, check_vma=False
            )(*arrays)
        )

    return run
```

```python
import functools
import types

import jax
import jax.numpy as jnp
from jax import lax
from jax.experimental import pallas as pl
from jax.experimental.pallas import tpu as pltpu
from jax.sharding import PartitionSpec as P

smooth_x = 0.1
smooth_y = 0.1
epsilon = 1e-06
highest = lax.Precision.HIGHEST
nn = (((1,), (0,)), ((), ()))
nt = (((1,), (1,)), ((), ()))


def exact(a, b, dims=nn):
    return lax.dot_general(a, b, dims, precision=highest, preferred_element_type=jnp.float32)


weights = (2.0 / 3.0, 2.0 / 4.0)
top_code = 65535.0
shift_code = 32768


def split3(value):
    hi = value.astype(jnp.bfloat16)
    left = value - hi.astype(jnp.float32)
    mid = left.astype(jnp.bfloat16)
    lo = (left - mid.astype(jnp.float32)).astype(jnp.bfloat16)
    return [hi, mid, lo]


def dot(a, b, dims=nn):
    return lax.dot_general(a, b, dims, preferred_element_type=jnp.float32)


def picked(parts, one_hot, dims=nn):
    size = parts[0].shape[0]
    out = dot(jnp.concatenate(parts, axis=0), one_hot, dims)
    return sum(out[i * size : (i + 1) * size] for i in range(len(parts)))


def mix(parts, factors, dims):
    size = parts[0].shape[0]
    total = None
    for i, factor in reversed(list(enumerate(factors))):
        count = min(len(parts), 3 - i)
        out = dot(jnp.concatenate(parts[:count], axis=0), factor, dims)
        for j in reversed(range(count)):
            term = out[j * size : (j + 1) * size]
            total = term if total is None else total + term
    return total


def encode(value, code_ref):
    if len(code_ref.shape) == 3:
        wide = code_ref.shape[2]
        for i in range(code_ref.shape[0]):
            encode(value[:, i * wide : (i + 1) * wide], code_ref.at[i])
        return
    rows = value.shape[0]
    top = jnp.maximum(jnp.max(jnp.abs(value), axis=0, keepdims=True), 1e-30)
    power = jnp.floor(256.0 * jnp.log2(top * (1.0 / 32767.0))) + 1.0
    code = jnp.floor(value * jnp.exp2(power * (-1.0 / 256.0)) + 0.5)
    code_ref[:rows, :] = code.astype(jnp.int32).astype(jnp.int16)
    power = jnp.broadcast_to(power, (16, value.shape[1]))
    code_ref[rows:, :] = power.astype(jnp.int32).astype(jnp.int16)


def decode(code_ref):
    if len(code_ref.shape) == 3:
        return jnp.concatenate([decode(code_ref.at[i]) for i in range(code_ref.shape[0])], axis=1)
    rows = code_ref.shape[0] - 16
    power = code_ref[rows:, :].astype(jnp.int32).astype(jnp.float32)[0:1, :]
    unit = jnp.exp2(power * (1.0 / 256.0))
    return code_ref[:rows, :].astype(jnp.int32).astype(jnp.float32) * unit


def line_kernel(names, n_r, n_b, *refs):
    k = types.SimpleNamespace(**dict(zip(names, refs)))
    f32, bf16 = jnp.float32, jnp.bfloat16
    _, rows, seqs = k.x_hbm.shape
    half = seqs // 2
    wide = half // 2
    part = rows // n_r
    pairs = n_b // 2
    me_r = lax.axis_index("round")
    me_b = lax.axis_index("bucket")
    pair = me_b // 2
    core = me_b % 2
    sibling = pair * 2 + 1 - core
    spans = ((0, slice(0, half)), (1, slice(0, wide)), (1, slice(wide, half)))
    quarters = (slice(0, 2), slice(2, 3), slice(3, 4))
    inner = (pair > 0) & (pair < pairs - 1)
    total_count = n_r * n_b * rows * seqs

    def remote(src, dst, send, recv, **where):
        return pltpu.make_async_remote_copy(
            src_ref=src,
            dst_ref=dst,
            send_sem=send,
            recv_sem=recv,
            device_id=where,
            device_id_type=pl.DeviceIdType.MESH,
        )

    load_y = pltpu.make_async_copy(k.y_hbm, k.yv, k.load_sem.at[0])
    load_pay = pltpu.make_async_copy(k.pay_hbm, k.pay, k.load_sem.at[1])
    load_x = pltpu.make_async_copy(k.x_hbm, k.xv, k.load_sem.at[2])
    load_y.start()
    load_pay.start()
    load_x.start()

    barrier = pltpu.get_barrier_semaphore()
    for d in range(1, n_b):
        pl.semaphore_signal(
            barrier,
            inc=1,
            device_id={"bucket": (me_b + d) % n_b},
            device_id_type=pl.DeviceIdType.MESH,
        )
    for d in range(1, n_r):
        pl.semaphore_signal(
            barrier,
            inc=1,
            device_id={"round": (me_r + d) % n_r},
            device_id_type=pl.DeviceIdType.MESH,
        )

    def order(i):
        return 2 * (i // half * wide + i % wide) + (i % half) // wide

    down = lax.broadcasted_iota(jnp.int32, (seqs, seqs), 0)
    across = lax.broadcasted_iota(jnp.int32, (seqs, seqs), 1)
    k.to_outer[...] = (order(down) == across).astype(f32).astype(bf16)

    tiles, per_row, tile, _ = k.coef_ref.shape[1:]
    for m in range(tiles):
        for c in range(tiles):
            value = jnp.zeros((tile, tile), f32)
            for t in range(per_row):
                value = value + jnp.where(k.col_ref[0, m, t] == c, k.coef_ref[0, m, t], 0.0)
            k.mixer[m * tile : (m + 1) * tile, c * tile : (c + 1) * tile] = value
    for i, piece in enumerate(split3(k.mixer[...])):
        k.mix_p[i] = dot(k.to_outer[...], piece).astype(bf16)

    def rows_of(s):
        return pl.ds(pl.multiple_of(s * part, part), part)

    def columns(j):
        return pl.ds(pl.multiple_of(j * rows, rows), rows)


    def own_copy(kind, s):
        target = (sibling, me_b + 2, me_b - 2)[kind]
        here = k.blocks.at[me_b, :, rows_of(s), :]
        return remote(here, here, k.ag_send.at[kind, s], k.ag_recv.at[me_b, s], bucket=target)

    def own_start(s):
        @pl.when(pair < pairs - 1)
        def _():
            own_copy(1, s).start()

        @pl.when(pair > 0)
        def _():
            own_copy(2, s).start()

        own_copy(0, s).start()

    def own_drain(s):
        @pl.when(pair < pairs - 1)
        def _():
            own_copy(1, s).wait_send()

        @pl.when(pair > 0)
        def _():
            own_copy(2, s).wait_send()

        own_copy(0, s).wait_send()

    def set_own(s, value):
        value = value.astype(bf16)
        for c in range(4):
            k.blocks[me_b, c, rows_of(s), :] = value[:, c * wide : (c + 1) * wide]

    load_y.wait()
    for s in range(n_r):
        value = mix(split3(k.yv[0, rows_of(s), :]), [k.mix_p[i] for i in range(3)], nt)
        k.f_y[rows_of(s), :] = value
        set_own(s, value)
        if s == 0:
            pl.semaphore_wait(barrier, n_b + n_r - 2)
        own_start(s)

    def part_of(b, s):
        return k.blocks.at[b, :, rows_of(s), :]

    def unit_of(b, u):
        return k.blocks.at[b, quarters[u]]

    def block(b, u):
        here = range(quarters[u].start, quarters[u].stop)
        return jnp.concatenate([k.blocks[b, c] for c in here], axis=1)

    def by_parts(b):
        for s in range(n_r):
            arrived(part_of(b, s), b, s)

    def by_whole(b):
        arrived(k.blocks.at[b], b, 0)

    def by_unit(b, u):
        arrived(unit_of(b, u), b, u)

    def arrived(here, b, i):
        remote(here, here, k.ag_send.at[0, 0], k.ag_recv.at[b, i], bucket=sibling).wait_recv()

    def go_on(here, b, i, step):
        return remote(here, here, k.line_send.at[b, i], k.ag_recv.at[b, i], bucket=me_b + step)

    def pass_on(here, b, i):
        return remote(here, here, k.pass_send.at[b, i], k.ag_recv.at[b, i], bucket=sibling)

    def add_product(b, u):
        h, lanes = spans[u]
        k.grad[h, :, lanes] += dot(k.pay[0, :, columns(b)], block(b, u))

    def setup():
        load_pay.wait()

        def turn(q, _):
            k.pay_out[q] = k.pay[0, :, columns(q * 2 + 1 - core)].T
            turned(q).start()
            k.pay_t[q, core] = k.pay[0, :, columns(q * 2 + core)].T
            return 0

        lax.fori_loop(0, pairs, turn, 0)
        for r in range(n_r - 1):
            place = order(lax.broadcasted_iota(jnp.int32, (seqs, half), 0))
            one_hot = (place == k.pred_ref[r : r + 1, :]).astype(f32).astype(bf16)
            k.gather[r] = one_hot
            k.spread[r] = one_hot.T
        load_x.wait()
        value = picked(split3(exact(k.xv[0], k.mixer[...])), k.to_outer[...], nt)
        k.f_x[...] = value
        for i in range(3):
            k.mix_p[i] = dot(k.mix_p[i], k.to_outer[...], nt).astype(bf16)

    def turned(q):
        return remote(
            k.pay_out.at[q],
            k.pay_t.at[q, core],
            k.turn_send.at[q],
            k.turn_recv.at[q],
            bucket=sibling,
        )


    def row_copy(d, u):
        s = (me_r + d) % n_r
        return remote(
            k.row_q.at[s, quarters[u]],
            k.row_in.at[me_r, quarters[u]],
            k.row_send.at[s, u],
            k.row_recv.at[me_r, u],
            round=s,
        )

    def row_arrival(d, u):
        s = (me_r + d) % n_r
        h, lanes = spans[u]
        here = k.row_in.at[s, quarters[u]]
        remote(here, here, k.row_send.at[s, u], k.row_recv.at[s, u], round=s).wait_recv()
        k.rows_f[s, h, :, lanes] = decode(here)

    def finish(u):
        h, lanes = spans[u]
        for d in range(1, n_r):
            s = (me_r + d) % n_r
            encode(k.grad[h, rows_of(s), lanes], k.row_q.at[s, quarters[u]])
            row_copy(d, u).start()
        squares = k.grad[h, :, lanes]
        squares = jnp.sum((squares * squares).reshape(rows // 8, 8, -1), axis=0)
        squares = sum(squares[:, i : i + wide] for i in range(0, squares.shape[1], wide))
        if u == 0:
            k.sq_b[me_b] = squares
        else:
            k.sq_b[me_b] += squares
        k.rows_f[me_r, h, :, lanes] = k.grad[h, rows_of(me_r), lanes]

    def sqb_copy(d):
        s = (me_b + d) % n_b
        here = k.sq_b.at[me_b]
        return remote(here, here, k.sqb_send.at[d], k.sqb_recv.at[me_b], bucket=s)

    def sqb_arrival(d):
        s = (me_b + d) % n_b
        here = k.sq_b.at[s]
        return remote(here, here, k.sqb_send.at[d], k.sqb_recv.at[s], bucket=s)

    def sqr_copy(d):
        s = (me_r + d) % n_r
        here = k.sq_r.at[me_r]
        return remote(here, here, k.sqr_send.at[d], k.sqr_recv.at[me_r], round=s)

    def sqr_arrival(d):
        s = (me_r + d) % n_r
        here = k.sq_r.at[s]
        return remote(here, here, k.sqr_send.at[d], k.sqr_recv.at[s], round=s)

    def back_copy(r):
        return remote(
            k.back_q.at[r], k.back_in.at[me_r], k.back_send.at[r], k.back_recv.at[me_r], round=r
        )

    def back_arrival(s):
        here = k.back_in.at[s]
        return remote(here, here, k.back_send.at[s], k.back_recv.at[s], round=s)

    def prox(sign, factor):
        for d in range(1, n_b):
            sqb_copy(d).start()
        for u in range(2):
            for d in range(1, n_r):
                row_arrival(d, u)
        for d in range(1, n_b):
            sqb_arrival(d).wait_recv()
        k.sq_r[me_r] = jnp.sum(k.sq_b[...], axis=0)
        for d in range(1, n_r):
            sqr_copy(d).start()
        for d in range(1, n_r):
            row_arrival(d, 2)
        for d in range(1, n_r):
            sqr_arrival(d).wait_recv()
        squares = jnp.sum(jnp.sum(k.sq_r[...], axis=0), axis=0, keepdims=True)
        squares = jnp.sum(squares, axis=1, keepdims=True)
        scale = sign / (factor * jnp.sqrt(squares / total_count + epsilon))

        carried = None
        shares = [None] * n_r
        for r in reversed(range(n_r)):
            norms = []
            shares[r] = []
            for h in range(2):
                values = k.rows_f[r, h] * scale
                if carried is not None:
                    values = values + carried[:, h * half : (h + 1) * half]
                even, odd = values[:, :wide], values[:, wide:]
                small = jnp.exp(-jnp.abs(even - odd))
                larger = 1.0 / (1.0 + small)
                smaller = small * larger
                ahead = even >= odd
                k.share[r, h, :, :wide] = jnp.where(ahead, larger, smaller)
                k.share[r, h, :, wide:] = jnp.where(ahead, smaller, larger)
                norms.append(jnp.maximum(even, odd) + jnp.log(1.0 + small))
            if r > 0:
                norm = jnp.concatenate(norms, axis=1)
                carried = picked(split3(norm), k.spread[r - 1])

        mass = None
        for r in range(n_r):
            halves = []
            if r > 0:
                parent = picked(split3(mass), k.gather[r - 1])
            for h in range(2):
                now = k.share[r, h]
                if r > 0:
                    above = parent[:, h * wide : (h + 1) * wide]
                    now = now * jnp.concatenate([above, above], axis=1)
                halves.append(now)
            mass = jnp.concatenate(halves, axis=1)
            code = jnp.floor(mass * top_code + 0.5).astype(jnp.int32) - shift_code
            k.back_q[r] = code.astype(jnp.int16)

            @pl.when(me_r != r)
            def _():
                back_copy(r).start()

            @pl.when(me_r == r)
            def _():
                k.back_in[me_r] = k.back_q[r]

    def prox_drain():
        for d in range(1, n_r):
            for u in range(3):
                row_copy(d, u).wait_send()
            back_copy((me_r + d) % n_r).wait_send()
            sqr_copy(d).wait_send()
        for d in range(1, n_b):
            sqb_copy(d).wait_send()

    def pieces(s):
        whole = (k.back_in[s].astype(jnp.int32) + shift_code).astype(f32)
        hi = whole.astype(bf16)
        return [hi, (whole - hi.astype(f32)).astype(bf16)]

    def mixed_part(s, state, weight, dims):
        value = mix(pieces(s), [k.mix_p[i] for i in range(3)], dims)
        value = (1.0 - weight) * state[rows_of(s), :] + (weight * (1.0 / top_code)) * value
        state[rows_of(s), :] = value
        return value

    def add_best(out, s, share):
        best = picked(pieces(s), k.to_outer[...])
        out[0, rows_of(s), :] += (share * (1.0 / top_code)) * best


    def mixed_copy(s):
        here = k.mixed.at[core, :, rows_of(s), :]
        return remote(here, here, k.mx_send.at[s], k.mx_recv.at[core, s], bucket=sibling)

    def mixed_arrival(s):
        here = k.mixed.at[1 - core, :, rows_of(s), :]
        return remote(here, here, k.mx_send.at[s], k.mx_recv.at[1 - core, s], bucket=sibling)

    def partial(q, h):
        return dot(k.pay_t[q, 0], k.mixed[0, h]) + dot(k.pay_t[q, 1], k.mixed[1, h])

    def sum_copy(way, q, u):
        return remote(
            k.sum_out.at[way, q, quarters[u]],
            k.sum_in.at[way, q, quarters[u]],
            k.sum_send.at[way, q, u],
            k.sum_recv.at[way, q, u],
            bucket=jnp.where(way == 0, me_b + 2, me_b - 2),
        )

    def sum_arrival(way, q, u):
        here = k.sum_in.at[way, q, quarters[u]]
        remote(
            here, here, k.sum_send.at[way, q, u], k.sum_recv.at[way, q, u], bucket=sibling
        ).wait_recv()
        return decode(here)

    def sum_unit(i):
        j = i // 2
        up = (i % 2 == 0) == (pair < pairs // 2)
        way = jnp.where(up, 0, 1)
        q = jnp.where(up, pairs - 1 - j, j)
        valid = jnp.where(up, q > pair, q < pair)
        fed = jnp.where(up, pair > 0, pair < pairs - 1)
        return way, q, valid, fed

    def out_copy(i, s):
        here, there = ((k.xo_ref, k.x_out), (k.yo_ref, k.y_out))[i]
        return pltpu.make_async_copy(
            here.at[:, rows_of(s)], there.at[:, rows_of(s)], k.out_sem.at[i, s]
        )

    def step(index, _):
        weight = 2.0 / (index.astype(f32) + 3.0)

        @pl.when(index == 0)
        def _():
            setup()

        outward = jnp.where(pair < pairs // 2, -2, 2)
        first = -outward
        second = jnp.where(inner, outward, -2 * outward)
        far = jnp.where(inner, -2 * outward, -3 * outward)

        for u in range(3):
            h, lanes = spans[u]
            k.grad[h, :, lanes] = dot(k.pay[0, :, columns(me_b)], block(me_b, u))
        by_parts(sibling)
        for u in range(2 + 1):
            add_product(sibling, u)

        @pl.when(index == 0)
        def _():
            for q in range(pairs):
                turned(q).wait()
            k.xo_ref[...] = (1.0 - weights[0]) * (1.0 - weights[1]) * k.xv[...]
            k.yo_ref[...] = (1.0 - weights[0]) * (1.0 - weights[1]) * k.yv[...]

        @pl.when(index == 1)
        def _():
            for s in range(n_r):
                add_best(k.yo_ref, s, weights[0] * (1.0 - weights[1]))

        def both(offset):
            for u in range(3):
                add_product(me_b + offset, u)
            by_whole(sibling + offset)
            for u in range(3):
                add_product(sibling + offset, u)

        b = me_b + first
        for s in range(n_r):
            arrived(part_of(b, s), b, s)

            @pl.when(inner)
            def _():
                go_on(part_of(b, s), b, s, outward).start()

        pass_on(k.blocks.at[b], b, 0).start()
        b2 = me_b + second

        @pl.when(inner)
        def _():
            by_parts(b2)
            for u in range(3):
                go_on(unit_of(b2, u), b2, u, -outward).start()
            pass_on(k.blocks.at[b2], b2, 0).start()

        both(first)

        @pl.when(jnp.logical_not(inner))
        def _():
            by_parts(b2)
            pass_on(k.blocks.at[b2], b2, 0).start()

        both(second)
        b3 = me_b + far
        for u in range(3):
            by_unit(b3, u)

            @pl.when(inner)
            def _():
                go_on(unit_of(b3, u), b3, u, outward).start()

            pass_on(unit_of(b3, u), b3, u).start()
            add_product(b3, u)
            by_unit(sibling + far, u)
            add_product(sibling + far, u)
            finish(u)

        @pl.when(inner)
        def _():
            for s in range(n_r):
                go_on(part_of(b, s), b, s, outward).wait_send()
            for u in range(3):
                go_on(unit_of(b2, u), b2, u, -outward).wait_send()
                go_on(unit_of(b3, u), b3, u, outward).wait_send()

        pass_on(k.blocks.at[b], b, 0).wait_send()
        pass_on(k.blocks.at[b2], b2, 0).wait_send()
        for u in range(3):
            pass_on(unit_of(b3, u), b3, u).wait_send()
        for s in range(n_r):
            own_drain(s)

        prox(-1.0, smooth_x)
        for d in range(n_r):
            s = (me_r + d) % n_r
            if d > 0:
                back_arrival(s).wait_recv()
            value = mixed_part(s, k.f_x, weight, nn).astype(bf16)
            for h in range(2):
                k.mixed[core, h, rows_of(s), :] = value[:, h * half : (h + 1) * half]
            mixed_copy(s).start()
        for d in range(n_r):
            mixed_arrival((me_r + d) % n_r).wait_recv()

        def move(i, _):
            way, q, valid, fed = sum_unit(i)

            @pl.when(valid)
            def _():
                for u in range(3):
                    if u != 2:
                        k.work[...] = partial(q, min(u, 1))
                    lanes = spans[u][1]

                    @pl.when(fed)
                    def _():
                        k.work[:, lanes] += sum_arrival(way, q, u)

                    encode(k.work[:, lanes], k.sum_out.at[way, q, quarters[u]])
                    sum_copy(way, q, u).start()

            return 0

        lax.fori_loop(0, 2 * (pairs - 1), move, 0)
        prox_drain()
        for s in range(n_r):
            mixed_copy(s).wait_send()
        share = jnp.where(index == 0, weights[0] * (1.0 - weights[1]), weights[1])
        for s in range(n_r):
            add_best(k.xo_ref, s, share)

            @pl.when(index == 1)
            def _():
                out_copy(0, s).start()

        for h in range(2):
            k.grad[h] = partial(pair, h)
        for u in range(3):
            h, lanes = spans[u]

            def add_sum(way):
                k.grad[h, :, lanes] += sum_arrival(way, pair, u)

            @pl.when(pair > 0)
            def _():
                add_sum(0)

            @pl.when(pair < pairs - 1)
            def _():
                add_sum(1)

            finish(u)

        def settle(i, _):
            way, q, valid, fed = sum_unit(i)

            @pl.when(valid)
            def _():
                for u in range(3):
                    sum_copy(way, q, u).wait_send()

            return 0

        lax.fori_loop(0, 2 * (pairs - 1), settle, 0)

        prox(1.0, smooth_y)
        for d in range(n_r):
            s = (me_r + d) % n_r
            if d > 0:
                back_arrival(s).wait_recv()

            @pl.when(index == 0)
            def _():
                set_own(s, mixed_part(s, k.f_y, weight, nt))
                own_start(s)

            @pl.when(index == 1)
            def _():
                add_best(k.yo_ref, s, weights[1])
                out_copy(1, s).start()

        prox_drain()
        return 0

    lax.fori_loop(0, 2, step, 0)
    for i in range(2):
        for s in range(n_r):
            out_copy(i, s).wait()


def place_kernel(x_in, y_in, x_out, y_out):
    x_out[...] = x_in[...]
    y_out[...] = y_in[...]


def line_body(x_start, y_start, bucket_payoff, column_blocks, public_coef, predecessor_sequences):
    n_r = lax.axis_size("round")
    n_b = lax.axis_size("bucket")
    _, rows, seqs = x_start.shape
    half = seqs // 2
    part = rows // n_r
    pairs = n_b // 2
    f32, bf16, i16 = jnp.float32, jnp.bfloat16, jnp.int16
    vmem = pl.BlockSpec(memory_space=pltpu.VMEM)
    smem = pl.BlockSpec(memory_space=pltpu.SMEM)
    hbm = pl.BlockSpec(memory_space=pl.ANY)
    dma = pltpu.SemaphoreType.DMA
    scratch = dict(
        xv=pltpu.VMEM((1, rows, seqs), f32),
        yv=pltpu.VMEM((1, rows, seqs), f32),
        xo_ref=pltpu.VMEM((1, rows, seqs), f32),
        yo_ref=pltpu.VMEM((1, rows, seqs), f32),
        pay=pltpu.VMEM((1, rows, n_b * rows), bf16),
        pay_t=pltpu.VMEM((pairs, 2, rows, rows), bf16),
        pay_out=pltpu.VMEM((pairs, rows, rows), bf16),
        blocks=pltpu.VMEM((n_b, 4, rows, half // 2), bf16),
        mixed=pltpu.VMEM((2, 2, rows, half), bf16),
        mixer=pltpu.VMEM((seqs, seqs), f32),
        mix_p=pltpu.VMEM((3, seqs, seqs), bf16),
        to_outer=pltpu.VMEM((seqs, seqs), bf16),
        gather=pltpu.VMEM((n_r - 1, seqs, half), bf16),
        spread=pltpu.VMEM((n_r - 1, half, seqs), bf16),
        f_x=pltpu.VMEM((rows, seqs), f32),
        f_y=pltpu.VMEM((rows, seqs), f32),
        grad=pltpu.VMEM((2, rows, half), f32),
        work=pltpu.VMEM((rows, half), f32),
        sum_out=pltpu.VMEM((2, pairs, 4, rows + 16, half // 2), i16),
        sum_in=pltpu.VMEM((2, pairs, 4, rows + 16, half // 2), i16),
        row_q=pltpu.VMEM((n_r, 4, part + 16, half // 2), i16),
        row_in=pltpu.VMEM((n_r, 4, part + 16, half // 2), i16),
        rows_f=pltpu.VMEM((n_r, 2, part, half), f32),
        share=pltpu.VMEM((n_r, 2, part, half), f32),
        back_q=pltpu.VMEM((n_r, part, seqs), i16),
        back_in=pltpu.VMEM((n_r, part, seqs), i16),
        sq_b=pltpu.VMEM((n_b, 8, 128), f32),
        sq_r=pltpu.VMEM((n_r, 8, 128), f32),
        load_sem=dma((3,)),
        out_sem=dma((2, n_r)),
        turn_send=dma((pairs,)),
        turn_recv=dma((pairs,)),
        ag_send=dma((3, n_r)),
        ag_recv=dma((n_b, n_r)),
        line_send=dma((n_b, n_r)),
        pass_send=dma((n_b, 3)),
        mx_send=dma((n_r,)),
        mx_recv=dma((2, n_r)),
        sum_send=dma((2, pairs, 3)),
        sum_recv=dma((2, pairs, 3)),
        row_send=dma((n_r, 3)),
        row_recv=dma((n_r, 3)),
        back_send=dma((n_r,)),
        back_recv=dma((n_r,)),
        sqb_send=dma((n_b,)),
        sqb_recv=dma((n_b,)),
        sqr_send=dma((n_r,)),
        sqr_recv=dma((n_r,)),
    )
    names = ["x_hbm", "y_hbm", "pay_hbm", "col_ref", "coef_ref", "pred_ref", "x_out", "y_out"]
    names += list(scratch)
    found = pl.pallas_call(
        functools.partial(line_kernel, names, n_r, n_b),
        out_shape=[jax.ShapeDtypeStruct(x_start.shape, f32)] * 2,
        in_specs=[hbm, hbm, hbm, smem, vmem, vmem],
        out_specs=[hbm, hbm],
        scratch_shapes=list(scratch.values()),
        compiler_params=pltpu.CompilerParams(
            collective_id=0, has_side_effects=True, vmem_limit_bytes=60 * 1024 * 1024
        ),
    )(x_start, y_start, bucket_payoff, column_blocks, public_coef, predecessor_sequences)
    block = pl.BlockSpec((1, rows // 2, seqs), lambda i: (0, i, 0))
    return pl.pallas_call(
        place_kernel,
        grid=(2,),
        out_shape=[jax.ShapeDtypeStruct(x_start.shape, f32)] * 2,
        in_specs=[block, block],
        out_specs=[block, block],
    )(*found)


def plain_kernel(
    n_r,
    n_b,
    x_ref,
    y_ref,
    pay_ref,
    col_ref,
    coef_ref,
    pred_ref,
    xo_ref,
    yo_ref,
    xs,
    ys,
    mixer,
    gather,
    pay_t,
    blocks,
    mixed,
    grad,
    sib_out,
    sib_in,
    far_out,
    far_in,
    sq_b,
    sq_r,
    rows_in,
    score,
    norm,
    mass,
    back_in,
    far_q,
    far_s,
    far_q_in,
    far_s_in,
    row_q,
    row_s,
    row_q_in,
    row_s_in,
    back_q,
    back_s,
    back_q_in,
    back_s_in,
    ag_send,
    ag_recv,
    fw_send,
    line_send,
    sib_send,
    sib_recv,
    far_send,
    far_recv,
    sqb_send,
    sqb_recv,
    sqr_send,
    sqr_recv,
    row_send,
    row_recv,
    back_send,
    back_recv,
    far_s_send,
    far_s_recv,
    row_s_send,
    row_s_recv,
    back_s_send,
    back_s_recv,
):
    rows, seqs = xs.shape
    half = seqs // 2
    part = rows // n_r
    pairs = n_b // 2
    me_r = lax.axis_index("round")
    me_b = lax.axis_index("bucket")
    pair = me_b // 2
    core = me_b % 2
    sibling = pair * 2 + 1 - core
    total_count = n_r * n_b * rows * seqs

    def remote(src, dst, send, recv, **where):
        return pltpu.make_async_remote_copy(
            src_ref=src,
            dst_ref=dst,
            send_sem=send,
            recv_sem=recv,
            device_id=where,
            device_id_type=pl.DeviceIdType.MESH,
        )

    barrier = pltpu.get_barrier_semaphore()
    for d in range(1, n_b):
        pl.semaphore_signal(
            barrier,
            inc=1,
            device_id={"bucket": (me_b + d) % n_b},
            device_id_type=pl.DeviceIdType.MESH,
        )
    for d in range(1, n_r):
        pl.semaphore_signal(
            barrier,
            inc=1,
            device_id={"round": (me_r + d) % n_r},
            device_id_type=pl.DeviceIdType.MESH,
        )
    pl.semaphore_wait(barrier, n_b + n_r - 2)

    def order(i):
        return jnp.where(i < half, 2 * i, 2 * (i - half) + 1)

    down = lax.broadcasted_iota(jnp.int32, (seqs, seqs), 0)
    across = lax.broadcasted_iota(jnp.int32, (seqs, seqs), 1)
    to_inner = (down == order(across)).astype(jnp.float32)
    to_outer = (order(down) == across).astype(jnp.float32)

    tiles, per_row, tile, _ = coef_ref.shape[1:]
    for m in range(tiles):
        for c in range(tiles):
            value = jnp.zeros((tile, tile), jnp.float32)
            for t in range(per_row):
                value = value + jnp.where(col_ref[0, m, t] == c, coef_ref[0, m, t], 0.0)
            mixer[m * tile : (m + 1) * tile, c * tile : (c + 1) * tile] = value
    mixer[...] = exact(to_outer, exact(mixer[...], to_inner))
    ys[...] = exact(y_ref[0], to_inner)
    for r in range(n_r - 1):
        place = order(lax.broadcasted_iota(jnp.int32, (seqs, half), 0))
        gather[r] = (place == pred_ref[r : r + 1, :]).astype(jnp.float32)

    def columns(j):
        return pl.ds(pl.multiple_of(j * rows, rows), rows)

    def coded(value, code_ref, scale_ref):
        top = jnp.max(jnp.abs(value), axis=0, keepdims=True)
        unit = jnp.maximum(top, 1e-30) / 32767.0
        code = jnp.floor(value * (1.0 / unit) + 0.5)
        code_ref[...] = code.astype(jnp.int32).astype(jnp.int16)
        scale_ref[...] = jnp.broadcast_to(unit, scale_ref.shape)

    def decoded(code_ref, scale_ref):
        return code_ref[...].astype(jnp.int32).astype(jnp.float32) * scale_ref[0:1, :]

    def prox(state, sign, factor, weight, short):
        def row_copy(d):
            s = (me_r + d) % n_r
            here = grad.at[pl.ds(pl.multiple_of(s * part, part), part)]
            if not short:
                return [
                    remote(here, rows_in.at[me_r], row_send.at[s], row_recv.at[me_r], round=s)
                ]
            return [
                remote(
                    row_q.at[s], row_q_in.at[me_r], row_send.at[s], row_recv.at[me_r], round=s
                ),
                remote(
                    row_s.at[s], row_s_in.at[me_r], row_s_send.at[s], row_s_recv.at[me_r], round=s
                ),
            ]

        def row_arrival(d):
            s = (me_r + d) % n_r
            if not short:
                return [
                    remote(rows_in.at[s], rows_in.at[s], row_send.at[s], row_recv.at[s], round=s)
                ]
            return [
                remote(row_q_in.at[s], row_q_in.at[s], row_send.at[s], row_recv.at[s], round=s),
                remote(
                    row_s_in.at[s], row_s_in.at[s], row_s_send.at[s], row_s_recv.at[s], round=s
                ),
            ]

        for d in range(1, n_r):
            if short:
                s = (me_r + d) % n_r
                here = pl.ds(pl.multiple_of(s * part, part), part)
                coded(grad[here, :], row_q.at[s], row_s.at[s])
            for copy in row_copy(d):
                copy.start()
        squares = grad[...]
        squares = jnp.sum((squares * squares).reshape(rows // 8, 8, seqs), axis=0)
        squares = sum(squares[:, i * 128 : (i + 1) * 128] for i in range(seqs // 128))
        sq_b[me_b] = squares

        def sqb_copy(d):
            s = (me_b + d) % n_b
            return remote(
                sq_b.at[me_b], sq_b.at[me_b], sqb_send.at[d], sqb_recv.at[me_b], bucket=s
            )

        def sqb_arrival(d):
            s = (me_b + d) % n_b
            return remote(sq_b.at[s], sq_b.at[s], sqb_send.at[d], sqb_recv.at[s], bucket=s)

        for d in range(1, n_b):
            sqb_copy(d).start()
        rows_in[me_r] = grad[pl.ds(pl.multiple_of(me_r * part, part), part), :]
        for d in range(1, n_b):
            sqb_arrival(d).wait_recv()
        sq_r[me_r] = jnp.sum(sq_b[...], axis=0)

        def sqr_copy(d):
            s = (me_r + d) % n_r
            return remote(sq_r.at[me_r], sq_r.at[me_r], sqr_send.at[d], sqr_recv.at[me_r], round=s)

        def sqr_arrival(d):
            s = (me_r + d) % n_r
            return remote(sq_r.at[s], sq_r.at[s], sqr_send.at[d], sqr_recv.at[s], round=s)

        for d in range(1, n_r):
            sqr_copy(d).start()
        for d in range(1, n_r):
            sqr_arrival(d).wait_recv()
        squares = jnp.sum(jnp.sum(sq_r[...], axis=0), axis=0, keepdims=True)
        squares = jnp.sum(squares, axis=1, keepdims=True)
        scale = sign / (factor * jnp.sqrt(squares / total_count + epsilon))
        for d in range(1, n_r):
            for copy in row_arrival(d):
                copy.wait_recv()
            if short:
                s = (me_r + d) % n_r
                rows_in[s] = decoded(row_q_in.at[s], row_s_in.at[s])

        for r in reversed(range(n_r)):
            values = rows_in[r] * scale
            if r < n_r - 1:
                values = values + exact(norm[r + 1], gather[r], nt)
            score[r] = values
            even, odd = values[:, :half], values[:, half:]
            larger = jnp.maximum(even, odd)
            norm[r] = larger + jnp.log(jnp.exp(even - larger) + jnp.exp(odd - larger))

        def back_copy(r):
            if not short:
                return [
                    remote(
                        mass.at[r], back_in.at[me_r], back_send.at[r], back_recv.at[me_r], round=r
                    )
                ]
            return [
                remote(
                    back_q.at[r], back_q_in.at[me_r], back_send.at[r], back_recv.at[me_r], round=r
                ),
                remote(
                    back_s.at[r],
                    back_s_in.at[me_r],
                    back_s_send.at[r],
                    back_s_recv.at[me_r],
                    round=r,
                ),
            ]

        def back_arrival(s):
            if not short:
                return [
                    remote(
                        back_in.at[s], back_in.at[s], back_send.at[s], back_recv.at[s], round=s
                    )
                ]
            return [
                remote(
                    back_q_in.at[s], back_q_in.at[s], back_send.at[s], back_recv.at[s], round=s
                ),
                remote(
                    back_s_in.at[s], back_s_in.at[s], back_s_send.at[s], back_s_recv.at[s], round=s
                ),
            ]

        for r in range(n_r):
            even = jnp.exp(score[r, :, :half] - norm[r])
            odd = jnp.exp(score[r, :, half:] - norm[r])
            if r > 0:
                parent = exact(mass[r - 1], gather[r - 1])
                even = parent * even
                odd = parent * odd
            mass[r, :, :half] = even
            mass[r, :, half:] = odd

            @pl.when(me_r != r)
            def _():
                if short:
                    coded(mass[r], back_q.at[r], back_s.at[r])
                for copy in back_copy(r):
                    copy.start()

        def update(s, best):
            here = pl.ds(pl.multiple_of(s * part, part), part)
            state[here, :] = (1.0 - weight) * state[here, :] + weight * best

        update(me_r, mass[me_r])
        for d in range(1, n_r):
            s = (me_r + d) % n_r
            for copy in back_arrival(s):
                copy.wait_recv()
            if short:
                update(s, decoded(back_q_in.at[s], back_s_in.at[s]))
            else:
                update(s, back_in[s])
        for d in range(1, n_r):
            for copy in row_copy(d) + back_copy((me_r + d) % n_r):
                copy.wait_send()
            sqr_copy(d).wait_send()
        for d in range(1, n_b):
            sqb_copy(d).wait_send()

    def step(index, _):
        weight = 2.0 / (index.astype(jnp.float32) + 3.0)
        short = False

        blocks[me_b] = exact(ys[...], mixer[...], nt).astype(jnp.bfloat16)

        def own_copy(kind):
            target = (sibling, me_b + 2, me_b - 2)[kind]
            return remote(
                blocks.at[me_b], blocks.at[me_b], ag_send.at[kind], ag_recv.at[me_b], bucket=target
            )

        def go_on(b, d, step):
            return remote(
                blocks.at[b], blocks.at[b], line_send.at[d], ag_recv.at[b], bucket=me_b + step
            )

        def pass_on(b, d):
            return remote(blocks.at[b], blocks.at[b], fw_send.at[d], ag_recv.at[b], bucket=sibling)

        def arrival(b):
            return remote(
                blocks.at[b], blocks.at[b], ag_send.at[0], ag_recv.at[b], bucket=sibling
            )

        def product(b):
            return jnp.dot(
                pay_ref[0, :, columns(b)], blocks[b], preferred_element_type=jnp.float32
            )

        @pl.when(pair < pairs - 1)
        def _():
            own_copy(1).start()

        @pl.when(pair > 0)
        def _():
            own_copy(2).start()

        own_copy(0).start()
        @pl.when(index == 0)
        def _():
            xs[...] = exact(x_ref[0], to_inner)

            def turn(j, _):
                pay_t[columns(j), :] = pay_ref[0, :, columns(j)].T
                return 0

            lax.fori_loop(0, n_b, turn, 0)
        grad[...] = product(me_b)
        arrival(sibling).wait_recv()
        grad[...] += product(sibling)

        def take(d, _):
            left = me_b - 2 * d
            right = me_b + 2 * d

            @pl.when(pair >= d)
            def _():
                arrival(left).wait_recv()

                @pl.when(pair < pairs - 1)
                def _():
                    go_on(left, d, 2).start()

                pass_on(left, d).start()

            @pl.when(pair + d < pairs)
            def _():
                arrival(right).wait_recv()

                @pl.when(pair > 0)
                def _():
                    go_on(right, pairs + d, -2).start()

                pass_on(right, pairs + d).start()

            def use(b, other):
                grad[...] += product(b)
                arrival(other).wait_recv()
                grad[...] += product(other)

            @pl.when(pair >= d)
            def _():
                use(left, sibling - 2 * d)

            @pl.when(pair + d < pairs)
            def _():
                use(right, sibling + 2 * d)

            return 0

        lax.fori_loop(1, pairs, take, 0)

        def drain(d, _):
            left = me_b - 2 * d
            right = me_b + 2 * d

            @pl.when(pair >= d)
            def _():
                pass_on(left, d).wait_send()

                @pl.when(pair < pairs - 1)
                def _():
                    go_on(left, d, 2).wait_send()

            @pl.when(pair + d < pairs)
            def _():
                pass_on(right, pairs + d).wait_send()

                @pl.when(pair > 0)
                def _():
                    go_on(right, pairs + d, -2).wait_send()

            return 0

        lax.fori_loop(1, pairs, drain, 0)
        own_copy(0).wait_send()

        @pl.when(pair < pairs - 1)
        def _():
            own_copy(1).wait_send()

        @pl.when(pair > 0)
        def _():
            own_copy(2).wait_send()

        prox(xs, -1.0, smooth_x, weight, short)

        mixed[...] = exact(xs[...], mixer[...]).astype(jnp.bfloat16)

        def partial(b):
            return jnp.dot(pay_t[columns(b), :], mixed[...], preferred_element_type=jnp.float32)

        def sib_copy(q):
            return remote(
                sib_out.at[q], sib_in.at[q], sib_send.at[q], sib_recv.at[q], bucket=sibling
            )

        def far_copy(q, step, target):
            slot = q if step > 0 else pairs + q
            if not short:
                return [
                    remote(
                        far_out.at[q],
                        far_in.at[slot],
                        far_send.at[q],
                        far_recv.at[slot],
                        bucket=target,
                    )
                ]
            return [
                remote(
                    far_q.at[q],
                    far_q_in.at[slot],
                    far_send.at[q],
                    far_recv.at[slot],
                    bucket=target,
                ),
                remote(
                    far_s.at[q],
                    far_s_in.at[slot],
                    far_s_send.at[q],
                    far_s_recv.at[slot],
                    bucket=target,
                ),
            ]

        def far_value(q, step):
            slot = q if step > 0 else pairs + q
            for copy in far_copy(q, step, sibling):
                copy.wait_recv()
            if short:
                return decoded(far_q_in.at[slot], far_s_in.at[slot])
            return far_in[slot]

        def to_sibling(q):
            sib_out[q] = partial(q * 2 + 1 - core)
            sib_copy(q).start()

        def move(q, step):
            far_out[q] = partial(q * 2 + core)
            sib_copy(q).wait_recv()
            far_out[q] += sib_in[q]

            @pl.when(pair > 0 if step > 0 else pair < pairs - 1)
            def _():
                far_out[q] += far_value(q, step)

            if short:
                coded(far_out[q], far_q.at[q], far_s.at[q])
            for copy in far_copy(q, step, me_b + step):
                copy.start()

        def outward(right, left):
            def one(i, _):
                @pl.when(pair < pairs - 1 - i)
                def _():
                    right(pairs - 1 - i)

                @pl.when(pair > i)
                def _():
                    left(i)

                return 0

            lax.fori_loop(0, pairs - 1, one, 0)

        def far_done(q, step):
            for copy in far_copy(q, step, me_b + step):
                copy.wait_send()

        outward(to_sibling, to_sibling)
        outward(lambda q: move(q, 2), lambda q: move(q, -2))
        to_sibling(pair)
        grad[...] = partial(me_b)
        sib_copy(pair).wait_recv()
        grad[...] += sib_in[pair]

        @pl.when(pair > 0)
        def _():
            grad[...] += far_value(pair, 2)

        @pl.when(pair < pairs - 1)
        def _():
            grad[...] += far_value(pair, -2)

        outward(lambda q: far_done(q, 2), lambda q: far_done(q, -2))
        for q in range(pairs):
            sib_copy(q).wait_send()
        prox(ys, 1.0, smooth_y, weight, short)
        return 0

    lax.fori_loop(0, 2, step, 0)
    down = lax.broadcasted_iota(jnp.int32, (seqs, seqs), 0)
    across = lax.broadcasted_iota(jnp.int32, (seqs, seqs), 1)
    to_outer = (order(down) == across).astype(jnp.float32)
    xo_ref[0] = exact(xs[...], to_outer)
    yo_ref[0] = exact(ys[...], to_outer)


def plain_body(x_start, y_start, bucket_payoff, column_blocks, public_coef, predecessor_sequences):
    n_r = lax.axis_size("round")
    n_b = lax.axis_size("bucket")
    _, rows, seqs = x_start.shape
    part = rows // n_r
    pairs = n_b // 2
    f32, bf16 = jnp.float32, jnp.bfloat16
    vmem = pl.BlockSpec(memory_space=pltpu.VMEM)
    smem = pl.BlockSpec(memory_space=pltpu.SMEM)
    dma = pltpu.SemaphoreType.DMA
    return pl.pallas_call(
        functools.partial(plain_kernel, n_r, n_b),
        out_shape=[jax.ShapeDtypeStruct(x_start.shape, f32)] * 2,
        in_specs=[vmem, vmem, vmem, smem, vmem, vmem],
        out_specs=[vmem, vmem],
        scratch_shapes=[
            pltpu.VMEM((rows, seqs), f32),
            pltpu.VMEM((rows, seqs), f32),
            pltpu.VMEM((seqs, seqs), f32),
            pltpu.VMEM((n_r - 1, seqs, seqs // 2), f32),
            pltpu.VMEM((n_b * rows, rows), bf16),
            pltpu.VMEM((n_b, rows, seqs), bf16),
            pltpu.VMEM((rows, seqs), bf16),
            pltpu.VMEM((rows, seqs), f32),
            pltpu.VMEM((pairs, rows, seqs), f32),
            pltpu.VMEM((pairs, rows, seqs), f32),
            pltpu.VMEM((pairs, rows, seqs), f32),
            pltpu.VMEM((2 * pairs, rows, seqs), f32),
            pltpu.VMEM((n_b, 8, 128), f32),
            pltpu.VMEM((n_r, 8, 128), f32),
            pltpu.VMEM((n_r, part, seqs), f32),
            pltpu.VMEM((n_r, part, seqs), f32),
            pltpu.VMEM((n_r, part, seqs // 2), f32),
            pltpu.VMEM((n_r, part, seqs), f32),
            pltpu.VMEM((n_r, part, seqs), f32),
            pltpu.VMEM((16, 128), jnp.int16),
            pltpu.VMEM((pairs, 8, seqs), f32),
            pltpu.VMEM((16, 128), jnp.int16),
            pltpu.VMEM((2 * pairs, 8, seqs), f32),
            pltpu.VMEM((16, 128), jnp.int16),
            pltpu.VMEM((n_r, 8, seqs), f32),
            pltpu.VMEM((16, 128), jnp.int16),
            pltpu.VMEM((n_r, 8, seqs), f32),
            pltpu.VMEM((16, 128), jnp.int16),
            pltpu.VMEM((n_r, 8, seqs), f32),
            pltpu.VMEM((16, 128), jnp.int16),
            pltpu.VMEM((n_r, 8, seqs), f32),
            dma((3,)),
            dma((n_b,)),
            dma((2 * pairs,)),
            dma((2 * pairs,)),
            dma((pairs,)),
            dma((pairs,)),
            dma((pairs,)),
            dma((2 * pairs,)),
            dma((n_b,)),
            dma((n_b,)),
            dma((n_r,)),
            dma((n_r,)),
            dma((n_r,)),
            dma((n_r,)),
            dma((n_r,)),
            dma((n_r,)),
            dma((pairs,)),
            dma((2 * pairs,)),
            dma((n_r,)),
            dma((n_r,)),
            dma((n_r,)),
            dma((n_r,)),
        ],
        compiler_params=pltpu.CompilerParams(
            collective_id=0, has_side_effects=True, vmem_limit_bytes=60 * 1024 * 1024
        ),
    )(x_start, y_start, bucket_payoff, column_blocks, public_coef, predecessor_sequences)


def solution(mesh):
    in_specs = (
        P("round", "bucket", None),
        P("round", "bucket", None),
        P("round", "bucket", None),
        P("round", None, None),
        P("round", None, None, None, None),
        P(),
    )
    out_specs = (P("round", "bucket", None), P("round", "bucket", None))

    line = mesh.shape["round"] == 4 and mesh.shape["bucket"] == 8

    def run(*arrays):
        return tuple(
            jax.shard_map(
                line_body if line else plain_body, mesh=mesh, in_specs=in_specs, out_specs=out_specs, check_vma=False
            )(*arrays)
        )

    return run
```

```python
import functools
import types

import jax
import jax.numpy as jnp
from jax import lax
from jax.experimental import pallas as pl
from jax.experimental.pallas import tpu as pltpu
from jax.sharding import PartitionSpec as P

smooth_x = 0.1
smooth_y = 0.1
epsilon = 1e-06
highest = lax.Precision.HIGHEST
nn = (((1,), (0,)), ((), ()))
nt = (((1,), (1,)), ((), ()))


def exact(a, b, dims=nn):
    return lax.dot_general(a, b, dims, precision=highest, preferred_element_type=jnp.float32)


weights = (2.0 / 3.0, 2.0 / 4.0)
top_code = 65535.0
shift_code = 32768


def split3(value):
    hi = value.astype(jnp.bfloat16)
    left = value - hi.astype(jnp.float32)
    mid = left.astype(jnp.bfloat16)
    lo = (left - mid.astype(jnp.float32)).astype(jnp.bfloat16)
    return [hi, mid, lo]


def dot(a, b, dims=nn):
    return lax.dot_general(a, b, dims, preferred_element_type=jnp.float32)


def picked(parts, one_hot, dims=nn):
    size = parts[0].shape[0]
    out = dot(jnp.concatenate(parts, axis=0), one_hot, dims)
    return sum(out[i * size : (i + 1) * size] for i in range(len(parts)))


def mix(parts, factors, dims):
    size = parts[0].shape[0]
    total = None
    for i, factor in reversed(list(enumerate(factors))):
        count = min(len(parts), 3 - i)
        out = dot(jnp.concatenate(parts[:count], axis=0), factor, dims)
        for j in reversed(range(count)):
            term = out[j * size : (j + 1) * size]
            total = term if total is None else total + term
    return total


def encode(value, code_ref):
    if len(code_ref.shape) == 3:
        wide = code_ref.shape[2]
        for i in range(code_ref.shape[0]):
            encode(value[:, i * wide : (i + 1) * wide], code_ref.at[i])
        return
    rows = value.shape[0]
    top = jnp.maximum(jnp.max(jnp.abs(value), axis=0, keepdims=True), 1e-30)
    power = jnp.floor(256.0 * jnp.log2(top * (1.0 / 32767.0))) + 1.0
    code = jnp.floor(value * jnp.exp2(power * (-1.0 / 256.0)) + 0.5)
    code_ref[:rows, :] = code.astype(jnp.int32).astype(jnp.int16)
    power = jnp.broadcast_to(power, (16, value.shape[1]))
    code_ref[rows:, :] = power.astype(jnp.int32).astype(jnp.int16)


def decode(code_ref):
    if len(code_ref.shape) == 3:
        return jnp.concatenate([decode(code_ref.at[i]) for i in range(code_ref.shape[0])], axis=1)
    rows = code_ref.shape[0] - 16
    power = code_ref[rows:, :].astype(jnp.int32).astype(jnp.float32)[0:1, :]
    unit = jnp.exp2(power * (1.0 / 256.0))
    return code_ref[:rows, :].astype(jnp.int32).astype(jnp.float32) * unit


def line_kernel(names, n_r, n_b, *refs):
    k = types.SimpleNamespace(**dict(zip(names, refs)))
    f32, bf16 = jnp.float32, jnp.bfloat16
    _, rows, seqs = k.x_hbm.shape
    half = seqs // 2
    wide = half // 2
    part = rows // n_r
    pairs = n_b // 2
    me_r = lax.axis_index("round")
    me_b = lax.axis_index("bucket")
    pair = me_b // 2
    core = me_b % 2
    sibling = pair * 2 + 1 - core
    spans = ((0, slice(0, half)), (1, slice(0, wide)), (1, slice(wide, half)))
    quarters = (slice(0, 2), slice(2, 3), slice(3, 4))
    members = ((0, 1), (2,), (3,))
    outward = jnp.where(pair < pairs // 2, -2, 2)
    end_chip = jnp.where(pair < pairs // 2, 0, pairs - 1)
    facing = pair - outward // 2
    far_end = pairs - 1 - end_chip
    inner = (pair > 0) & (pair < pairs - 1)
    total_count = n_r * n_b * rows * seqs

    def remote(src, dst, send, recv, **where):
        return pltpu.make_async_remote_copy(
            src_ref=src,
            dst_ref=dst,
            send_sem=send,
            recv_sem=recv,
            device_id=where,
            device_id_type=pl.DeviceIdType.MESH,
        )

    load_y = pltpu.make_async_copy(k.y_hbm, k.yv, k.load_sem.at[0])
    load_pay = pltpu.make_async_copy(k.pay_hbm, k.pay, k.load_sem.at[1])
    load_x = pltpu.make_async_copy(k.x_hbm, k.xv, k.load_sem.at[2])
    load_y.start()
    load_pay.start()
    load_x.start()

    barrier = pltpu.get_barrier_semaphore()
    for d in range(1, n_b):
        pl.semaphore_signal(
            barrier,
            inc=1,
            device_id={"bucket": (me_b + d) % n_b},
            device_id_type=pl.DeviceIdType.MESH,
        )
    for d in range(1, n_r):
        pl.semaphore_signal(
            barrier,
            inc=1,
            device_id={"round": (me_r + d) % n_r},
            device_id_type=pl.DeviceIdType.MESH,
        )

    def order(i):
        return 2 * (i // half * wide + i % wide) + (i % half) // wide

    down = lax.broadcasted_iota(jnp.int32, (seqs, seqs), 0)
    across = lax.broadcasted_iota(jnp.int32, (seqs, seqs), 1)
    k.to_outer[...] = (order(down) == across).astype(f32).astype(bf16)

    tiles, per_row, tile, _ = k.coef_ref.shape[1:]
    for m in range(tiles):
        for c in range(tiles):
            value = jnp.zeros((tile, tile), f32)
            for t in range(per_row):
                value = value + jnp.where(k.col_ref[0, m, t] == c, k.coef_ref[0, m, t], 0.0)
            k.mixer[m * tile : (m + 1) * tile, c * tile : (c + 1) * tile] = value
    for i, piece in enumerate(split3(k.mixer[...])):
        k.mix_p[i] = dot(k.to_outer[...], piece).astype(bf16)

    def rows_of(s):
        return pl.ds(pl.multiple_of(s * part, part), part)

    def columns(j):
        return pl.ds(pl.multiple_of(j * rows, rows), rows)

    away = jnp.where(pair < pairs // 2, pairs // 2, 0)

    def lent_place(o):
        return (far_end - away, 1 - (far_end - away))[o]

    def lend(turn):
        o, i, p = turn // 4, turn // 2 % 2, turn % 2
        here = pl.ds(p * (rows // 2), rows // 2)
        b = 2 * lent_place(o) + i
        return remote(
            k.pay.at[0, here, columns(2 * away + b)],
            k.lent.at[b, here],
            k.lend_send.at[turn],
            k.lend_recv.at[turn],
            bucket=me_b - outward,
        )

    def lend_start(turns):
        @pl.when(jnp.logical_not(inner))
        def _():
            for turn in turns:
                lend(turn).start()

    def lent_swap(j, o):
        return remote(
            k.pay_out.at[j],
            k.lent_t.at[j, core],
            k.swap_send.at[o],
            k.swap_recv.at[o],
            bucket=sibling,
        )

    def take_lent(o):
        j = lent_place(o)
        for i in range(2):
            for p in range(2):
                here = k.lent.at[2 * j + i, pl.ds(p * (rows // 2), rows // 2)]
                turn = 4 * o + 2 * i + p
                remote(
                    here, here, k.lend_send.at[turn], k.lend_recv.at[turn], bucket=sibling
                ).wait_recv()
        k.pay_out[j] = k.lent[2 * j + 1 - core].T
        lent_swap(j, o).start()
        k.lent_t[j, core] = k.lent[2 * j + core].T
        lent_swap(j, o).wait()


    def own_copy(kind, s):
        target = (sibling, me_b + 2, me_b - 2)[kind]
        here = k.blocks.at[me_b, :, rows_of(s), :]
        return remote(here, here, k.ag_send.at[kind, s], k.ag_recv.at[me_b, s], bucket=target)

    def own_start(s):
        @pl.when(pair < pairs - 1)
        def _():
            own_copy(1, s).start()

        @pl.when(pair > 0)
        def _():
            own_copy(2, s).start()

        own_copy(0, s).start()

    def own_drain(s):
        @pl.when(pair < pairs - 1)
        def _():
            own_copy(1, s).wait_send()

        @pl.when(pair > 0)
        def _():
            own_copy(2, s).wait_send()

        own_copy(0, s).wait_send()

    def set_own(s, value):
        value = value.astype(bf16)
        for c in range(4):
            k.blocks[me_b, c, rows_of(s), :] = value[:, c * wide : (c + 1) * wide]

    pl.semaphore_wait(barrier, n_b + n_r - 2)
    load_y.wait()
    load_pay.wait()
    lend_start(range(1))
    for s in range(n_r):
        value = mix(split3(k.yv[0, rows_of(s), :]), [k.mix_p[i] for i in range(3)], nt)
        k.f_y[rows_of(s), :] = value
        set_own(s, value)
        own_start(s)

    def part_of(b, s):
        return k.blocks.at[b, :, rows_of(s), :]

    def unit_of(b, c):
        return k.blocks.at[b, c]

    def block(b, u):
        return jnp.concatenate([k.blocks[b, c] for c in members[u]], axis=1)

    def by_parts(b):
        for s in range(n_r):
            arrived(part_of(b, s), b, s)

    def by_whole(b):
        arrived(k.blocks.at[b], b, 0)

    def by_unit(b, c):
        arrived(unit_of(b, c), b, c)

    def arrived(here, b, i):
        remote(here, here, k.ag_send.at[0, 0], k.ag_recv.at[b, i], bucket=sibling).wait_recv()

    def go_on(here, b, i, step):
        return remote(here, here, k.line_send.at[b, i], k.ag_recv.at[b, i], bucket=me_b + step)

    def pass_on(here, b, i):
        return remote(here, here, k.pass_send.at[b, i], k.ag_recv.at[b, i], bucket=sibling)

    def add_product(b, u):
        value = dot(k.pay[0, :, columns(b)], block(b, u))
        for i, c in enumerate(members[u]):
            k.grad[c] += value[:, i * wide : (i + 1) * wide]

    def lent_product(b, c):
        return dot(k.lent[b - 2 * away], k.blocks[b, c])

    def setup():
        lend_start(range(1, 5))


        def turn(q, _):
            k.pay_out[q] = k.pay[0, :, columns(q * 2 + 1 - core)].T
            turned(q).start()
            k.pay_t[q, core] = k.pay[0, :, columns(q * 2 + core)].T
            return 0

        lax.fori_loop(0, pairs, turn, 0)
        for r in range(n_r - 1):
            place = order(lax.broadcasted_iota(jnp.int32, (seqs, half), 0))
            one_hot = (place == k.pred_ref[r : r + 1, :]).astype(f32).astype(bf16)
            k.gather[r] = one_hot
            k.spread[r] = one_hot.T
        load_x.wait()
        value = picked(split3(exact(k.xv[0], k.mixer[...])), k.to_outer[...], nt)
        k.f_x[...] = value
        for i in range(3):
            k.mix_p[i] = dot(k.mix_p[i], k.to_outer[...], nt).astype(bf16)

    def turned(q):
        return remote(
            k.pay_out.at[q],
            k.pay_t.at[q, core],
            k.turn_send.at[q],
            k.turn_recv.at[q],
            bucket=sibling,
        )


    def row_copy(d, u):
        s = (me_r + d) % n_r
        return remote(
            k.row_q.at[s, quarters[u]],
            k.row_in.at[me_r, quarters[u]],
            k.row_send.at[s, u],
            k.row_recv.at[me_r, u],
            round=s,
        )

    def row_arrival(d, u):
        s = (me_r + d) % n_r
        h, lanes = spans[u]
        here = k.row_in.at[s, quarters[u]]
        remote(here, here, k.row_send.at[s, u], k.row_recv.at[s, u], round=s).wait_recv()
        k.rows_f[s, h, :, lanes] = decode(here)

    def finish(u):
        for d in range(1, n_r):
            s = (me_r + d) % n_r
            for c in members[u]:
                encode(k.grad[c, rows_of(s), :], k.row_q.at[s, c])
            row_copy(d, u).start()
        for c in members[u]:
            squares = k.grad[c]
            squares = jnp.sum((squares * squares).reshape(rows // 8, 8, wide), axis=0)
            if c == 0:
                k.sq_b[me_b] = squares
            else:
                k.sq_b[me_b] += squares
            h, lanes = c // 2, slice(c % 2 * wide, c % 2 * wide + wide)
            k.rows_f[me_r, h, :, lanes] = k.grad[c, rows_of(me_r), :]

    def sqb_copy(d):
        s = (me_b + d) % n_b
        here = k.sq_b.at[me_b]
        return remote(here, here, k.sqb_send.at[d], k.sqb_recv.at[me_b], bucket=s)

    def sqb_arrival(d):
        s = (me_b + d) % n_b
        here = k.sq_b.at[s]
        return remote(here, here, k.sqb_send.at[d], k.sqb_recv.at[s], bucket=s)

    def sqr_copy(d):
        s = (me_r + d) % n_r
        here = k.sq_r.at[me_r]
        return remote(here, here, k.sqr_send.at[d], k.sqr_recv.at[me_r], round=s)

    def sqr_arrival(d):
        s = (me_r + d) % n_r
        here = k.sq_r.at[s]
        return remote(here, here, k.sqr_send.at[d], k.sqr_recv.at[s], round=s)

    def back_copy(r):
        return remote(
            k.back_q.at[r], k.back_in.at[me_r], k.back_send.at[r], k.back_recv.at[me_r], round=r
        )

    def back_arrival(s):
        here = k.back_in.at[s]
        return remote(here, here, k.back_send.at[s], k.back_recv.at[s], round=s)

    def prox(sign, factor, after_scale=None):
        for d in range(1, n_b):
            sqb_copy(d).start()
        for u in range(2):
            for d in range(1, n_r):
                row_arrival(d, u)
        for d in range(1, n_b):
            sqb_arrival(d).wait_recv()
        k.sq_r[me_r] = jnp.sum(k.sq_b[...], axis=0)
        for d in range(1, n_r):
            sqr_copy(d).start()
        for d in range(1, n_r):
            row_arrival(d, 2)
        for d in range(1, n_r):
            sqr_arrival(d).wait_recv()
        squares = jnp.sum(jnp.sum(k.sq_r[...], axis=0), axis=0, keepdims=True)
        squares = jnp.sum(squares, axis=1, keepdims=True)
        scale = sign / (factor * jnp.sqrt(squares / total_count + epsilon))

        if after_scale is not None:
            after_scale()
        carried = None
        shares = [None] * n_r
        for r in reversed(range(n_r)):
            norms = []
            shares[r] = []
            for h in range(2):
                values = k.rows_f[r, h] * scale
                if carried is not None:
                    values = values + carried[:, h * half : (h + 1) * half]
                even, odd = values[:, :wide], values[:, wide:]
                small = jnp.exp(-jnp.abs(even - odd))
                larger = 1.0 / (1.0 + small)
                smaller = small * larger
                ahead = even >= odd
                k.share[r, h, :, :wide] = jnp.where(ahead, larger, smaller)
                k.share[r, h, :, wide:] = jnp.where(ahead, smaller, larger)
                norms.append(jnp.maximum(even, odd) + jnp.log(1.0 + small))
            if r > 0:
                norm = jnp.concatenate(norms, axis=1)
                carried = picked(split3(norm), k.spread[r - 1])

        mass = None
        for r in range(n_r):
            halves = []
            if r > 0:
                parent = picked(split3(mass), k.gather[r - 1])
            for h in range(2):
                now = k.share[r, h]
                if r > 0:
                    above = parent[:, h * wide : (h + 1) * wide]
                    now = now * jnp.concatenate([above, above], axis=1)
                halves.append(now)
            mass = jnp.concatenate(halves, axis=1)
            code = jnp.floor(mass * top_code + 0.5).astype(jnp.int32) - shift_code
            k.back_q[r] = code.astype(jnp.int16)

            @pl.when(me_r != r)
            def _():
                back_copy(r).start()

            @pl.when(me_r == r)
            def _():
                k.back_in[me_r] = k.back_q[r]

    def prox_drain():
        for d in range(1, n_r):
            for u in range(3):
                row_copy(d, u).wait_send()
            back_copy((me_r + d) % n_r).wait_send()
            sqr_copy(d).wait_send()
        for d in range(1, n_b):
            sqb_copy(d).wait_send()

    def pieces(s):
        whole = (k.back_in[s].astype(jnp.int32) + shift_code).astype(f32)
        hi = whole.astype(bf16)
        return [hi, (whole - hi.astype(f32)).astype(bf16)]

    def mixed_part(s, state, weight, dims):
        value = mix(pieces(s), [k.mix_p[i] for i in range(3)], dims)
        value = (1.0 - weight) * state[rows_of(s), :] + (weight * (1.0 / top_code)) * value
        state[rows_of(s), :] = value
        return value

    def add_best(out, s, share):
        best = picked(pieces(s), k.to_outer[...])
        out[0, rows_of(s), :] += (share * (1.0 / top_code)) * best


    def mixed_copy(s):
        here = k.mixed.at[core, :, rows_of(s), :]
        return remote(here, here, k.mx_send.at[s], k.mx_recv.at[core, s], bucket=sibling)

    def mixed_arrival(s):
        here = k.mixed.at[1 - core, :, rows_of(s), :]
        return remote(here, here, k.mx_send.at[s], k.mx_recv.at[1 - core, s], bucket=sibling)

    def raw_copy(n):
        return remote(
            k.mixed.at[core, n],
            k.mixed.at[2 + core, n],
            k.raw_send.at[n],
            k.raw_recv.at[core, n],
            bucket=me_b - outward,
        )

    def raw_pass(n):
        here = k.mixed.at[2 + core, n]
        return remote(here, here, k.raw_send.at[n], k.raw_recv.at[core, n], bucket=sibling)

    def raw_arrival(source, n):
        here = k.mixed.at[2 + source, n]
        remote(
            here, here, k.raw_send.at[n], k.raw_recv.at[source, n], bucket=sibling
        ).wait_recv()

    def partial(q, n):
        return dot(k.pay_t[q, 0], k.mixed[0, n]) + dot(k.pay_t[q, 1], k.mixed[1, n])

    def lent_partial(j, n):
        return dot(k.lent_t[j, 0], k.mixed[2, n]) + dot(k.lent_t[j, 1], k.mixed[3, n])

    def sum_copy(kind, n, step):
        return remote(
            k.sum_out.at[kind, n],
            k.sum_in.at[kind, n],
            k.sum_send.at[kind, n],
            k.sum_recv.at[kind, n],
            bucket=me_b + step,
        )

    def sum_arrival(kind, n):
        here = k.sum_in.at[kind, n]
        remote(
            here, here, k.sum_send.at[kind, n], k.sum_recv.at[kind, n], bucket=sibling
        ).wait_recv()
        return decode(here)

    def sums_of_end(index):
        for n in range(4):
            raw_copy(n).start()

        def lend_sum(n, _):
            k.work[...] = partial(facing - outward // 2, n)
            encode(k.work[...], k.sum_out.at[4, n])
            sum_copy(4, n, -outward).start()
            return 0

        @pl.when(index == 0)
        def _():
            lax.fori_loop(0, 4, lend_sum, 0)

        def give(n, _):
            k.work[...] = partial(facing, n)
            encode(k.work[...], k.sum_out.at[3, n])
            sum_copy(3, n, -outward).start()
            return 0

        lax.fori_loop(0, 4, give, 0)

    def sums_of_inner(index):
        def give(i, _):
            n = i % 4

            @pl.when(i < 4)
            def _():
                raw_arrival(core, n)
                raw_pass(n).start()

            q = jnp.where(i < 4, far_end, facing)
            k.work[...] = partial(q, n)

            @pl.when(i < 4)
            def _():
                raw_arrival(1 - core, n)

            @pl.when((i < 4) | (index == 1))
            def _():
                k.work[...] += lent_partial(q - away, n)

            @pl.when((i >= 4) & (index == 0))
            def _():
                k.work[...] += sum_arrival(4, n)

            encode(k.work[...], k.sum_out.at[i // 4, n])
            sum_copy(i // 4, n, -outward).start()

            @pl.when((i >= 2) & (i < 6))
            def _():
                k.work[...] = partial(end_chip, i - 2)
                k.work[...] += sum_arrival(0, i - 2)
                encode(k.work[...], k.sum_out.at[2, i - 2])
                sum_copy(2, i - 2, outward).start()

            return 0

        lax.fori_loop(0, 8, give, 0)

    def sums_drain(index):
        @pl.when(inner)
        def _():
            for n in range(4):
                raw_pass(n).wait_send()
                sum_copy(0, n, -outward).wait_send()
                sum_copy(1, n, -outward).wait_send()
                sum_copy(2, n, outward).wait_send()

        @pl.when(jnp.logical_not(inner))
        def _():
            for n in range(4):
                raw_copy(n).wait_send()
                sum_copy(3, n, -outward).wait_send()

                @pl.when(index == 0)
                def _():
                    sum_copy(4, n, -outward).wait_send()

    def out_copy(i, s):
        here, there = ((k.xo_ref, k.x_out), (k.yo_ref, k.y_out))[i]
        return pltpu.make_async_copy(
            here.at[:, rows_of(s)], there.at[:, rows_of(s)], k.out_sem.at[i, s]
        )

    def step(index, _):
        weight = 2.0 / (index.astype(f32) + 3.0)

        @pl.when(index == 0)
        def _():
            setup()

        first = -outward
        second = jnp.where(inner, outward, -2 * outward)
        far = jnp.where(inner, -2 * outward, -3 * outward)

        for u in range(3):
            value = dot(k.pay[0, :, columns(me_b)], block(me_b, u))
            for i, c in enumerate(members[u]):
                k.grad[c] = value[:, i * wide : (i + 1) * wide]
        by_parts(sibling)
        for u in range(2 + 1):
            add_product(sibling, u)

        @pl.when(index == 0)
        def _():
            for q in range(pairs):
                turned(q).wait()
            k.xo_ref[...] = (1.0 - weights[0]) * (1.0 - weights[1]) * k.xv[...]
            k.yo_ref[...] = (1.0 - weights[0]) * (1.0 - weights[1]) * k.yv[...]

        @pl.when(index == 1)
        def _():
            for s in range(n_r):
                add_best(k.yo_ref, s, weights[0] * (1.0 - weights[1]))

        def both(offset):
            for u in range(3):
                add_product(me_b + offset, u)
            by_whole(sibling + offset)
            for u in range(3):
                add_product(sibling + offset, u)

        plain = index == 0
        b = me_b + first
        for s in range(n_r):
            arrived(part_of(b, s), b, s)

            @pl.when(inner & plain)
            def _():
                go_on(part_of(b, s), b, s, outward).start()

        pass_on(k.blocks.at[b], b, 0).start()
        b2 = me_b + second

        @pl.when(inner)
        def _():
            by_parts(b2)
            for c in range(4):
                go_on(unit_of(b2, c), b2, c, -outward).start()
            pass_on(k.blocks.at[b2], b2, 0).start()

        both(first)

        @pl.when(jnp.logical_not(inner) & plain)
        def _():
            by_parts(b2)
            pass_on(k.blocks.at[b2], b2, 0).start()

        @pl.when(inner | plain)
        def _():
            both(second)

        @pl.when(inner & jnp.logical_not(plain))
        def _():
            take_lent(1)
            for c in range(4):
                k.early[c] = lent_product(b, c) + lent_product(sibling + first, c)

        b3 = me_b + far
        for c in range(4):

            @pl.when(inner | plain)
            def _():
                by_unit(b3, c)

                @pl.when(inner & plain)
                def _():
                    go_on(unit_of(b3, c), b3, c, outward).start()

                pass_on(unit_of(b3, c), b3, c).start()

                @pl.when(plain)
                def _():
                    k.grad[c] += dot(k.pay[0, :, columns(b3)], k.blocks[b3, c])

                by_unit(sibling + far, c)

                @pl.when(jnp.logical_not(plain))
                def _():
                    k.early[c] += lent_product(b3, c) + lent_product(sibling + far, c)
                    encode(k.early[c], k.sum_out.at[5, c])
                    sum_copy(5, c, outward).start()
                    k.grad[c] += dot(k.pay[0, :, columns(b3)], k.blocks[b3, c])

                k.grad[c] += dot(k.pay[0, :, columns(sibling + far)], k.blocks[sibling + far, c])

            @pl.when(jnp.logical_not(inner | plain))
            def _():
                k.grad[c] += sum_arrival(5, c)

            if c > 0:
                finish(c - 1)

        @pl.when(inner & plain)
        def _():
            for c in range(4):
                go_on(part_of(b, c), b, c, outward).wait_send()
                go_on(unit_of(b3, c), b3, c, outward).wait_send()

        @pl.when(inner)
        def _():
            for c in range(4):
                go_on(unit_of(b2, c), b2, c, -outward).wait_send()

        pass_on(k.blocks.at[b], b, 0).wait_send()

        @pl.when(inner | plain)
        def _():
            pass_on(k.blocks.at[b2], b2, 0).wait_send()
            for c in range(4):
                pass_on(unit_of(b3, c), b3, c).wait_send()

        @pl.when(inner & jnp.logical_not(plain))
        def _():
            for c in range(4):
                sum_copy(5, c, outward).wait_send()

        @pl.when(jnp.logical_not(inner | plain))
        def _():
            for turn in range(8):
                lend(turn).wait_send()

        for s in range(n_r):
            own_drain(s)

        def lend_more(turns):
            @pl.when(index == 0)
            def _():
                lend_start(turns)

        prox(-1.0, smooth_x, functools.partial(lend_more, range(5, 7)))
        for d in range(n_r):
            s = (me_r + d) % n_r
            if d > 0:
                back_arrival(s).wait_recv()
            value = mixed_part(s, k.f_x, weight, nn).astype(bf16)
            for c in range(4):
                k.mixed[core, c, rows_of(s), :] = value[:, c * wide : (c + 1) * wide]
            mixed_copy(s).start()
        for d in range(n_r):
            mixed_arrival((me_r + d) % n_r).wait_recv()

        @pl.when(inner)
        def _():
            @pl.when(index == 0)
            def _():
                take_lent(0)

            sums_of_inner(index)

        @pl.when(jnp.logical_not(inner))
        def _():
            sums_of_end(index)

        prox_drain()
        for s in range(n_r):
            mixed_copy(s).wait_send()
        share = jnp.where(index == 0, weights[0] * (1.0 - weights[1]), weights[1])
        for s in range(n_r):
            add_best(k.xo_ref, s, share)

            @pl.when(index == 1)
            def _():
                out_copy(0, s).start()

        for n in range(4):
            k.grad[n] = partial(pair, n)
        for u in range(3):
            for n in members[u]:

                @pl.when(inner)
                def _():
                    k.grad[n] += sum_arrival(3, n)
                    k.grad[n] += sum_arrival(1, n)

                @pl.when(jnp.logical_not(inner))
                def _():
                    k.grad[n] += sum_arrival(2, n)

            finish(u)
        sums_drain(index)

        prox(1.0, smooth_y, functools.partial(lend_more, range(7, 8)))
        for d in range(n_r):
            s = (me_r + d) % n_r
            if d > 0:
                back_arrival(s).wait_recv()

            @pl.when(index == 0)
            def _():
                set_own(s, mixed_part(s, k.f_y, weight, nt))
                own_start(s)

            @pl.when(index == 1)
            def _():
                add_best(k.yo_ref, s, weights[1])
                out_copy(1, s).start()

        prox_drain()
        return 0

    lax.fori_loop(0, 2, step, 0)
    for i in range(2):
        for s in range(n_r):
            out_copy(i, s).wait()


def place_kernel(x_in, y_in, x_out, y_out):
    x_out[...] = x_in[...]
    y_out[...] = y_in[...]


def line_body(x_start, y_start, bucket_payoff, column_blocks, public_coef, predecessor_sequences):
    n_r = lax.axis_size("round")
    n_b = lax.axis_size("bucket")
    _, rows, seqs = x_start.shape
    half = seqs // 2
    part = rows // n_r
    pairs = n_b // 2
    f32, bf16, i16 = jnp.float32, jnp.bfloat16, jnp.int16
    vmem = pl.BlockSpec(memory_space=pltpu.VMEM)
    smem = pl.BlockSpec(memory_space=pltpu.SMEM)
    hbm = pl.BlockSpec(memory_space=pl.ANY)
    dma = pltpu.SemaphoreType.DMA
    scratch = dict(
        xv=pltpu.VMEM((1, rows, seqs), f32),
        yv=pltpu.VMEM((1, rows, seqs), f32),
        xo_ref=pltpu.VMEM((1, rows, seqs), f32),
        yo_ref=pltpu.VMEM((1, rows, seqs), f32),
        pay=pltpu.VMEM((1, rows, n_b * rows), bf16),
        pay_t=pltpu.VMEM((pairs, 2, rows, rows), bf16),
        pay_out=pltpu.VMEM((pairs, rows, rows), bf16),
        blocks=pltpu.VMEM((n_b, 4, rows, half // 2), bf16),
        mixed=pltpu.VMEM((4, 4, rows, half // 2), bf16),
        mixer=pltpu.VMEM((seqs, seqs), f32),
        mix_p=pltpu.VMEM((3, seqs, seqs), bf16),
        to_outer=pltpu.VMEM((seqs, seqs), bf16),
        gather=pltpu.VMEM((n_r - 1, seqs, half), bf16),
        spread=pltpu.VMEM((n_r - 1, half, seqs), bf16),
        f_x=pltpu.VMEM((rows, seqs), f32),
        f_y=pltpu.VMEM((rows, seqs), f32),
        grad=pltpu.VMEM((4, rows, half // 2), f32),
        work=pltpu.VMEM((rows, half // 2), f32),
        early=pltpu.VMEM((4, rows, half // 2), f32),
        lent=pltpu.VMEM((4, rows, rows), bf16),
        lent_t=pltpu.VMEM((2, 2, rows, rows), bf16),
        sum_out=pltpu.VMEM((6, 4, rows + 16, half // 2), i16),
        sum_in=pltpu.VMEM((6, 4, rows + 16, half // 2), i16),
        row_q=pltpu.VMEM((n_r, 4, part + 16, half // 2), i16),
        row_in=pltpu.VMEM((n_r, 4, part + 16, half // 2), i16),
        rows_f=pltpu.VMEM((n_r, 2, part, half), f32),
        share=pltpu.VMEM((n_r, 2, part, half), f32),
        back_q=pltpu.VMEM((n_r, part, seqs), i16),
        back_in=pltpu.VMEM((n_r, part, seqs), i16),
        sq_b=pltpu.VMEM((n_b, 8, 128), f32),
        sq_r=pltpu.VMEM((n_r, 8, 128), f32),
        load_sem=dma((3,)),
        out_sem=dma((2, n_r)),
        turn_send=dma((pairs,)),
        turn_recv=dma((pairs,)),
        ag_send=dma((3, n_r)),
        ag_recv=dma((n_b, n_r)),
        line_send=dma((n_b, n_r)),
        pass_send=dma((n_b, 4)),
        mx_send=dma((n_r,)),
        mx_recv=dma((2, n_r)),
        sum_send=dma((6, 4)),
        sum_recv=dma((6, 4)),
        lend_send=dma((8,)),
        lend_recv=dma((8,)),
        swap_send=dma((2,)),
        swap_recv=dma((2,)),
        raw_send=dma((4,)),
        raw_recv=dma((2, 4)),
        row_send=dma((n_r, 3)),
        row_recv=dma((n_r, 3)),
        back_send=dma((n_r,)),
        back_recv=dma((n_r,)),
        sqb_send=dma((n_b,)),
        sqb_recv=dma((n_b,)),
        sqr_send=dma((n_r,)),
        sqr_recv=dma((n_r,)),
    )
    names = ["x_hbm", "y_hbm", "pay_hbm", "col_ref", "coef_ref", "pred_ref", "x_out", "y_out"]
    names += list(scratch)
    found = pl.pallas_call(
        functools.partial(line_kernel, names, n_r, n_b),
        out_shape=[jax.ShapeDtypeStruct(x_start.shape, f32)] * 2,
        in_specs=[hbm, hbm, hbm, smem, vmem, vmem],
        out_specs=[hbm, hbm],
        scratch_shapes=list(scratch.values()),
        compiler_params=pltpu.CompilerParams(
            collective_id=0, has_side_effects=True, vmem_limit_bytes=60 * 1024 * 1024
        ),
    )(x_start, y_start, bucket_payoff, column_blocks, public_coef, predecessor_sequences)
    block = pl.BlockSpec((1, rows // 2, seqs), lambda i: (0, i, 0))
    return pl.pallas_call(
        place_kernel,
        grid=(2,),
        out_shape=[jax.ShapeDtypeStruct(x_start.shape, f32)] * 2,
        in_specs=[block, block],
        out_specs=[block, block],
    )(*found)


def plain_kernel(
    n_r,
    n_b,
    x_ref,
    y_ref,
    pay_ref,
    col_ref,
    coef_ref,
    pred_ref,
    xo_ref,
    yo_ref,
    xs,
    ys,
    mixer,
    gather,
    pay_t,
    blocks,
    mixed,
    grad,
    sib_out,
    sib_in,
    far_out,
    far_in,
    sq_b,
    sq_r,
    rows_in,
    score,
    norm,
    mass,
    back_in,
    far_q,
    far_s,
    far_q_in,
    far_s_in,
    row_q,
    row_s,
    row_q_in,
    row_s_in,
    back_q,
    back_s,
    back_q_in,
    back_s_in,
    ag_send,
    ag_recv,
    fw_send,
    line_send,
    sib_send,
    sib_recv,
    far_send,
    far_recv,
    sqb_send,
    sqb_recv,
    sqr_send,
    sqr_recv,
    row_send,
    row_recv,
    back_send,
    back_recv,
    far_s_send,
    far_s_recv,
    row_s_send,
    row_s_recv,
    back_s_send,
    back_s_recv,
):
    rows, seqs = xs.shape
    half = seqs // 2
    part = rows // n_r
    pairs = n_b // 2
    me_r = lax.axis_index("round")
    me_b = lax.axis_index("bucket")
    pair = me_b // 2
    core = me_b % 2
    sibling = pair * 2 + 1 - core
    total_count = n_r * n_b * rows * seqs

    def remote(src, dst, send, recv, **where):
        return pltpu.make_async_remote_copy(
            src_ref=src,
            dst_ref=dst,
            send_sem=send,
            recv_sem=recv,
            device_id=where,
            device_id_type=pl.DeviceIdType.MESH,
        )

    barrier = pltpu.get_barrier_semaphore()
    for d in range(1, n_b):
        pl.semaphore_signal(
            barrier,
            inc=1,
            device_id={"bucket": (me_b + d) % n_b},
            device_id_type=pl.DeviceIdType.MESH,
        )
    for d in range(1, n_r):
        pl.semaphore_signal(
            barrier,
            inc=1,
            device_id={"round": (me_r + d) % n_r},
            device_id_type=pl.DeviceIdType.MESH,
        )
    pl.semaphore_wait(barrier, n_b + n_r - 2)

    def order(i):
        return jnp.where(i < half, 2 * i, 2 * (i - half) + 1)

    down = lax.broadcasted_iota(jnp.int32, (seqs, seqs), 0)
    across = lax.broadcasted_iota(jnp.int32, (seqs, seqs), 1)
    to_inner = (down == order(across)).astype(jnp.float32)
    to_outer = (order(down) == across).astype(jnp.float32)

    tiles, per_row, tile, _ = coef_ref.shape[1:]
    for m in range(tiles):
        for c in range(tiles):
            value = jnp.zeros((tile, tile), jnp.float32)
            for t in range(per_row):
                value = value + jnp.where(col_ref[0, m, t] == c, coef_ref[0, m, t], 0.0)
            mixer[m * tile : (m + 1) * tile, c * tile : (c + 1) * tile] = value
    mixer[...] = exact(to_outer, exact(mixer[...], to_inner))
    ys[...] = exact(y_ref[0], to_inner)
    for r in range(n_r - 1):
        place = order(lax.broadcasted_iota(jnp.int32, (seqs, half), 0))
        gather[r] = (place == pred_ref[r : r + 1, :]).astype(jnp.float32)

    def columns(j):
        return pl.ds(pl.multiple_of(j * rows, rows), rows)

    def coded(value, code_ref, scale_ref):
        top = jnp.max(jnp.abs(value), axis=0, keepdims=True)
        unit = jnp.maximum(top, 1e-30) / 32767.0
        code = jnp.floor(value * (1.0 / unit) + 0.5)
        code_ref[...] = code.astype(jnp.int32).astype(jnp.int16)
        scale_ref[...] = jnp.broadcast_to(unit, scale_ref.shape)

    def decoded(code_ref, scale_ref):
        return code_ref[...].astype(jnp.int32).astype(jnp.float32) * scale_ref[0:1, :]

    def prox(state, sign, factor, weight, short):
        def row_copy(d):
            s = (me_r + d) % n_r
            here = grad.at[pl.ds(pl.multiple_of(s * part, part), part)]
            if not short:
                return [
                    remote(here, rows_in.at[me_r], row_send.at[s], row_recv.at[me_r], round=s)
                ]
            return [
                remote(
                    row_q.at[s], row_q_in.at[me_r], row_send.at[s], row_recv.at[me_r], round=s
                ),
                remote(
                    row_s.at[s], row_s_in.at[me_r], row_s_send.at[s], row_s_recv.at[me_r], round=s
                ),
            ]

        def row_arrival(d):
            s = (me_r + d) % n_r
            if not short:
                return [
                    remote(rows_in.at[s], rows_in.at[s], row_send.at[s], row_recv.at[s], round=s)
                ]
            return [
                remote(row_q_in.at[s], row_q_in.at[s], row_send.at[s], row_recv.at[s], round=s),
                remote(
                    row_s_in.at[s], row_s_in.at[s], row_s_send.at[s], row_s_recv.at[s], round=s
                ),
            ]

        for d in range(1, n_r):
            if short:
                s = (me_r + d) % n_r
                here = pl.ds(pl.multiple_of(s * part, part), part)
                coded(grad[here, :], row_q.at[s], row_s.at[s])
            for copy in row_copy(d):
                copy.start()
        squares = grad[...]
        squares = jnp.sum((squares * squares).reshape(rows // 8, 8, seqs), axis=0)
        squares = sum(squares[:, i * 128 : (i + 1) * 128] for i in range(seqs // 128))
        sq_b[me_b] = squares

        def sqb_copy(d):
            s = (me_b + d) % n_b
            return remote(
                sq_b.at[me_b], sq_b.at[me_b], sqb_send.at[d], sqb_recv.at[me_b], bucket=s
            )

        def sqb_arrival(d):
            s = (me_b + d) % n_b
            return remote(sq_b.at[s], sq_b.at[s], sqb_send.at[d], sqb_recv.at[s], bucket=s)

        for d in range(1, n_b):
            sqb_copy(d).start()
        rows_in[me_r] = grad[pl.ds(pl.multiple_of(me_r * part, part), part), :]
        for d in range(1, n_b):
            sqb_arrival(d).wait_recv()
        sq_r[me_r] = jnp.sum(sq_b[...], axis=0)

        def sqr_copy(d):
            s = (me_r + d) % n_r
            return remote(sq_r.at[me_r], sq_r.at[me_r], sqr_send.at[d], sqr_recv.at[me_r], round=s)

        def sqr_arrival(d):
            s = (me_r + d) % n_r
            return remote(sq_r.at[s], sq_r.at[s], sqr_send.at[d], sqr_recv.at[s], round=s)

        for d in range(1, n_r):
            sqr_copy(d).start()
        for d in range(1, n_r):
            sqr_arrival(d).wait_recv()
        squares = jnp.sum(jnp.sum(sq_r[...], axis=0), axis=0, keepdims=True)
        squares = jnp.sum(squares, axis=1, keepdims=True)
        scale = sign / (factor * jnp.sqrt(squares / total_count + epsilon))
        for d in range(1, n_r):
            for copy in row_arrival(d):
                copy.wait_recv()
            if short:
                s = (me_r + d) % n_r
                rows_in[s] = decoded(row_q_in.at[s], row_s_in.at[s])

        for r in reversed(range(n_r)):
            values = rows_in[r] * scale
            if r < n_r - 1:
                values = values + exact(norm[r + 1], gather[r], nt)
            score[r] = values
            even, odd = values[:, :half], values[:, half:]
            larger = jnp.maximum(even, odd)
            norm[r] = larger + jnp.log(jnp.exp(even - larger) + jnp.exp(odd - larger))

        def back_copy(r):
            if not short:
                return [
                    remote(
                        mass.at[r], back_in.at[me_r], back_send.at[r], back_recv.at[me_r], round=r
                    )
                ]
            return [
                remote(
                    back_q.at[r], back_q_in.at[me_r], back_send.at[r], back_recv.at[me_r], round=r
                ),
                remote(
                    back_s.at[r],
                    back_s_in.at[me_r],
                    back_s_send.at[r],
                    back_s_recv.at[me_r],
                    round=r,
                ),
            ]

        def back_arrival(s):
            if not short:
                return [
                    remote(
                        back_in.at[s], back_in.at[s], back_send.at[s], back_recv.at[s], round=s
                    )
                ]
            return [
                remote(
                    back_q_in.at[s], back_q_in.at[s], back_send.at[s], back_recv.at[s], round=s
                ),
                remote(
                    back_s_in.at[s], back_s_in.at[s], back_s_send.at[s], back_s_recv.at[s], round=s
                ),
            ]

        for r in range(n_r):
            even = jnp.exp(score[r, :, :half] - norm[r])
            odd = jnp.exp(score[r, :, half:] - norm[r])
            if r > 0:
                parent = exact(mass[r - 1], gather[r - 1])
                even = parent * even
                odd = parent * odd
            mass[r, :, :half] = even
            mass[r, :, half:] = odd

            @pl.when(me_r != r)
            def _():
                if short:
                    coded(mass[r], back_q.at[r], back_s.at[r])
                for copy in back_copy(r):
                    copy.start()

        def update(s, best):
            here = pl.ds(pl.multiple_of(s * part, part), part)
            state[here, :] = (1.0 - weight) * state[here, :] + weight * best

        update(me_r, mass[me_r])
        for d in range(1, n_r):
            s = (me_r + d) % n_r
            for copy in back_arrival(s):
                copy.wait_recv()
            if short:
                update(s, decoded(back_q_in.at[s], back_s_in.at[s]))
            else:
                update(s, back_in[s])
        for d in range(1, n_r):
            for copy in row_copy(d) + back_copy((me_r + d) % n_r):
                copy.wait_send()
            sqr_copy(d).wait_send()
        for d in range(1, n_b):
            sqb_copy(d).wait_send()

    def step(index, _):
        weight = 2.0 / (index.astype(jnp.float32) + 3.0)
        short = False

        blocks[me_b] = exact(ys[...], mixer[...], nt).astype(jnp.bfloat16)

        def own_copy(kind):
            target = (sibling, me_b + 2, me_b - 2)[kind]
            return remote(
                blocks.at[me_b], blocks.at[me_b], ag_send.at[kind], ag_recv.at[me_b], bucket=target
            )

        def go_on(b, d, step):
            return remote(
                blocks.at[b], blocks.at[b], line_send.at[d], ag_recv.at[b], bucket=me_b + step
            )

        def pass_on(b, d):
            return remote(blocks.at[b], blocks.at[b], fw_send.at[d], ag_recv.at[b], bucket=sibling)

        def arrival(b):
            return remote(
                blocks.at[b], blocks.at[b], ag_send.at[0], ag_recv.at[b], bucket=sibling
            )

        def product(b):
            return jnp.dot(
                pay_ref[0, :, columns(b)], blocks[b], preferred_element_type=jnp.float32
            )

        @pl.when(pair < pairs - 1)
        def _():
            own_copy(1).start()

        @pl.when(pair > 0)
        def _():
            own_copy(2).start()

        own_copy(0).start()
        @pl.when(index == 0)
        def _():
            xs[...] = exact(x_ref[0], to_inner)

            def turn(j, _):
                pay_t[columns(j), :] = pay_ref[0, :, columns(j)].T
                return 0

            lax.fori_loop(0, n_b, turn, 0)
        grad[...] = product(me_b)
        arrival(sibling).wait_recv()
        grad[...] += product(sibling)

        def take(d, _):
            left = me_b - 2 * d
            right = me_b + 2 * d

            @pl.when(pair >= d)
            def _():
                arrival(left).wait_recv()

                @pl.when(pair < pairs - 1)
                def _():
                    go_on(left, d, 2).start()

                pass_on(left, d).start()

            @pl.when(pair + d < pairs)
            def _():
                arrival(right).wait_recv()

                @pl.when(pair > 0)
                def _():
                    go_on(right, pairs + d, -2).start()

                pass_on(right, pairs + d).start()

            def use(b, other):
                grad[...] += product(b)
                arrival(other).wait_recv()
                grad[...] += product(other)

            @pl.when(pair >= d)
            def _():
                use(left, sibling - 2 * d)

            @pl.when(pair + d < pairs)
            def _():
                use(right, sibling + 2 * d)

            return 0

        lax.fori_loop(1, pairs, take, 0)

        def drain(d, _):
            left = me_b - 2 * d
            right = me_b + 2 * d

            @pl.when(pair >= d)
            def _():
                pass_on(left, d).wait_send()

                @pl.when(pair < pairs - 1)
                def _():
                    go_on(left, d, 2).wait_send()

            @pl.when(pair + d < pairs)
            def _():
                pass_on(right, pairs + d).wait_send()

                @pl.when(pair > 0)
                def _():
                    go_on(right, pairs + d, -2).wait_send()

            return 0

        lax.fori_loop(1, pairs, drain, 0)
        own_copy(0).wait_send()

        @pl.when(pair < pairs - 1)
        def _():
            own_copy(1).wait_send()

        @pl.when(pair > 0)
        def _():
            own_copy(2).wait_send()

        prox(xs, -1.0, smooth_x, weight, short)

        mixed[...] = exact(xs[...], mixer[...]).astype(jnp.bfloat16)

        def partial(b):
            return jnp.dot(pay_t[columns(b), :], mixed[...], preferred_element_type=jnp.float32)

        def sib_copy(q):
            return remote(
                sib_out.at[q], sib_in.at[q], sib_send.at[q], sib_recv.at[q], bucket=sibling
            )

        def far_copy(q, step, target):
            slot = q if step > 0 else pairs + q
            if not short:
                return [
                    remote(
                        far_out.at[q],
                        far_in.at[slot],
                        far_send.at[q],
                        far_recv.at[slot],
                        bucket=target,
                    )
                ]
            return [
                remote(
                    far_q.at[q],
                    far_q_in.at[slot],
                    far_send.at[q],
                    far_recv.at[slot],
                    bucket=target,
                ),
                remote(
                    far_s.at[q],
                    far_s_in.at[slot],
                    far_s_send.at[q],
                    far_s_recv.at[slot],
                    bucket=target,
                ),
            ]

        def far_value(q, step):
            slot = q if step > 0 else pairs + q
            for copy in far_copy(q, step, sibling):
                copy.wait_recv()
            if short:
                return decoded(far_q_in.at[slot], far_s_in.at[slot])
            return far_in[slot]

        def to_sibling(q):
            sib_out[q] = partial(q * 2 + 1 - core)
            sib_copy(q).start()

        def move(q, step):
            far_out[q] = partial(q * 2 + core)
            sib_copy(q).wait_recv()
            far_out[q] += sib_in[q]

            @pl.when(pair > 0 if step > 0 else pair < pairs - 1)
            def _():
                far_out[q] += far_value(q, step)

            if short:
                coded(far_out[q], far_q.at[q], far_s.at[q])
            for copy in far_copy(q, step, me_b + step):
                copy.start()

        def outward(right, left):
            def one(i, _):
                @pl.when(pair < pairs - 1 - i)
                def _():
                    right(pairs - 1 - i)

                @pl.when(pair > i)
                def _():
                    left(i)

                return 0

            lax.fori_loop(0, pairs - 1, one, 0)

        def far_done(q, step):
            for copy in far_copy(q, step, me_b + step):
                copy.wait_send()

        outward(to_sibling, to_sibling)
        outward(lambda q: move(q, 2), lambda q: move(q, -2))
        to_sibling(pair)
        grad[...] = partial(me_b)
        sib_copy(pair).wait_recv()
        grad[...] += sib_in[pair]

        @pl.when(pair > 0)
        def _():
            grad[...] += far_value(pair, 2)

        @pl.when(pair < pairs - 1)
        def _():
            grad[...] += far_value(pair, -2)

        outward(lambda q: far_done(q, 2), lambda q: far_done(q, -2))
        for q in range(pairs):
            sib_copy(q).wait_send()
        prox(ys, 1.0, smooth_y, weight, short)
        return 0

    lax.fori_loop(0, 2, step, 0)
    down = lax.broadcasted_iota(jnp.int32, (seqs, seqs), 0)
    across = lax.broadcasted_iota(jnp.int32, (seqs, seqs), 1)
    to_outer = (order(down) == across).astype(jnp.float32)
    xo_ref[0] = exact(xs[...], to_outer)
    yo_ref[0] = exact(ys[...], to_outer)


def plain_body(x_start, y_start, bucket_payoff, column_blocks, public_coef, predecessor_sequences):
    n_r = lax.axis_size("round")
    n_b = lax.axis_size("bucket")
    _, rows, seqs = x_start.shape
    part = rows // n_r
    pairs = n_b // 2
    f32, bf16 = jnp.float32, jnp.bfloat16
    vmem = pl.BlockSpec(memory_space=pltpu.VMEM)
    smem = pl.BlockSpec(memory_space=pltpu.SMEM)
    dma = pltpu.SemaphoreType.DMA
    return pl.pallas_call(
        functools.partial(plain_kernel, n_r, n_b),
        out_shape=[jax.ShapeDtypeStruct(x_start.shape, f32)] * 2,
        in_specs=[vmem, vmem, vmem, smem, vmem, vmem],
        out_specs=[vmem, vmem],
        scratch_shapes=[
            pltpu.VMEM((rows, seqs), f32),
            pltpu.VMEM((rows, seqs), f32),
            pltpu.VMEM((seqs, seqs), f32),
            pltpu.VMEM((n_r - 1, seqs, seqs // 2), f32),
            pltpu.VMEM((n_b * rows, rows), bf16),
            pltpu.VMEM((n_b, rows, seqs), bf16),
            pltpu.VMEM((rows, seqs), bf16),
            pltpu.VMEM((rows, seqs), f32),
            pltpu.VMEM((pairs, rows, seqs), f32),
            pltpu.VMEM((pairs, rows, seqs), f32),
            pltpu.VMEM((pairs, rows, seqs), f32),
            pltpu.VMEM((2 * pairs, rows, seqs), f32),
            pltpu.VMEM((n_b, 8, 128), f32),
            pltpu.VMEM((n_r, 8, 128), f32),
            pltpu.VMEM((n_r, part, seqs), f32),
            pltpu.VMEM((n_r, part, seqs), f32),
            pltpu.VMEM((n_r, part, seqs // 2), f32),
            pltpu.VMEM((n_r, part, seqs), f32),
            pltpu.VMEM((n_r, part, seqs), f32),
            pltpu.VMEM((16, 128), jnp.int16),
            pltpu.VMEM((pairs, 8, seqs), f32),
            pltpu.VMEM((16, 128), jnp.int16),
            pltpu.VMEM((2 * pairs, 8, seqs), f32),
            pltpu.VMEM((16, 128), jnp.int16),
            pltpu.VMEM((n_r, 8, seqs), f32),
            pltpu.VMEM((16, 128), jnp.int16),
            pltpu.VMEM((n_r, 8, seqs), f32),
            pltpu.VMEM((16, 128), jnp.int16),
            pltpu.VMEM((n_r, 8, seqs), f32),
            pltpu.VMEM((16, 128), jnp.int16),
            pltpu.VMEM((n_r, 8, seqs), f32),
            dma((3,)),
            dma((n_b,)),
            dma((2 * pairs,)),
            dma((2 * pairs,)),
            dma((pairs,)),
            dma((pairs,)),
            dma((pairs,)),
            dma((2 * pairs,)),
            dma((n_b,)),
            dma((n_b,)),
            dma((n_r,)),
            dma((n_r,)),
            dma((n_r,)),
            dma((n_r,)),
            dma((n_r,)),
            dma((n_r,)),
            dma((pairs,)),
            dma((2 * pairs,)),
            dma((n_r,)),
            dma((n_r,)),
            dma((n_r,)),
            dma((n_r,)),
        ],
        compiler_params=pltpu.CompilerParams(
            collective_id=0, has_side_effects=True, vmem_limit_bytes=60 * 1024 * 1024
        ),
    )(x_start, y_start, bucket_payoff, column_blocks, public_coef, predecessor_sequences)


def solution(mesh):
    in_specs = (
        P("round", "bucket", None),
        P("round", "bucket", None),
        P("round", "bucket", None),
        P("round", None, None),
        P("round", None, None, None, None),
        P(),
    )
    out_specs = (P("round", "bucket", None), P("round", "bucket", None))

    line = mesh.shape["round"] == 4 and mesh.shape["bucket"] == 8

    def run(*arrays):
        return tuple(
            jax.shard_map(
                line_body if line else plain_body, mesh=mesh, in_specs=in_specs, out_specs=out_specs, check_vma=False
            )(*arrays)
        )

    return run
```

```python
import functools
import types

import jax
import jax.numpy as jnp
from jax import lax
from jax.experimental import pallas as pl
from jax.experimental.pallas import tpu as pltpu
from jax.sharding import PartitionSpec as P

smooth_x = 0.1
smooth_y = 0.1
epsilon = 1e-06
highest = lax.Precision.HIGHEST
nn = (((1,), (0,)), ((), ()))
nt = (((1,), (1,)), ((), ()))


def exact(a, b, dims=nn):
    return lax.dot_general(a, b, dims, precision=highest, preferred_element_type=jnp.float32)


weights = (2.0 / 3.0, 2.0 / 4.0)
top_code = 65535.0
shift_code = 32768


def split3(value):
    hi = value.astype(jnp.bfloat16)
    left = value - hi.astype(jnp.float32)
    mid = left.astype(jnp.bfloat16)
    lo = (left - mid.astype(jnp.float32)).astype(jnp.bfloat16)
    return [hi, mid, lo]


def dot(a, b, dims=nn):
    return lax.dot_general(a, b, dims, preferred_element_type=jnp.float32)


def picked(parts, one_hot, dims=nn):
    size = parts[0].shape[0]
    out = dot(jnp.concatenate(parts, axis=0), one_hot, dims)
    return sum(out[i * size : (i + 1) * size] for i in range(len(parts)))


def mix(parts, factors, dims):
    size = parts[0].shape[0]
    total = None
    for i, factor in reversed(list(enumerate(factors))):
        count = min(len(parts), 3 - i)
        out = dot(jnp.concatenate(parts[:count], axis=0), factor, dims)
        for j in reversed(range(count)):
            term = out[j * size : (j + 1) * size]
            total = term if total is None else total + term
    return total


def encode(value, code_ref):
    if len(code_ref.shape) == 3:
        wide = code_ref.shape[2]
        for i in range(code_ref.shape[0]):
            encode(value[:, i * wide : (i + 1) * wide], code_ref.at[i])
        return
    rows = value.shape[0]
    top = jnp.maximum(jnp.max(jnp.abs(value), axis=0, keepdims=True), 1e-30)
    power = jnp.floor(256.0 * jnp.log2(top * (1.0 / 32767.0))) + 1.0
    code = jnp.floor(value * jnp.exp2(power * (-1.0 / 256.0)) + 0.5)
    code_ref[:rows, :] = code.astype(jnp.int32).astype(jnp.int16)
    power = jnp.broadcast_to(power, (16, value.shape[1]))
    code_ref[rows:, :] = power.astype(jnp.int32).astype(jnp.int16)


def decode(code_ref):
    if len(code_ref.shape) == 3:
        return jnp.concatenate([decode(code_ref.at[i]) for i in range(code_ref.shape[0])], axis=1)
    rows = code_ref.shape[0] - 16
    power = code_ref[rows:, :].astype(jnp.int32).astype(jnp.float32)[0:1, :]
    unit = jnp.exp2(power * (1.0 / 256.0))
    return code_ref[:rows, :].astype(jnp.int32).astype(jnp.float32) * unit


def line_kernel(names, n_r, n_b, *refs):
    k = types.SimpleNamespace(**dict(zip(names, refs)))
    f32, bf16 = jnp.float32, jnp.bfloat16
    _, rows, seqs = k.x_hbm.shape
    half = seqs // 2
    wide = half // 2
    part = rows // n_r
    pairs = n_b // 2
    me_r = lax.axis_index("round")
    me_b = lax.axis_index("bucket")
    pair = me_b // 2
    core = me_b % 2
    sibling = pair * 2 + 1 - core
    spans = ((0, slice(0, half)), (1, slice(0, wide)), (1, slice(wide, half)))
    quarters = (slice(0, 2), slice(2, 3), slice(3, 4))
    members = ((0, 1), (2,), (3,))
    outward = jnp.where(pair < pairs // 2, -2, 2)
    end_chip = jnp.where(pair < pairs // 2, 0, pairs - 1)
    facing = pair - outward // 2
    far_end = pairs - 1 - end_chip
    inner = (pair > 0) & (pair < pairs - 1)
    total_count = n_r * n_b * rows * seqs

    def remote(src, dst, send, recv, **where):
        return pltpu.make_async_remote_copy(
            src_ref=src,
            dst_ref=dst,
            send_sem=send,
            recv_sem=recv,
            device_id=where,
            device_id_type=pl.DeviceIdType.MESH,
        )

    load_y = pltpu.make_async_copy(k.y_hbm, k.yv, k.load_sem.at[0])
    load_pay = pltpu.make_async_copy(k.pay_hbm, k.pay, k.load_sem.at[1])
    load_x = pltpu.make_async_copy(k.x_hbm, k.xv, k.load_sem.at[2])
    load_y.start()
    load_pay.start()
    load_x.start()

    barrier = pltpu.get_barrier_semaphore()
    for dr in range(n_r):
        for db in range(n_b):
            if dr or db:
                pl.semaphore_signal(
                    barrier,
                    inc=1,
                    device_id={"round": (me_r + dr) % n_r, "bucket": (me_b + db) % n_b},
                    device_id_type=pl.DeviceIdType.MESH,
                )

    def order(i):
        return 2 * (i // half * wide + i % wide) + (i % half) // wide

    down = lax.broadcasted_iota(jnp.int32, (seqs, seqs), 0)
    across = lax.broadcasted_iota(jnp.int32, (seqs, seqs), 1)
    k.to_outer[...] = (order(down) == across).astype(f32).astype(bf16)

    tiles, per_row, tile, _ = k.coef_ref.shape[1:]
    for m in range(tiles):
        for c in range(tiles):
            value = jnp.zeros((tile, tile), f32)
            for t in range(per_row):
                value = value + jnp.where(k.col_ref[0, m, t] == c, k.coef_ref[0, m, t], 0.0)
            k.mixer[m * tile : (m + 1) * tile, c * tile : (c + 1) * tile] = value
    for i, piece in enumerate(split3(k.mixer[...])):
        k.mix_p[i] = dot(k.to_outer[...], piece).astype(bf16)

    def rows_of(s):
        return pl.ds(pl.multiple_of(s * part, part), part)

    def columns(j):
        return pl.ds(pl.multiple_of(j * rows, rows), rows)

    away = jnp.where(pair < pairs // 2, pairs // 2, 0)

    def lent_place(o):
        return (far_end - away, 1 - (far_end - away))[o]

    def lend(turn):
        o, i, p = turn // 4, turn // 2 % 2, turn % 2
        here = pl.ds(p * (rows // 2), rows // 2)
        b = 2 * lent_place(o) + i
        return remote(
            k.pay.at[0, here, columns(2 * away + b)],
            k.lent.at[b, here],
            k.lend_send.at[turn],
            k.lend_recv.at[turn],
            bucket=me_b - outward,
        )

    def lend_start(turns):
        @pl.when(jnp.logical_not(inner))
        def _():
            for turn in turns:
                lend(turn).start()

    def lent_swap(j, o):
        return remote(
            k.pay_out.at[j],
            k.lent_t.at[j, core],
            k.swap_send.at[o],
            k.swap_recv.at[o],
            bucket=sibling,
        )

    def take_lent(o):
        j = lent_place(o)
        for i in range(2):
            for p in range(2):
                here = k.lent.at[2 * j + i, pl.ds(p * (rows // 2), rows // 2)]
                turn = 4 * o + 2 * i + p
                remote(
                    here, here, k.lend_send.at[turn], k.lend_recv.at[turn], bucket=sibling
                ).wait_recv()
        k.pay_out[j] = k.lent[2 * j + 1 - core].T
        lent_swap(j, o).start()
        k.lent_t[j, core] = k.lent[2 * j + core].T
        lent_swap(j, o).wait()


    def own_copy(kind, s):
        target = (sibling, me_b + 2, me_b - 2)[kind]
        here = k.blocks.at[me_b, :, rows_of(s), :]
        return remote(here, here, k.ag_send.at[kind, s], k.ag_recv.at[me_b, s], bucket=target)

    def own_start(s):
        @pl.when(pair < pairs - 1)
        def _():
            own_copy(1, s).start()

        @pl.when(pair > 0)
        def _():
            own_copy(2, s).start()

        own_copy(0, s).start()

    def own_drain(s):
        @pl.when(pair < pairs - 1)
        def _():
            own_copy(1, s).wait_send()

        @pl.when(pair > 0)
        def _():
            own_copy(2, s).wait_send()

        own_copy(0, s).wait_send()

    def set_own(s, value):
        value = value.astype(bf16)
        for c in range(4):
            k.blocks[me_b, c, rows_of(s), :] = value[:, c * wide : (c + 1) * wide]

    pl.semaphore_wait(barrier, n_b * n_r - 1)
    load_y.wait()
    load_pay.wait()
    lend_start(range(1))
    for s in range(n_r):
        value = mix(split3(k.yv[0, rows_of(s), :]), [k.mix_p[i] for i in range(3)], nt)
        k.f_y[rows_of(s), :] = value
        set_own(s, value)
        own_start(s)

    def part_of(b, s):
        return k.blocks.at[b, :, rows_of(s), :]

    def unit_of(b, c):
        return k.blocks.at[b, c]

    def block(b, u):
        return jnp.concatenate([k.blocks[b, c] for c in members[u]], axis=1)

    def by_parts(b):
        for s in range(n_r):
            arrived(part_of(b, s), b, s)

    def by_whole(b):
        arrived(k.blocks.at[b], b, 0)

    def by_unit(b, c):
        arrived(unit_of(b, c), b, c)

    def arrived(here, b, i):
        remote(here, here, k.ag_send.at[0, 0], k.ag_recv.at[b, i], bucket=sibling).wait_recv()

    def go_on(here, b, i, step):
        return remote(here, here, k.line_send.at[b, i], k.ag_recv.at[b, i], bucket=me_b + step)

    def pass_on(here, b, i):
        return remote(here, here, k.pass_send.at[b, i], k.ag_recv.at[b, i], bucket=sibling)

    def add_product(b, u):
        value = dot(k.pay[0, :, columns(b)], block(b, u))
        for i, c in enumerate(members[u]):
            k.grad[c] += value[:, i * wide : (i + 1) * wide]

    def lent_product(b, c):
        return dot(k.lent[b - 2 * away], k.blocks[b, c])

    def setup():
        lend_start(range(1, 5))


        def turn(q, _):
            k.pay_out[q] = k.pay[0, :, columns(q * 2 + 1 - core)].T
            turned(q).start()
            k.pay_t[q, core] = k.pay[0, :, columns(q * 2 + core)].T
            return 0

        lax.fori_loop(0, pairs, turn, 0)
        for r in range(n_r - 1):
            place = order(lax.broadcasted_iota(jnp.int32, (seqs, half), 0))
            one_hot = (place == k.pred_ref[r : r + 1, :]).astype(f32).astype(bf16)
            k.gather[r] = one_hot
            k.spread[r] = one_hot.T

        @pl.when(me_r == 0)
        def _():
            for s in range(n_r):
                k.back_in[s, 1] = jnp.full((part, half), 65535 - shift_code, jnp.int32).astype(
                    jnp.int16
                )

        load_x.wait()
        value = picked(split3(exact(k.xv[0], k.mixer[...])), k.to_outer[...], nt)
        k.f_x[...] = value
        for i in range(3):
            k.mix_p[i] = dot(k.mix_p[i], k.to_outer[...], nt).astype(bf16)

    def turned(q):
        return remote(
            k.pay_out.at[q],
            k.pay_t.at[q, core],
            k.turn_send.at[q],
            k.turn_recv.at[q],
            bucket=sibling,
        )


    def row_copy(d, u):
        s = (me_r + d) % n_r
        return remote(
            k.row_q.at[s, quarters[u]],
            k.row_in.at[me_r, quarters[u]],
            k.row_send.at[s, u],
            k.row_recv.at[me_r, u],
            round=s,
        )

    def row_arrival(d, u):
        s = (me_r + d) % n_r
        h, lanes = spans[u]
        here = k.row_in.at[s, quarters[u]]
        remote(here, here, k.row_send.at[s, u], k.row_recv.at[s, u], round=s).wait_recv()
        k.rows_f[s, h, :, lanes] = decode(here)

    def finish(u):
        for d in range(1, n_r):
            s = (me_r + d) % n_r
            for c in members[u]:
                encode(k.grad[c, rows_of(s), :], k.row_q.at[s, c])
            row_copy(d, u).start()
        for c in members[u]:
            squares = k.grad[c]
            squares = jnp.sum((squares * squares).reshape(rows // 8, 8, wide), axis=0)
            if c == 0:
                k.sq_mine[...] = squares
            else:
                k.sq_mine[...] += squares
            h, lanes = c // 2, slice(c % 2 * wide, c % 2 * wide + wide)
            k.rows_f[me_r, h, :, lanes] = k.grad[c, rows_of(me_r), :]

    me = me_r * n_b + me_b

    def square_copy(dr, db):
        here = k.sq_all.at[me]
        return remote(
            here,
            here,
            k.sq_send.at[dr * n_b + db],
            k.sq_recv.at[me],
            round=(me_r + dr) % n_r,
            bucket=(me_b + db) % n_b,
        )

    def square_arrival(dr, db):
        s = (me_r + dr) % n_r * n_b + (me_b + db) % n_b
        here = k.sq_all.at[s]
        return remote(here, here, k.sq_send.at[0], k.sq_recv.at[s], bucket=sibling)

    others = [(dr, db) for dr in range(n_r) for db in range(n_b) if dr or db]

    def back_copy(r, i):
        return remote(
            k.back_q.at[r, i],
            k.back_in.at[me_r, i],
            k.back_send.at[r, i],
            k.back_recv.at[me_r, i],
            round=r,
        )

    def back_arrival(s):
        for i in range(2):

            def wait():
                here = k.back_in.at[s, i]
                remote(
                    here, here, k.back_send.at[s, i], k.back_recv.at[s, i], round=s
                ).wait_recv()

            if i == 0:
                wait()
            else:
                pl.when(me_r > 0)(wait)

    def back_drain(s):
        back_copy(s, 0).wait_send()

        @pl.when(s > 0)
        def _():
            back_copy(s, 1).wait_send()

    def give_back(r, i, value):
        code = jnp.floor(value * top_code + 0.5).astype(jnp.int32) - shift_code
        k.back_q[r, i] = code.astype(jnp.int16)

        @pl.when(me_r != r)
        def _():
            back_copy(r, i).start()

        @pl.when(me_r == r)
        def _():
            k.back_in[me_r, i] = k.back_q[r, i]

    def prox(sign, factor, after_scale=None):
        k.sq_all[me] = jnp.sum(k.sq_mine[...], axis=0, keepdims=True)
        for dr, db in others:
            square_copy(dr, db).start()
        for u in range(2):
            for d in range(1, n_r):
                row_arrival(d, u)
        for d in range(1, n_r):
            row_arrival(d, 2)
        for dr, db in others:
            square_arrival(dr, db).wait_recv()
        squares = jnp.sum(k.sq_all[...], axis=0)
        squares = jnp.sum(squares, axis=1, keepdims=True)
        scale = sign / (factor * jnp.sqrt(squares / total_count + epsilon))

        if after_scale is not None:
            after_scale()
        carried = None
        for r in reversed(range(n_r)):
            norms = []
            evens = []
            for h in range(2):
                values = k.rows_f[r, h] * scale
                if carried is not None:
                    values = values + carried[:, h * half : (h + 1) * half]
                even, odd = values[:, :wide], values[:, wide:]
                small = jnp.exp(-jnp.abs(even - odd))
                larger = 1.0 / (1.0 + small)
                smaller = small * larger
                ahead = even >= odd
                evens.append(jnp.where(ahead, larger, smaller))
                k.share[r, h, :, :wide] = evens[h]
                k.share[r, h, :, wide:] = jnp.where(ahead, smaller, larger)
                norms.append(jnp.maximum(even, odd) + jnp.log(1.0 + small))
            give_back(r, 0, jnp.concatenate(evens, axis=1))
            if r > 0:
                norm = jnp.concatenate(norms, axis=1)
                carried = picked(split3(norm), k.spread[r - 1])

        mass = jnp.concatenate([k.share[0, 0], k.share[0, 1]], axis=1)
        for r in range(1, n_r):
            parent = picked(split3(mass), k.gather[r - 1])
            give_back(r, 1, parent)
            above = [parent[:, h * wide : (h + 1) * wide] for h in (0, 0, 1, 1)]
            shares = jnp.concatenate([k.share[r, 0], k.share[r, 1]], axis=1)
            mass = shares * jnp.concatenate(above, axis=1)

    def prox_drain():
        for d in range(1, n_r):
            for u in range(3):
                row_copy(d, u).wait_send()
            back_drain((me_r + d) % n_r)
        for dr, db in others:
            square_copy(dr, db).wait_send()

    def pieces(s):
        share, parent = [
            (k.back_in[s, i].astype(jnp.int32) + shift_code).astype(f32) * (1.0 / top_code)
            for i in range(2)
        ]
        even = parent * share
        odd = parent - even
        both = (even[:, :wide], odd[:, :wide], even[:, wide:], odd[:, wide:])
        whole = jnp.concatenate(both, axis=1)
        return split3(whole)[:2]

    def mixed_part(s, state, weight, dims):
        value = mix(pieces(s), [k.mix_p[i] for i in range(3)], dims)
        value = (1.0 - weight) * state[rows_of(s), :] + weight * value
        state[rows_of(s), :] = value
        return value

    def add_best(out, s, share):
        best = picked(pieces(s), k.to_outer[...])
        out[0, rows_of(s), :] += share * best


    def mixed_copy(s):
        here = k.mixed.at[core, :, rows_of(s), :]
        return remote(here, here, k.mx_send.at[s], k.mx_recv.at[core, s], bucket=sibling)

    def mixed_arrival(s):
        here = k.mixed.at[1 - core, :, rows_of(s), :]
        return remote(here, here, k.mx_send.at[s], k.mx_recv.at[1 - core, s], bucket=sibling)

    def raw_copy(n):
        return remote(
            k.mixed.at[core, n],
            k.mixed.at[2 + core, n],
            k.raw_send.at[n],
            k.raw_recv.at[core, n],
            bucket=me_b - outward,
        )

    def raw_pass(n):
        here = k.mixed.at[2 + core, n]
        return remote(here, here, k.raw_send.at[n], k.raw_recv.at[core, n], bucket=sibling)

    def raw_arrival(source, n):
        here = k.mixed.at[2 + source, n]
        remote(
            here, here, k.raw_send.at[n], k.raw_recv.at[source, n], bucket=sibling
        ).wait_recv()

    def partial(q, n):
        return dot(k.pay_t[q, 0], k.mixed[0, n]) + dot(k.pay_t[q, 1], k.mixed[1, n])

    def lent_partial(j, n):
        return dot(k.lent_t[j, 0], k.mixed[2, n]) + dot(k.lent_t[j, 1], k.mixed[3, n])

    def sum_copy(kind, n, step):
        return remote(
            k.sum_out.at[kind, n],
            k.sum_in.at[kind, n],
            k.sum_send.at[kind, n],
            k.sum_recv.at[kind, n],
            bucket=me_b + step,
        )

    def sum_arrival(kind, n):
        here = k.sum_in.at[kind, n]
        remote(
            here, here, k.sum_send.at[kind, n], k.sum_recv.at[kind, n], bucket=sibling
        ).wait_recv()
        return decode(here)

    def sums_of_end(index):
        for n in range(4):
            raw_copy(n).start()

        def lend_sum(n, _):
            k.work[...] = partial(facing - outward // 2, n)
            encode(k.work[...], k.sum_out.at[4, n])
            sum_copy(4, n, -outward).start()
            return 0

        @pl.when(index == 0)
        def _():
            lax.fori_loop(0, 4, lend_sum, 0)

        def give(n, _):
            k.work[...] = partial(facing, n)
            encode(k.work[...], k.sum_out.at[3, n])
            sum_copy(3, n, -outward).start()
            return 0

        lax.fori_loop(0, 4, give, 0)

    def sums_of_inner(index):
        def give(i, _):
            n = i % 4

            @pl.when(i < 4)
            def _():
                raw_arrival(core, n)
                raw_pass(n).start()

            q = jnp.where(i < 4, far_end, facing)
            k.work[...] = partial(q, n)

            @pl.when(i < 4)
            def _():
                raw_arrival(1 - core, n)

            @pl.when((i < 4) | (index == 1))
            def _():
                k.work[...] += lent_partial(q - away, n)

            @pl.when((i >= 4) & (index == 0))
            def _():
                k.work[...] += sum_arrival(4, n)

            encode(k.work[...], k.sum_out.at[i // 4, n])
            sum_copy(i // 4, n, -outward).start()

            @pl.when((i >= 2) & (i < 6))
            def _():
                k.work[...] = partial(end_chip, i - 2)
                k.work[...] += sum_arrival(0, i - 2)
                encode(k.work[...], k.sum_out.at[2, i - 2])
                sum_copy(2, i - 2, outward).start()

            return 0

        lax.fori_loop(0, 8, give, 0)

    def sums_drain(index):
        @pl.when(inner)
        def _():
            for n in range(4):
                raw_pass(n).wait_send()
                sum_copy(0, n, -outward).wait_send()
                sum_copy(1, n, -outward).wait_send()
                sum_copy(2, n, outward).wait_send()

        @pl.when(jnp.logical_not(inner))
        def _():
            for n in range(4):
                raw_copy(n).wait_send()
                sum_copy(3, n, -outward).wait_send()

                @pl.when(index == 0)
                def _():
                    sum_copy(4, n, -outward).wait_send()

    def out_copy(i, s):
        here, there = ((k.xo_ref, k.x_out), (k.yo_ref, k.y_out))[i]
        return pltpu.make_async_copy(
            here.at[:, rows_of(s)], there.at[:, rows_of(s)], k.out_sem.at[i, s]
        )

    def step(index, _):
        weight = 2.0 / (index.astype(f32) + 3.0)

        @pl.when(index == 0)
        def _():
            setup()

        first = -outward
        second = jnp.where(inner, outward, -2 * outward)
        far = jnp.where(inner, -2 * outward, -3 * outward)

        for u in range(3):
            value = dot(k.pay[0, :, columns(me_b)], block(me_b, u))
            for i, c in enumerate(members[u]):
                k.grad[c] = value[:, i * wide : (i + 1) * wide]
        by_parts(sibling)
        for u in range(2 + 1):
            add_product(sibling, u)

        @pl.when(index == 0)
        def _():
            for q in range(pairs):
                turned(q).wait()
            k.xo_ref[...] = (1.0 - weights[0]) * (1.0 - weights[1]) * k.xv[...]
            k.yo_ref[...] = (1.0 - weights[0]) * (1.0 - weights[1]) * k.yv[...]

        @pl.when(index == 1)
        def _():
            for s in range(n_r):
                add_best(k.yo_ref, s, weights[0] * (1.0 - weights[1]))

        def both(offset):
            for u in range(3):
                add_product(me_b + offset, u)
            by_whole(sibling + offset)
            for u in range(3):
                add_product(sibling + offset, u)

        plain = index == 0
        b = me_b + first
        for s in range(n_r):
            arrived(part_of(b, s), b, s)

            @pl.when(inner & plain)
            def _():
                go_on(part_of(b, s), b, s, outward).start()

        pass_on(k.blocks.at[b], b, 0).start()
        b2 = me_b + second

        @pl.when(inner)
        def _():
            by_parts(b2)
            for c in range(4):
                go_on(unit_of(b2, c), b2, c, -outward).start()
            pass_on(k.blocks.at[b2], b2, 0).start()

        both(first)

        @pl.when(jnp.logical_not(inner) & plain)
        def _():
            by_parts(b2)
            pass_on(k.blocks.at[b2], b2, 0).start()

        @pl.when(inner | plain)
        def _():
            both(second)

        @pl.when(inner & jnp.logical_not(plain))
        def _():
            take_lent(1)
            for c in range(4):
                k.early[c] = lent_product(b, c) + lent_product(sibling + first, c)

        b3 = me_b + far
        for c in range(4):

            @pl.when(inner | plain)
            def _():
                by_unit(b3, c)

                @pl.when(inner & plain)
                def _():
                    go_on(unit_of(b3, c), b3, c, outward).start()

                pass_on(unit_of(b3, c), b3, c).start()

                @pl.when(plain)
                def _():
                    k.grad[c] += dot(k.pay[0, :, columns(b3)], k.blocks[b3, c])

                by_unit(sibling + far, c)

                @pl.when(jnp.logical_not(plain))
                def _():
                    k.early[c] += lent_product(b3, c) + lent_product(sibling + far, c)
                    encode(k.early[c], k.sum_out.at[5, c])
                    sum_copy(5, c, outward).start()
                    k.grad[c] += dot(k.pay[0, :, columns(b3)], k.blocks[b3, c])

                k.grad[c] += dot(k.pay[0, :, columns(sibling + far)], k.blocks[sibling + far, c])

            @pl.when(jnp.logical_not(inner | plain))
            def _():
                k.grad[c] += sum_arrival(5, c)

            if c > 0:
                finish(c - 1)

        @pl.when(inner & plain)
        def _():
            for c in range(4):
                go_on(part_of(b, c), b, c, outward).wait_send()
                go_on(unit_of(b3, c), b3, c, outward).wait_send()

        @pl.when(inner)
        def _():
            for c in range(4):
                go_on(unit_of(b2, c), b2, c, -outward).wait_send()

        pass_on(k.blocks.at[b], b, 0).wait_send()

        @pl.when(inner | plain)
        def _():
            pass_on(k.blocks.at[b2], b2, 0).wait_send()
            for c in range(4):
                pass_on(unit_of(b3, c), b3, c).wait_send()

        @pl.when(inner & jnp.logical_not(plain))
        def _():
            for c in range(4):
                sum_copy(5, c, outward).wait_send()

        @pl.when(jnp.logical_not(inner | plain))
        def _():
            for turn in range(8):
                lend(turn).wait_send()

        for s in range(n_r):
            own_drain(s)

        def lend_more(turns):
            @pl.when(index == 0)
            def _():
                lend_start(turns)

        prox(-1.0, smooth_x, functools.partial(lend_more, range(5, 7)))
        for d in range(n_r):
            s = (me_r + d) % n_r
            if d > 0:
                back_arrival(s)
            value = mixed_part(s, k.f_x, weight, nn).astype(bf16)
            for c in range(4):
                k.mixed[core, c, rows_of(s), :] = value[:, c * wide : (c + 1) * wide]
            mixed_copy(s).start()
        for d in range(n_r):
            mixed_arrival((me_r + d) % n_r).wait_recv()

        @pl.when(inner)
        def _():
            @pl.when(index == 0)
            def _():
                take_lent(0)

            sums_of_inner(index)

        @pl.when(jnp.logical_not(inner))
        def _():
            sums_of_end(index)

        prox_drain()
        for s in range(n_r):
            mixed_copy(s).wait_send()
        share = jnp.where(index == 0, weights[0] * (1.0 - weights[1]), weights[1])
        for s in range(n_r):
            add_best(k.xo_ref, s, share)

            @pl.when(index == 1)
            def _():
                out_copy(0, s).start()

        for n in range(4):
            k.grad[n] = partial(pair, n)
        for u in range(3):
            for n in members[u]:

                @pl.when(inner)
                def _():
                    k.grad[n] += sum_arrival(3, n)
                    k.grad[n] += sum_arrival(1, n)

                @pl.when(jnp.logical_not(inner))
                def _():
                    k.grad[n] += sum_arrival(2, n)

            finish(u)
        sums_drain(index)

        prox(1.0, smooth_y, functools.partial(lend_more, range(7, 8)))
        for d in range(n_r):
            s = (me_r + d) % n_r
            if d > 0:
                back_arrival(s)

            @pl.when(index == 0)
            def _():
                set_own(s, mixed_part(s, k.f_y, weight, nt))
                own_start(s)

            @pl.when(index == 1)
            def _():
                add_best(k.yo_ref, s, weights[1])
                out_copy(1, s).start()

        prox_drain()
        return 0

    lax.fori_loop(0, 2, step, 0)
    for i in range(2):
        for s in range(n_r):
            out_copy(i, s).wait()


def place_kernel(x_in, y_in, x_out, y_out):
    x_out[...] = x_in[...]
    y_out[...] = y_in[...]


def line_body(x_start, y_start, bucket_payoff, column_blocks, public_coef, predecessor_sequences):
    n_r = lax.axis_size("round")
    n_b = lax.axis_size("bucket")
    _, rows, seqs = x_start.shape
    half = seqs // 2
    part = rows // n_r
    pairs = n_b // 2
    f32, bf16, i16 = jnp.float32, jnp.bfloat16, jnp.int16
    vmem = pl.BlockSpec(memory_space=pltpu.VMEM)
    smem = pl.BlockSpec(memory_space=pltpu.SMEM)
    hbm = pl.BlockSpec(memory_space=pl.ANY)
    dma = pltpu.SemaphoreType.DMA
    scratch = dict(
        xv=pltpu.VMEM((1, rows, seqs), f32),
        yv=pltpu.VMEM((1, rows, seqs), f32),
        xo_ref=pltpu.VMEM((1, rows, seqs), f32),
        yo_ref=pltpu.VMEM((1, rows, seqs), f32),
        pay=pltpu.VMEM((1, rows, n_b * rows), bf16),
        pay_t=pltpu.VMEM((pairs, 2, rows, rows), bf16),
        pay_out=pltpu.VMEM((pairs, rows, rows), bf16),
        blocks=pltpu.VMEM((n_b, 4, rows, half // 2), bf16),
        mixed=pltpu.VMEM((4, 4, rows, half // 2), bf16),
        mixer=pltpu.VMEM((seqs, seqs), f32),
        mix_p=pltpu.VMEM((3, seqs, seqs), bf16),
        to_outer=pltpu.VMEM((seqs, seqs), bf16),
        gather=pltpu.VMEM((n_r - 1, seqs, half), bf16),
        spread=pltpu.VMEM((n_r - 1, half, seqs), bf16),
        f_x=pltpu.VMEM((rows, seqs), f32),
        f_y=pltpu.VMEM((rows, seqs), f32),
        grad=pltpu.VMEM((4, rows, half // 2), f32),
        work=pltpu.VMEM((rows, half // 2), f32),
        early=pltpu.VMEM((4, rows, half // 2), f32),
        lent=pltpu.VMEM((4, rows, rows), bf16),
        lent_t=pltpu.VMEM((2, 2, rows, rows), bf16),
        sum_out=pltpu.VMEM((6, 4, rows + 16, half // 2), i16),
        sum_in=pltpu.VMEM((6, 4, rows + 16, half // 2), i16),
        row_q=pltpu.VMEM((n_r, 4, part + 16, half // 2), i16),
        row_in=pltpu.VMEM((n_r, 4, part + 16, half // 2), i16),
        rows_f=pltpu.VMEM((n_r, 2, part, half), f32),
        share=pltpu.VMEM((n_r, 2, part, half), f32),
        back_q=pltpu.VMEM((n_r, 2, part, half), i16),
        back_in=pltpu.VMEM((n_r, 2, part, half), i16),
        sq_mine=pltpu.VMEM((8, 128), f32),
        sq_all=pltpu.VMEM((n_r * n_b, 1, 128), f32),
        load_sem=dma((3,)),
        out_sem=dma((2, n_r)),
        turn_send=dma((pairs,)),
        turn_recv=dma((pairs,)),
        ag_send=dma((3, n_r)),
        ag_recv=dma((n_b, n_r)),
        line_send=dma((n_b, n_r)),
        pass_send=dma((n_b, 4)),
        mx_send=dma((n_r,)),
        mx_recv=dma((2, n_r)),
        sum_send=dma((6, 4)),
        sum_recv=dma((6, 4)),
        lend_send=dma((8,)),
        lend_recv=dma((8,)),
        swap_send=dma((2,)),
        swap_recv=dma((2,)),
        raw_send=dma((4,)),
        raw_recv=dma((2, 4)),
        row_send=dma((n_r, 3)),
        row_recv=dma((n_r, 3)),
        back_send=dma((n_r, 2)),
        back_recv=dma((n_r, 2)),
        sq_send=dma((n_r * n_b,)),
        sq_recv=dma((n_r * n_b,)),
    )
    names = ["x_hbm", "y_hbm", "pay_hbm", "col_ref", "coef_ref", "pred_ref", "x_out", "y_out"]
    names += list(scratch)
    found = pl.pallas_call(
        functools.partial(line_kernel, names, n_r, n_b),
        out_shape=[jax.ShapeDtypeStruct(x_start.shape, f32)] * 2,
        in_specs=[hbm, hbm, hbm, smem, vmem, vmem],
        out_specs=[hbm, hbm],
        scratch_shapes=list(scratch.values()),
        compiler_params=pltpu.CompilerParams(
            collective_id=0, has_side_effects=True, vmem_limit_bytes=60 * 1024 * 1024
        ),
    )(x_start, y_start, bucket_payoff, column_blocks, public_coef, predecessor_sequences)
    block = pl.BlockSpec((1, rows // 2, seqs), lambda i: (0, i, 0))
    return pl.pallas_call(
        place_kernel,
        grid=(2,),
        out_shape=[jax.ShapeDtypeStruct(x_start.shape, f32)] * 2,
        in_specs=[block, block],
        out_specs=[block, block],
    )(*found)


def plain_kernel(
    n_r,
    n_b,
    x_ref,
    y_ref,
    pay_ref,
    col_ref,
    coef_ref,
    pred_ref,
    xo_ref,
    yo_ref,
    xs,
    ys,
    mixer,
    gather,
    pay_t,
    blocks,
    mixed,
    grad,
    sib_out,
    sib_in,
    far_out,
    far_in,
    sq_b,
    sq_r,
    rows_in,
    score,
    norm,
    mass,
    back_in,
    far_q,
    far_s,
    far_q_in,
    far_s_in,
    row_q,
    row_s,
    row_q_in,
    row_s_in,
    back_q,
    back_s,
    back_q_in,
    back_s_in,
    ag_send,
    ag_recv,
    fw_send,
    line_send,
    sib_send,
    sib_recv,
    far_send,
    far_recv,
    sqb_send,
    sqb_recv,
    sqr_send,
    sqr_recv,
    row_send,
    row_recv,
    back_send,
    back_recv,
    far_s_send,
    far_s_recv,
    row_s_send,
    row_s_recv,
    back_s_send,
    back_s_recv,
):
    rows, seqs = xs.shape
    half = seqs // 2
    part = rows // n_r
    pairs = n_b // 2
    me_r = lax.axis_index("round")
    me_b = lax.axis_index("bucket")
    pair = me_b // 2
    core = me_b % 2
    sibling = pair * 2 + 1 - core
    total_count = n_r * n_b * rows * seqs

    def remote(src, dst, send, recv, **where):
        return pltpu.make_async_remote_copy(
            src_ref=src,
            dst_ref=dst,
            send_sem=send,
            recv_sem=recv,
            device_id=where,
            device_id_type=pl.DeviceIdType.MESH,
        )

    barrier = pltpu.get_barrier_semaphore()
    for d in range(1, n_b):
        pl.semaphore_signal(
            barrier,
            inc=1,
            device_id={"bucket": (me_b + d) % n_b},
            device_id_type=pl.DeviceIdType.MESH,
        )
    for d in range(1, n_r):
        pl.semaphore_signal(
            barrier,
            inc=1,
            device_id={"round": (me_r + d) % n_r},
            device_id_type=pl.DeviceIdType.MESH,
        )
    pl.semaphore_wait(barrier, n_b + n_r - 2)

    def order(i):
        return jnp.where(i < half, 2 * i, 2 * (i - half) + 1)

    down = lax.broadcasted_iota(jnp.int32, (seqs, seqs), 0)
    across = lax.broadcasted_iota(jnp.int32, (seqs, seqs), 1)
    to_inner = (down == order(across)).astype(jnp.float32)
    to_outer = (order(down) == across).astype(jnp.float32)

    tiles, per_row, tile, _ = coef_ref.shape[1:]
    for m in range(tiles):
        for c in range(tiles):
            value = jnp.zeros((tile, tile), jnp.float32)
            for t in range(per_row):
                value = value + jnp.where(col_ref[0, m, t] == c, coef_ref[0, m, t], 0.0)
            mixer[m * tile : (m + 1) * tile, c * tile : (c + 1) * tile] = value
    mixer[...] = exact(to_outer, exact(mixer[...], to_inner))
    ys[...] = exact(y_ref[0], to_inner)
    for r in range(n_r - 1):
        place = order(lax.broadcasted_iota(jnp.int32, (seqs, half), 0))
        gather[r] = (place == pred_ref[r : r + 1, :]).astype(jnp.float32)

    def columns(j):
        return pl.ds(pl.multiple_of(j * rows, rows), rows)

    def coded(value, code_ref, scale_ref):
        top = jnp.max(jnp.abs(value), axis=0, keepdims=True)
        unit = jnp.maximum(top, 1e-30) / 32767.0
        code = jnp.floor(value * (1.0 / unit) + 0.5)
        code_ref[...] = code.astype(jnp.int32).astype(jnp.int16)
        scale_ref[...] = jnp.broadcast_to(unit, scale_ref.shape)

    def decoded(code_ref, scale_ref):
        return code_ref[...].astype(jnp.int32).astype(jnp.float32) * scale_ref[0:1, :]

    def prox(state, sign, factor, weight, short):
        def row_copy(d):
            s = (me_r + d) % n_r
            here = grad.at[pl.ds(pl.multiple_of(s * part, part), part)]
            if not short:
                return [
                    remote(here, rows_in.at[me_r], row_send.at[s], row_recv.at[me_r], round=s)
                ]
            return [
                remote(
                    row_q.at[s], row_q_in.at[me_r], row_send.at[s], row_recv.at[me_r], round=s
                ),
                remote(
                    row_s.at[s], row_s_in.at[me_r], row_s_send.at[s], row_s_recv.at[me_r], round=s
                ),
            ]

        def row_arrival(d):
            s = (me_r + d) % n_r
            if not short:
                return [
                    remote(rows_in.at[s], rows_in.at[s], row_send.at[s], row_recv.at[s], round=s)
                ]
            return [
                remote(row_q_in.at[s], row_q_in.at[s], row_send.at[s], row_recv.at[s], round=s),
                remote(
                    row_s_in.at[s], row_s_in.at[s], row_s_send.at[s], row_s_recv.at[s], round=s
                ),
            ]

        for d in range(1, n_r):
            if short:
                s = (me_r + d) % n_r
                here = pl.ds(pl.multiple_of(s * part, part), part)
                coded(grad[here, :], row_q.at[s], row_s.at[s])
            for copy in row_copy(d):
                copy.start()
        squares = grad[...]
        squares = jnp.sum((squares * squares).reshape(rows // 8, 8, seqs), axis=0)
        squares = sum(squares[:, i * 128 : (i + 1) * 128] for i in range(seqs // 128))
        sq_b[me_b] = squares

        def sqb_copy(d):
            s = (me_b + d) % n_b
            return remote(
                sq_b.at[me_b], sq_b.at[me_b], sqb_send.at[d], sqb_recv.at[me_b], bucket=s
            )

        def sqb_arrival(d):
            s = (me_b + d) % n_b
            return remote(sq_b.at[s], sq_b.at[s], sqb_send.at[d], sqb_recv.at[s], bucket=s)

        for d in range(1, n_b):
            sqb_copy(d).start()
        rows_in[me_r] = grad[pl.ds(pl.multiple_of(me_r * part, part), part), :]
        for d in range(1, n_b):
            sqb_arrival(d).wait_recv()
        sq_r[me_r] = jnp.sum(sq_b[...], axis=0)

        def sqr_copy(d):
            s = (me_r + d) % n_r
            return remote(sq_r.at[me_r], sq_r.at[me_r], sqr_send.at[d], sqr_recv.at[me_r], round=s)

        def sqr_arrival(d):
            s = (me_r + d) % n_r
            return remote(sq_r.at[s], sq_r.at[s], sqr_send.at[d], sqr_recv.at[s], round=s)

        for d in range(1, n_r):
            sqr_copy(d).start()
        for d in range(1, n_r):
            sqr_arrival(d).wait_recv()
        squares = jnp.sum(jnp.sum(sq_r[...], axis=0), axis=0, keepdims=True)
        squares = jnp.sum(squares, axis=1, keepdims=True)
        scale = sign / (factor * jnp.sqrt(squares / total_count + epsilon))
        for d in range(1, n_r):
            for copy in row_arrival(d):
                copy.wait_recv()
            if short:
                s = (me_r + d) % n_r
                rows_in[s] = decoded(row_q_in.at[s], row_s_in.at[s])

        for r in reversed(range(n_r)):
            values = rows_in[r] * scale
            if r < n_r - 1:
                values = values + exact(norm[r + 1], gather[r], nt)
            score[r] = values
            even, odd = values[:, :half], values[:, half:]
            larger = jnp.maximum(even, odd)
            norm[r] = larger + jnp.log(jnp.exp(even - larger) + jnp.exp(odd - larger))

        def back_copy(r):
            if not short:
                return [
                    remote(
                        mass.at[r], back_in.at[me_r], back_send.at[r], back_recv.at[me_r], round=r
                    )
                ]
            return [
                remote(
                    back_q.at[r], back_q_in.at[me_r], back_send.at[r], back_recv.at[me_r], round=r
                ),
                remote(
                    back_s.at[r],
                    back_s_in.at[me_r],
                    back_s_send.at[r],
                    back_s_recv.at[me_r],
                    round=r,
                ),
            ]

        def back_arrival(s):
            if not short:
                return [
                    remote(
                        back_in.at[s], back_in.at[s], back_send.at[s], back_recv.at[s], round=s
                    )
                ]
            return [
                remote(
                    back_q_in.at[s], back_q_in.at[s], back_send.at[s], back_recv.at[s], round=s
                ),
                remote(
                    back_s_in.at[s], back_s_in.at[s], back_s_send.at[s], back_s_recv.at[s], round=s
                ),
            ]

        for r in range(n_r):
            even = jnp.exp(score[r, :, :half] - norm[r])
            odd = jnp.exp(score[r, :, half:] - norm[r])
            if r > 0:
                parent = exact(mass[r - 1], gather[r - 1])
                even = parent * even
                odd = parent * odd
            mass[r, :, :half] = even
            mass[r, :, half:] = odd

            @pl.when(me_r != r)
            def _():
                if short:
                    coded(mass[r], back_q.at[r], back_s.at[r])
                for copy in back_copy(r):
                    copy.start()

        def update(s, best):
            here = pl.ds(pl.multiple_of(s * part, part), part)
            state[here, :] = (1.0 - weight) * state[here, :] + weight * best

        update(me_r, mass[me_r])
        for d in range(1, n_r):
            s = (me_r + d) % n_r
            for copy in back_arrival(s):
                copy.wait_recv()
            if short:
                update(s, decoded(back_q_in.at[s], back_s_in.at[s]))
            else:
                update(s, back_in[s])
        for d in range(1, n_r):
            for copy in row_copy(d) + back_copy((me_r + d) % n_r):
                copy.wait_send()
            sqr_copy(d).wait_send()
        for d in range(1, n_b):
            sqb_copy(d).wait_send()

    def step(index, _):
        weight = 2.0 / (index.astype(jnp.float32) + 3.0)
        short = False

        blocks[me_b] = exact(ys[...], mixer[...], nt).astype(jnp.bfloat16)

        def own_copy(kind):
            target = (sibling, me_b + 2, me_b - 2)[kind]
            return remote(
                blocks.at[me_b], blocks.at[me_b], ag_send.at[kind], ag_recv.at[me_b], bucket=target
            )

        def go_on(b, d, step):
            return remote(
                blocks.at[b], blocks.at[b], line_send.at[d], ag_recv.at[b], bucket=me_b + step
            )

        def pass_on(b, d):
            return remote(blocks.at[b], blocks.at[b], fw_send.at[d], ag_recv.at[b], bucket=sibling)

        def arrival(b):
            return remote(
                blocks.at[b], blocks.at[b], ag_send.at[0], ag_recv.at[b], bucket=sibling
            )

        def product(b):
            return jnp.dot(
                pay_ref[0, :, columns(b)], blocks[b], preferred_element_type=jnp.float32
            )

        @pl.when(pair < pairs - 1)
        def _():
            own_copy(1).start()

        @pl.when(pair > 0)
        def _():
            own_copy(2).start()

        own_copy(0).start()
        @pl.when(index == 0)
        def _():
            xs[...] = exact(x_ref[0], to_inner)

            def turn(j, _):
                pay_t[columns(j), :] = pay_ref[0, :, columns(j)].T
                return 0

            lax.fori_loop(0, n_b, turn, 0)
        grad[...] = product(me_b)
        arrival(sibling).wait_recv()
        grad[...] += product(sibling)

        def take(d, _):
            left = me_b - 2 * d
            right = me_b + 2 * d

            @pl.when(pair >= d)
            def _():
                arrival(left).wait_recv()

                @pl.when(pair < pairs - 1)
                def _():
                    go_on(left, d, 2).start()

                pass_on(left, d).start()

            @pl.when(pair + d < pairs)
            def _():
                arrival(right).wait_recv()

                @pl.when(pair > 0)
                def _():
                    go_on(right, pairs + d, -2).start()

                pass_on(right, pairs + d).start()

            def use(b, other):
                grad[...] += product(b)
                arrival(other).wait_recv()
                grad[...] += product(other)

            @pl.when(pair >= d)
            def _():
                use(left, sibling - 2 * d)

            @pl.when(pair + d < pairs)
            def _():
                use(right, sibling + 2 * d)

            return 0

        lax.fori_loop(1, pairs, take, 0)

        def drain(d, _):
            left = me_b - 2 * d
            right = me_b + 2 * d

            @pl.when(pair >= d)
            def _():
                pass_on(left, d).wait_send()

                @pl.when(pair < pairs - 1)
                def _():
                    go_on(left, d, 2).wait_send()

            @pl.when(pair + d < pairs)
            def _():
                pass_on(right, pairs + d).wait_send()

                @pl.when(pair > 0)
                def _():
                    go_on(right, pairs + d, -2).wait_send()

            return 0

        lax.fori_loop(1, pairs, drain, 0)
        own_copy(0).wait_send()

        @pl.when(pair < pairs - 1)
        def _():
            own_copy(1).wait_send()

        @pl.when(pair > 0)
        def _():
            own_copy(2).wait_send()

        prox(xs, -1.0, smooth_x, weight, short)

        mixed[...] = exact(xs[...], mixer[...]).astype(jnp.bfloat16)

        def partial(b):
            return jnp.dot(pay_t[columns(b), :], mixed[...], preferred_element_type=jnp.float32)

        def sib_copy(q):
            return remote(
                sib_out.at[q], sib_in.at[q], sib_send.at[q], sib_recv.at[q], bucket=sibling
            )

        def far_copy(q, step, target):
            slot = q if step > 0 else pairs + q
            if not short:
                return [
                    remote(
                        far_out.at[q],
                        far_in.at[slot],
                        far_send.at[q],
                        far_recv.at[slot],
                        bucket=target,
                    )
                ]
            return [
                remote(
                    far_q.at[q],
                    far_q_in.at[slot],
                    far_send.at[q],
                    far_recv.at[slot],
                    bucket=target,
                ),
                remote(
                    far_s.at[q],
                    far_s_in.at[slot],
                    far_s_send.at[q],
                    far_s_recv.at[slot],
                    bucket=target,
                ),
            ]

        def far_value(q, step):
            slot = q if step > 0 else pairs + q
            for copy in far_copy(q, step, sibling):
                copy.wait_recv()
            if short:
                return decoded(far_q_in.at[slot], far_s_in.at[slot])
            return far_in[slot]

        def to_sibling(q):
            sib_out[q] = partial(q * 2 + 1 - core)
            sib_copy(q).start()

        def move(q, step):
            far_out[q] = partial(q * 2 + core)
            sib_copy(q).wait_recv()
            far_out[q] += sib_in[q]

            @pl.when(pair > 0 if step > 0 else pair < pairs - 1)
            def _():
                far_out[q] += far_value(q, step)

            if short:
                coded(far_out[q], far_q.at[q], far_s.at[q])
            for copy in far_copy(q, step, me_b + step):
                copy.start()

        def outward(right, left):
            def one(i, _):
                @pl.when(pair < pairs - 1 - i)
                def _():
                    right(pairs - 1 - i)

                @pl.when(pair > i)
                def _():
                    left(i)

                return 0

            lax.fori_loop(0, pairs - 1, one, 0)

        def far_done(q, step):
            for copy in far_copy(q, step, me_b + step):
                copy.wait_send()

        outward(to_sibling, to_sibling)
        outward(lambda q: move(q, 2), lambda q: move(q, -2))
        to_sibling(pair)
        grad[...] = partial(me_b)
        sib_copy(pair).wait_recv()
        grad[...] += sib_in[pair]

        @pl.when(pair > 0)
        def _():
            grad[...] += far_value(pair, 2)

        @pl.when(pair < pairs - 1)
        def _():
            grad[...] += far_value(pair, -2)

        outward(lambda q: far_done(q, 2), lambda q: far_done(q, -2))
        for q in range(pairs):
            sib_copy(q).wait_send()
        prox(ys, 1.0, smooth_y, weight, short)
        return 0

    lax.fori_loop(0, 2, step, 0)
    down = lax.broadcasted_iota(jnp.int32, (seqs, seqs), 0)
    across = lax.broadcasted_iota(jnp.int32, (seqs, seqs), 1)
    to_outer = (order(down) == across).astype(jnp.float32)
    xo_ref[0] = exact(xs[...], to_outer)
    yo_ref[0] = exact(ys[...], to_outer)


def plain_body(x_start, y_start, bucket_payoff, column_blocks, public_coef, predecessor_sequences):
    n_r = lax.axis_size("round")
    n_b = lax.axis_size("bucket")
    _, rows, seqs = x_start.shape
    part = rows // n_r
    pairs = n_b // 2
    f32, bf16 = jnp.float32, jnp.bfloat16
    vmem = pl.BlockSpec(memory_space=pltpu.VMEM)
    smem = pl.BlockSpec(memory_space=pltpu.SMEM)
    dma = pltpu.SemaphoreType.DMA
    return pl.pallas_call(
        functools.partial(plain_kernel, n_r, n_b),
        out_shape=[jax.ShapeDtypeStruct(x_start.shape, f32)] * 2,
        in_specs=[vmem, vmem, vmem, smem, vmem, vmem],
        out_specs=[vmem, vmem],
        scratch_shapes=[
            pltpu.VMEM((rows, seqs), f32),
            pltpu.VMEM((rows, seqs), f32),
            pltpu.VMEM((seqs, seqs), f32),
            pltpu.VMEM((n_r - 1, seqs, seqs // 2), f32),
            pltpu.VMEM((n_b * rows, rows), bf16),
            pltpu.VMEM((n_b, rows, seqs), bf16),
            pltpu.VMEM((rows, seqs), bf16),
            pltpu.VMEM((rows, seqs), f32),
            pltpu.VMEM((pairs, rows, seqs), f32),
            pltpu.VMEM((pairs, rows, seqs), f32),
            pltpu.VMEM((pairs, rows, seqs), f32),
            pltpu.VMEM((2 * pairs, rows, seqs), f32),
            pltpu.VMEM((n_b, 8, 128), f32),
            pltpu.VMEM((n_r, 8, 128), f32),
            pltpu.VMEM((n_r, part, seqs), f32),
            pltpu.VMEM((n_r, part, seqs), f32),
            pltpu.VMEM((n_r, part, seqs // 2), f32),
            pltpu.VMEM((n_r, part, seqs), f32),
            pltpu.VMEM((n_r, part, seqs), f32),
            pltpu.VMEM((16, 128), jnp.int16),
            pltpu.VMEM((pairs, 8, seqs), f32),
            pltpu.VMEM((16, 128), jnp.int16),
            pltpu.VMEM((2 * pairs, 8, seqs), f32),
            pltpu.VMEM((16, 128), jnp.int16),
            pltpu.VMEM((n_r, 8, seqs), f32),
            pltpu.VMEM((16, 128), jnp.int16),
            pltpu.VMEM((n_r, 8, seqs), f32),
            pltpu.VMEM((16, 128), jnp.int16),
            pltpu.VMEM((n_r, 8, seqs), f32),
            pltpu.VMEM((16, 128), jnp.int16),
            pltpu.VMEM((n_r, 8, seqs), f32),
            dma((3,)),
            dma((n_b,)),
            dma((2 * pairs,)),
            dma((2 * pairs,)),
            dma((pairs,)),
            dma((pairs,)),
            dma((pairs,)),
            dma((2 * pairs,)),
            dma((n_b,)),
            dma((n_b,)),
            dma((n_r,)),
            dma((n_r,)),
            dma((n_r,)),
            dma((n_r,)),
            dma((n_r,)),
            dma((n_r,)),
            dma((pairs,)),
            dma((2 * pairs,)),
            dma((n_r,)),
            dma((n_r,)),
            dma((n_r,)),
            dma((n_r,)),
        ],
        compiler_params=pltpu.CompilerParams(
            collective_id=0, has_side_effects=True, vmem_limit_bytes=60 * 1024 * 1024
        ),
    )(x_start, y_start, bucket_payoff, column_blocks, public_coef, predecessor_sequences)


def solution(mesh):
    in_specs = (
        P("round", "bucket", None),
        P("round", "bucket", None),
        P("round", "bucket", None),
        P("round", None, None),
        P("round", None, None, None, None),
        P(),
    )
    out_specs = (P("round", "bucket", None), P("round", "bucket", None))

    line = mesh.shape["round"] == 4 and mesh.shape["bucket"] == 8

    def run(*arrays):
        return tuple(
            jax.shard_map(
                line_body if line else plain_body, mesh=mesh, in_specs=in_specs, out_specs=out_specs, check_vma=False
            )(*arrays)
        )

    return run
```

```python
import functools
import types

import jax
import jax.numpy as jnp
from jax import lax
from jax.experimental import pallas as pl
from jax.experimental.pallas import tpu as pltpu
from jax.sharding import PartitionSpec as P

smooth_x = 0.1
smooth_y = 0.1
epsilon = 1e-06
highest = lax.Precision.HIGHEST
nn = (((1,), (0,)), ((), ()))
nt = (((1,), (1,)), ((), ()))


def exact(a, b, dims=nn):
    return lax.dot_general(a, b, dims, precision=highest, preferred_element_type=jnp.float32)


weights = (2.0 / 3.0, 2.0 / 4.0)
top_code = 65535.0
shift_code = 32768


def split3(value):
    hi = value.astype(jnp.bfloat16)
    left = value - hi.astype(jnp.float32)
    mid = left.astype(jnp.bfloat16)
    lo = (left - mid.astype(jnp.float32)).astype(jnp.bfloat16)
    return [hi, mid, lo]


def dot(a, b, dims=nn):
    return lax.dot_general(a, b, dims, preferred_element_type=jnp.float32)


def picked(parts, one_hot, dims=nn):
    size = parts[0].shape[0]
    out = dot(jnp.concatenate(parts, axis=0), one_hot, dims)
    return sum(out[i * size : (i + 1) * size] for i in range(len(parts)))


def mix(parts, factors, dims):
    size = parts[0].shape[0]
    total = None
    for i, factor in reversed(list(enumerate(factors))):
        count = min(len(parts), 3 - i)
        out = dot(jnp.concatenate(parts[:count], axis=0), factor, dims)
        for j in reversed(range(count)):
            term = out[j * size : (j + 1) * size]
            total = term if total is None else total + term
    return total


def encode(value, code_ref):
    if len(code_ref.shape) == 3:
        wide = code_ref.shape[2]
        for i in range(code_ref.shape[0]):
            encode(value[:, i * wide : (i + 1) * wide], code_ref.at[i])
        return
    rows = value.shape[0]
    top = jnp.maximum(jnp.max(jnp.abs(value), axis=0, keepdims=True), 1e-30)
    power = jnp.floor(256.0 * jnp.log2(top * (1.0 / 32767.0))) + 1.0
    code = jnp.floor(value * jnp.exp2(power * (-1.0 / 256.0)) + 0.5)
    code_ref[:rows, :] = code.astype(jnp.int32).astype(jnp.int16)
    power = jnp.broadcast_to(power, (16, value.shape[1]))
    code_ref[rows:, :] = power.astype(jnp.int32).astype(jnp.int16)


def decode(code_ref):
    if len(code_ref.shape) == 3:
        return jnp.concatenate([decode(code_ref.at[i]) for i in range(code_ref.shape[0])], axis=1)
    rows = code_ref.shape[0] - 16
    power = code_ref[rows:, :].astype(jnp.int32).astype(jnp.float32)[0:1, :]
    unit = jnp.exp2(power * (1.0 / 256.0))
    return code_ref[:rows, :].astype(jnp.int32).astype(jnp.float32) * unit


def line_kernel(names, n_r, n_b, *refs):
    k = types.SimpleNamespace(**dict(zip(names, refs)))
    f32, bf16 = jnp.float32, jnp.bfloat16
    _, rows, seqs = k.x_hbm.shape
    half = seqs // 2
    wide = half // 2
    part = rows // n_r
    pairs = n_b // 2
    me_r = lax.axis_index("round")
    me_b = lax.axis_index("bucket")
    pair = me_b // 2
    core = me_b % 2
    sibling = pair * 2 + 1 - core
    spans = ((0, slice(0, half)), (1, slice(0, wide)), (1, slice(wide, half)))
    quarters = (slice(0, 2), slice(2, 3), slice(3, 4))
    members = ((0, 1), (2,), (3,))
    outward = jnp.where(pair < pairs // 2, -2, 2)
    end_chip = jnp.where(pair < pairs // 2, 0, pairs - 1)
    facing = pair - outward // 2
    far_end = pairs - 1 - end_chip
    inner = (pair > 0) & (pair < pairs - 1)
    total_count = n_r * n_b * rows * seqs

    def remote(src, dst, send, recv, **where):
        return pltpu.make_async_remote_copy(
            src_ref=src,
            dst_ref=dst,
            send_sem=send,
            recv_sem=recv,
            device_id=where,
            device_id_type=pl.DeviceIdType.MESH,
        )

    load_y = pltpu.make_async_copy(k.y_hbm, k.yv, k.load_sem.at[0])
    load_pay = pltpu.make_async_copy(k.pay_hbm, k.pay, k.load_sem.at[1])
    load_x = pltpu.make_async_copy(k.x_hbm, k.xv, k.load_sem.at[2])
    load_y.start()
    load_pay.start()
    load_x.start()

    barrier = pltpu.get_barrier_semaphore()
    for dr in range(n_r):
        for db in range(n_b):
            if dr or db:
                pl.semaphore_signal(
                    barrier,
                    inc=1,
                    device_id={"round": (me_r + dr) % n_r, "bucket": (me_b + db) % n_b},
                    device_id_type=pl.DeviceIdType.MESH,
                )

    def order(i):
        return 2 * (i // half * wide + i % wide) + (i % half) // wide

    down = lax.broadcasted_iota(jnp.int32, (seqs, seqs), 0)
    across = lax.broadcasted_iota(jnp.int32, (seqs, seqs), 1)
    k.to_outer[...] = (order(down) == across).astype(f32).astype(bf16)

    tiles, per_row, tile, _ = k.coef_ref.shape[1:]
    for m in range(tiles):
        for c in range(tiles):
            value = jnp.zeros((tile, tile), f32)
            for t in range(per_row):
                value = value + jnp.where(k.col_ref[t, 0, m] == c, k.coef_ref[0, m, t], 0.0)
            k.mixer[m * tile : (m + 1) * tile, c * tile : (c + 1) * tile] = value
    for i, piece in enumerate(split3(k.mixer[...])):
        k.mix_p[i] = dot(k.to_outer[...], piece).astype(bf16)

    def rows_of(s):
        return pl.ds(pl.multiple_of(s * part, part), part)

    def columns(j):
        return pl.ds(pl.multiple_of(j * rows, rows), rows)

    away = jnp.where(pair < pairs // 2, pairs // 2, 0)

    def lent_place(o):
        return (far_end - away, 1 - (far_end - away))[o]

    def lend(turn):
        o, i, p = turn // 4, turn // 2 % 2, turn % 2
        here = pl.ds(p * (rows // 2), rows // 2)
        b = 2 * lent_place(o) + i
        return remote(
            k.pay.at[0, here, columns(2 * away + b)],
            k.lent.at[b, here],
            k.lend_send.at[turn],
            k.lend_recv.at[turn],
            bucket=me_b - outward,
        )

    def lend_start(turns):
        @pl.when(jnp.logical_not(inner))
        def _():
            for turn in turns:
                lend(turn).start()

    def lent_swap(j, o):
        return remote(
            k.pay_out.at[j],
            k.lent_t.at[j, core],
            k.swap_send.at[o],
            k.swap_recv.at[o],
            bucket=sibling,
        )

    def take_lent(o):
        j = lent_place(o)
        for i in range(2):
            for p in range(2):
                here = k.lent.at[2 * j + i, pl.ds(p * (rows // 2), rows // 2)]
                turn = 4 * o + 2 * i + p
                remote(
                    here, here, k.lend_send.at[turn], k.lend_recv.at[turn], bucket=sibling
                ).wait_recv()
        k.pay_out[j] = k.lent[2 * j + 1 - core].T
        lent_swap(j, o).start()
        k.lent_t[j, core] = k.lent[2 * j + core].T
        lent_swap(j, o).wait()


    def own_copy(kind, s):
        target = (sibling, me_b + 2, me_b - 2)[kind]
        here = k.blocks.at[me_b, :, rows_of(s), :]
        return remote(here, here, k.ag_send.at[kind, s], k.ag_recv.at[me_b, s], bucket=target)

    def own_start(s):
        @pl.when(pair < pairs - 1)
        def _():
            own_copy(1, s).start()

        @pl.when(pair > 0)
        def _():
            own_copy(2, s).start()

        own_copy(0, s).start()

    def own_drain(s):
        @pl.when(pair < pairs - 1)
        def _():
            own_copy(1, s).wait_send()

        @pl.when(pair > 0)
        def _():
            own_copy(2, s).wait_send()

        own_copy(0, s).wait_send()

    def set_own(s, value):
        value = value.astype(bf16)
        for c in range(4):
            k.blocks[me_b, c, rows_of(s), :] = value[:, c * wide : (c + 1) * wide]

    pl.semaphore_wait(barrier, n_b * n_r - 1)
    load_y.wait()
    load_pay.wait()
    lend_start(range(1))
    for s in range(n_r):
        value = mix(split3(k.yv[0, rows_of(s), :]), [k.mix_p[i] for i in range(3)], nt)
        k.f_y[rows_of(s), :] = value
        set_own(s, value)
        own_start(s)

    def part_of(b, s):
        return k.blocks.at[b, :, rows_of(s), :]

    def unit_of(b, c):
        return k.blocks.at[b, c]

    def block(b, u):
        return jnp.concatenate([k.blocks[b, c] for c in members[u]], axis=1)

    def by_parts(b):
        for s in range(n_r):
            arrived(part_of(b, s), b, s)

    def by_whole(b):
        arrived(k.blocks.at[b], b, 0)

    def by_unit(b, c):
        arrived(unit_of(b, c), b, c)

    def arrived(here, b, i):
        remote(here, here, k.ag_send.at[0, 0], k.ag_recv.at[b, i], bucket=sibling).wait_recv()

    def go_on(here, b, i, step):
        return remote(here, here, k.line_send.at[b, i], k.ag_recv.at[b, i], bucket=me_b + step)

    def pass_on(here, b, i):
        return remote(here, here, k.pass_send.at[b, i], k.ag_recv.at[b, i], bucket=sibling)

    def add_product(b, u):
        value = dot(k.pay[0, :, columns(b)], block(b, u))
        for i, c in enumerate(members[u]):
            k.grad[c] += value[:, i * wide : (i + 1) * wide]

    def lent_product(b, c):
        return dot(k.lent[b - 2 * away], k.blocks[b, c])

    def setup():
        lend_start(range(1, 5))


        def turn(q, _):
            k.pay_out[q] = k.pay[0, :, columns(q * 2 + 1 - core)].T
            turned(q).start()
            k.pay_t[q, core] = k.pay[0, :, columns(q * 2 + core)].T
            return 0

        lax.fori_loop(0, pairs, turn, 0)
        for r in range(n_r - 1):
            place = order(lax.broadcasted_iota(jnp.int32, (seqs, half), 0))
            one_hot = (place == k.pred_ref[r : r + 1, :]).astype(f32).astype(bf16)
            k.gather[r] = one_hot
            k.spread[r] = one_hot.T

        @pl.when(me_r == 0)
        def _():
            for s in range(n_r):
                k.back_in[s, 1] = jnp.full((part, half), 65535 - shift_code, jnp.int32).astype(
                    jnp.int16
                )

        load_x.wait()
        value = picked(split3(exact(k.xv[0], k.mixer[...])), k.to_outer[...], nt)
        k.f_x[...] = value
        for i in range(3):
            k.mix_p[i] = dot(k.mix_p[i], k.to_outer[...], nt).astype(bf16)

    def turned(q):
        return remote(
            k.pay_out.at[q],
            k.pay_t.at[q, core],
            k.turn_send.at[q],
            k.turn_recv.at[q],
            bucket=sibling,
        )


    def row_copy(d, u):
        s = (me_r + d) % n_r
        return remote(
            k.row_q.at[s, quarters[u]],
            k.row_in.at[me_r, quarters[u]],
            k.row_send.at[s, u],
            k.row_recv.at[me_r, u],
            round=s,
        )

    def row_arrival(d, u):
        s = (me_r + d) % n_r
        h, lanes = spans[u]
        here = k.row_in.at[s, quarters[u]]
        remote(here, here, k.row_send.at[s, u], k.row_recv.at[s, u], round=s).wait_recv()
        k.rows_f[s, h, :, lanes] = decode(here)

    def finish(u):
        for c in members[u]:
            squares = k.grad[c]
            squares = jnp.sum((squares * squares).reshape(rows // 8, 8, wide), axis=0)
            if c == 0:
                k.sq_mine[...] = squares
            else:
                k.sq_mine[...] += squares
        if u == 2:
            k.sq_all[me] = jnp.sum(k.sq_mine[...], axis=0, keepdims=True)
            for dr, db in others:
                square_copy(dr, db).start()
        for d in range(1, n_r):
            s = (me_r + d) % n_r
            for c in members[u]:
                encode(k.grad[c, rows_of(s), :], k.row_q.at[s, c])
            row_copy(d, u).start()
        for c in members[u]:
            h, lanes = c // 2, slice(c % 2 * wide, c % 2 * wide + wide)
            k.rows_f[me_r, h, :, lanes] = k.grad[c, rows_of(me_r), :]

    me = me_r * n_b + me_b

    def square_copy(dr, db):
        here = k.sq_all.at[me]
        return remote(
            here,
            here,
            k.sq_send.at[dr * n_b + db],
            k.sq_recv.at[me],
            round=(me_r + dr) % n_r,
            bucket=(me_b + db) % n_b,
        )

    def square_arrival(dr, db):
        s = (me_r + dr) % n_r * n_b + (me_b + db) % n_b
        here = k.sq_all.at[s]
        return remote(here, here, k.sq_send.at[0], k.sq_recv.at[s], bucket=sibling)

    others = [(dr, db) for dr in range(n_r) for db in range(n_b) if dr or db]

    def back_copy(r, i):
        return remote(
            k.back_q.at[r, i],
            k.back_in.at[me_r, i],
            k.back_send.at[r, i],
            k.back_recv.at[me_r, i],
            round=r,
        )

    def back_arrival(s):
        for i in range(2):

            def wait():
                here = k.back_in.at[s, i]
                remote(
                    here, here, k.back_send.at[s, i], k.back_recv.at[s, i], round=s
                ).wait_recv()

            if i == 0:
                wait()
            else:
                pl.when(me_r > 0)(wait)

    def back_drain(s):
        back_copy(s, 0).wait_send()

        @pl.when(s > 0)
        def _():
            back_copy(s, 1).wait_send()

    def give_back(r, i, value):
        code = jnp.floor(value * top_code + 0.5).astype(jnp.int32) - shift_code
        k.back_q[r, i] = code.astype(jnp.int16)

        @pl.when(me_r != r)
        def _():
            back_copy(r, i).start()

        @pl.when(me_r == r)
        def _():
            k.back_in[me_r, i] = k.back_q[r, i]

    def prox(sign, factor, after_scale=None):
        for u in range(2):
            for d in range(1, n_r):
                row_arrival(d, u)
        for d in range(1, n_r):
            row_arrival(d, 2)
        for dr, db in others:
            square_arrival(dr, db).wait_recv()
        squares = jnp.sum(k.sq_all[...], axis=0)
        squares = jnp.sum(squares, axis=1, keepdims=True)
        scale = sign / (factor * jnp.sqrt(squares / total_count + epsilon))

        if after_scale is not None:
            after_scale()
        carried = None
        for r in reversed(range(n_r)):
            norms = []
            evens = []
            for h in range(2):
                values = k.rows_f[r, h] * scale
                if carried is not None:
                    values = values + carried[:, h * half : (h + 1) * half]
                even, odd = values[:, :wide], values[:, wide:]
                small = jnp.exp(-jnp.abs(even - odd))
                larger = 1.0 / (1.0 + small)
                smaller = small * larger
                ahead = even >= odd
                evens.append(jnp.where(ahead, larger, smaller))
                k.share[r, h, :, :wide] = evens[h]
                k.share[r, h, :, wide:] = jnp.where(ahead, smaller, larger)
                norms.append(jnp.maximum(even, odd) + jnp.log(1.0 + small))
            give_back(r, 0, jnp.concatenate(evens, axis=1))
            if r > 0:
                norm = jnp.concatenate(norms, axis=1)
                carried = picked(split3(norm), k.spread[r - 1])

        mass = jnp.concatenate([k.share[0, 0], k.share[0, 1]], axis=1)
        for r in range(1, n_r):
            parent = picked(split3(mass), k.gather[r - 1])
            give_back(r, 1, parent)
            above = [parent[:, h * wide : (h + 1) * wide] for h in (0, 0, 1, 1)]
            shares = jnp.concatenate([k.share[r, 0], k.share[r, 1]], axis=1)
            mass = shares * jnp.concatenate(above, axis=1)

    def prox_drain():
        for d in range(1, n_r):
            for u in range(3):
                row_copy(d, u).wait_send()
            back_drain((me_r + d) % n_r)
        for dr, db in others:
            square_copy(dr, db).wait_send()

    def pieces(s):
        share, parent = [
            (k.back_in[s, i].astype(jnp.int32) + shift_code).astype(f32) * (1.0 / top_code)
            for i in range(2)
        ]
        even = parent * share
        odd = parent - even
        both = (even[:, :wide], odd[:, :wide], even[:, wide:], odd[:, wide:])
        whole = jnp.concatenate(both, axis=1)
        return split3(whole)[:2]

    def mixed_part(s, state, weight, dims):
        value = mix(pieces(s), [k.mix_p[i] for i in range(3)], dims)
        value = (1.0 - weight) * state[rows_of(s), :] + weight * value
        state[rows_of(s), :] = value
        return value

    def add_best(out, s, share):
        best = picked(pieces(s), k.to_outer[...])
        out[0, rows_of(s), :] += share * best


    def mixed_copy(s):
        here = k.mixed.at[core, :, rows_of(s), :]
        return remote(here, here, k.mx_send.at[s], k.mx_recv.at[core, s], bucket=sibling)

    def mixed_arrival(s):
        here = k.mixed.at[1 - core, :, rows_of(s), :]
        return remote(here, here, k.mx_send.at[s], k.mx_recv.at[1 - core, s], bucket=sibling)

    def raw_copy(n):
        return remote(
            k.mixed.at[core, n],
            k.mixed.at[2 + core, n],
            k.raw_send.at[n],
            k.raw_recv.at[core, n],
            bucket=me_b - outward,
        )

    def raw_pass(n):
        here = k.mixed.at[2 + core, n]
        return remote(here, here, k.raw_send.at[n], k.raw_recv.at[core, n], bucket=sibling)

    def raw_arrival(source, n):
        here = k.mixed.at[2 + source, n]
        remote(
            here, here, k.raw_send.at[n], k.raw_recv.at[source, n], bucket=sibling
        ).wait_recv()

    def partial(q, n):
        return dot(k.pay_t[q, 0], k.mixed[0, n]) + dot(k.pay_t[q, 1], k.mixed[1, n])

    def lent_partial(j, n):
        return dot(k.lent_t[j, 0], k.mixed[2, n]) + dot(k.lent_t[j, 1], k.mixed[3, n])

    def sum_copy(kind, n, step):
        return remote(
            k.sum_out.at[kind, n],
            k.sum_in.at[kind, n],
            k.sum_send.at[kind, n],
            k.sum_recv.at[kind, n],
            bucket=me_b + step,
        )

    def sum_arrival(kind, n):
        here = k.sum_in.at[kind, n]
        remote(
            here, here, k.sum_send.at[kind, n], k.sum_recv.at[kind, n], bucket=sibling
        ).wait_recv()
        return decode(here)

    def sums_of_end(index):
        def lend_sum(n, _):
            k.work[...] = partial(facing - outward // 2, n)
            encode(k.work[...], k.sum_out.at[4, n])
            sum_copy(4, n, -outward).start()
            return 0

        @pl.when(index == 0)
        def _():
            lax.fori_loop(0, 4, lend_sum, 0)

        def give(n, _):
            k.work[...] = partial(facing, n)
            encode(k.work[...], k.sum_out.at[3, n])
            sum_copy(3, n, -outward).start()
            return 0

        lax.fori_loop(0, 4, give, 0)

    def sums_of_inner(index):
        def give(i, _):
            n = i % 4

            @pl.when(i < 4)
            def _():
                raw_arrival(core, n)
                raw_pass(n).start()

            q = jnp.where(i < 4, far_end, facing)
            k.work[...] = partial(q, n)

            @pl.when(i < 4)
            def _():
                raw_arrival(1 - core, n)

            @pl.when((i < 4) | (index == 1))
            def _():
                k.work[...] += lent_partial(q - away, n)

            @pl.when((i >= 4) & (index == 0))
            def _():
                k.work[...] += sum_arrival(4, n)

            encode(k.work[...], k.sum_out.at[i // 4, n])
            sum_copy(i // 4, n, -outward).start()

            @pl.when((i >= 2) & (i < 6))
            def _():
                k.work[...] = partial(end_chip, i - 2)
                k.work[...] += sum_arrival(0, i - 2)
                encode(k.work[...], k.sum_out.at[2, i - 2])
                sum_copy(2, i - 2, outward).start()

            return 0

        lax.fori_loop(0, 8, give, 0)

    def sums_drain(index):
        @pl.when(inner)
        def _():
            for n in range(4):
                raw_pass(n).wait_send()
                sum_copy(0, n, -outward).wait_send()
                sum_copy(1, n, -outward).wait_send()
                sum_copy(2, n, outward).wait_send()

        @pl.when(jnp.logical_not(inner))
        def _():
            for n in range(4):
                raw_copy(n).wait_send()
                sum_copy(3, n, -outward).wait_send()

                @pl.when(index == 0)
                def _():
                    sum_copy(4, n, -outward).wait_send()

    def out_copy(i, s):
        here, there = ((k.xo_ref, k.x_out), (k.yo_ref, k.y_out))[i]
        return pltpu.make_async_copy(
            here.at[:, rows_of(s)], there.at[:, rows_of(s)], k.out_sem.at[i, s]
        )

    def step(index, _):
        weight = 2.0 / (index.astype(f32) + 3.0)

        @pl.when(index == 0)
        def _():
            setup()

        first = -outward
        second = jnp.where(inner, outward, -2 * outward)
        far = jnp.where(inner, -2 * outward, -3 * outward)

        for u in range(3):
            value = dot(k.pay[0, :, columns(me_b)], block(me_b, u))
            for i, c in enumerate(members[u]):
                k.grad[c] = value[:, i * wide : (i + 1) * wide]
        by_parts(sibling)
        for u in range(2 + 1):
            add_product(sibling, u)

        @pl.when(index == 0)
        def _():
            for q in range(pairs):
                turned(q).wait()
            k.xo_ref[...] = (1.0 - weights[0]) * (1.0 - weights[1]) * k.xv[...]
            k.yo_ref[...] = (1.0 - weights[0]) * (1.0 - weights[1]) * k.yv[...]

        @pl.when(index == 1)
        def _():
            for s in range(n_r):
                add_best(k.yo_ref, s, weights[0] * (1.0 - weights[1]))

        def both(offset):
            for u in range(3):
                add_product(me_b + offset, u)
            by_whole(sibling + offset)
            for u in range(3):
                add_product(sibling + offset, u)

        plain = index == 0
        b = me_b + first
        for s in range(n_r):
            arrived(part_of(b, s), b, s)

            @pl.when(inner & plain)
            def _():
                go_on(part_of(b, s), b, s, outward).start()

        pass_on(k.blocks.at[b], b, 0).start()
        b2 = me_b + second

        @pl.when(inner)
        def _():
            by_parts(b2)
            for c in range(4):
                go_on(unit_of(b2, c), b2, c, -outward).start()
            pass_on(k.blocks.at[b2], b2, 0).start()

        both(first)

        @pl.when(jnp.logical_not(inner) & plain)
        def _():
            by_parts(b2)
            pass_on(k.blocks.at[b2], b2, 0).start()

        @pl.when(inner | plain)
        def _():
            both(second)

        @pl.when(inner & jnp.logical_not(plain))
        def _():
            take_lent(1)
            for c in range(4):
                k.early[c] = lent_product(b, c) + lent_product(sibling + first, c)

        b3 = me_b + far
        for c in range(4):

            @pl.when(inner | plain)
            def _():
                by_unit(b3, c)

                @pl.when(inner & plain)
                def _():
                    go_on(unit_of(b3, c), b3, c, outward).start()

                pass_on(unit_of(b3, c), b3, c).start()

                @pl.when(plain)
                def _():
                    k.grad[c] += dot(k.pay[0, :, columns(b3)], k.blocks[b3, c])

                by_unit(sibling + far, c)

                @pl.when(jnp.logical_not(plain))
                def _():
                    k.early[c] += lent_product(b3, c) + lent_product(sibling + far, c)
                    encode(k.early[c], k.sum_out.at[5, c])
                    sum_copy(5, c, outward).start()
                    k.grad[c] += dot(k.pay[0, :, columns(b3)], k.blocks[b3, c])

                k.grad[c] += dot(k.pay[0, :, columns(sibling + far)], k.blocks[sibling + far, c])

            @pl.when(jnp.logical_not(inner | plain))
            def _():
                k.grad[c] += sum_arrival(5, c)

            if c > 0:
                finish(c - 1)

        @pl.when(inner & plain)
        def _():
            for c in range(4):
                go_on(part_of(b, c), b, c, outward).wait_send()
                go_on(unit_of(b3, c), b3, c, outward).wait_send()

        @pl.when(inner)
        def _():
            for c in range(4):
                go_on(unit_of(b2, c), b2, c, -outward).wait_send()

        pass_on(k.blocks.at[b], b, 0).wait_send()

        @pl.when(inner | plain)
        def _():
            pass_on(k.blocks.at[b2], b2, 0).wait_send()
            for c in range(4):
                pass_on(unit_of(b3, c), b3, c).wait_send()

        @pl.when(inner & jnp.logical_not(plain))
        def _():
            for c in range(4):
                sum_copy(5, c, outward).wait_send()

        @pl.when(jnp.logical_not(inner | plain))
        def _():
            for turn in range(8):
                lend(turn).wait_send()

        for s in range(n_r):
            own_drain(s)

        def lend_more(turns):
            @pl.when(index == 0)
            def _():
                lend_start(turns)

        prox(-1.0, smooth_x, functools.partial(lend_more, range(5, 7)))
        for d in range(n_r):
            s = (me_r + d) % n_r
            if d > 0:
                back_arrival(s)
            value = mixed_part(s, k.f_x, weight, nn).astype(bf16)
            for c in range(4):
                k.mixed[core, c, rows_of(s), :] = value[:, c * wide : (c + 1) * wide]
            mixed_copy(s).start()

        @pl.when(jnp.logical_not(inner))
        def _():
            for n in range(4):
                raw_copy(n).start()

        for d in range(n_r):
            mixed_arrival((me_r + d) % n_r).wait_recv()

        @pl.when(inner)
        def _():
            @pl.when(index == 0)
            def _():
                take_lent(0)

            sums_of_inner(index)

        @pl.when(jnp.logical_not(inner))
        def _():
            sums_of_end(index)

        prox_drain()
        for s in range(n_r):
            mixed_copy(s).wait_send()
        share = jnp.where(index == 0, weights[0] * (1.0 - weights[1]), weights[1])
        for s in range(n_r):
            add_best(k.xo_ref, s, share)

            @pl.when(index == 1)
            def _():
                out_copy(0, s).start()

        for n in range(4):
            k.grad[n] = partial(pair, n)
        for u in range(3):
            for n in members[u]:

                @pl.when(inner)
                def _():
                    k.grad[n] += sum_arrival(3, n)
                    k.grad[n] += sum_arrival(1, n)

                @pl.when(jnp.logical_not(inner))
                def _():
                    k.grad[n] += sum_arrival(2, n)

            finish(u)
        sums_drain(index)

        prox(1.0, smooth_y, functools.partial(lend_more, range(7, 8)))
        for d in range(n_r):
            s = (me_r + d) % n_r
            if d > 0:
                back_arrival(s)

            @pl.when(index == 0)
            def _():
                set_own(s, mixed_part(s, k.f_y, weight, nt))
                own_start(s)

            @pl.when(index == 1)
            def _():
                add_best(k.yo_ref, s, weights[1])
                out_copy(1, s).start()

        prox_drain()
        return 0

    lax.fori_loop(0, 2, step, 0)
    for i in range(2):
        for s in range(n_r):
            out_copy(i, s).wait()


def place_kernel(x_in, y_in, x_out, y_out):
    x_out[...] = x_in[...]
    y_out[...] = y_in[...]


def line_body(x_start, y_start, bucket_payoff, column_blocks, public_coef, predecessor_sequences):
    n_r = lax.axis_size("round")
    n_b = lax.axis_size("bucket")
    _, rows, seqs = x_start.shape
    half = seqs // 2
    part = rows // n_r
    pairs = n_b // 2
    f32, bf16, i16 = jnp.float32, jnp.bfloat16, jnp.int16
    vmem = pl.BlockSpec(memory_space=pltpu.VMEM)
    smem = pl.BlockSpec(memory_space=pltpu.SMEM)
    hbm = pl.BlockSpec(memory_space=pl.ANY)
    dma = pltpu.SemaphoreType.DMA
    scratch = dict(
        xv=pltpu.VMEM((1, rows, seqs), f32),
        yv=pltpu.VMEM((1, rows, seqs), f32),
        xo_ref=pltpu.VMEM((1, rows, seqs), f32),
        yo_ref=pltpu.VMEM((1, rows, seqs), f32),
        pay=pltpu.VMEM((1, rows, n_b * rows), bf16),
        pay_t=pltpu.VMEM((pairs, 2, rows, rows), bf16),
        pay_out=pltpu.VMEM((pairs, rows, rows), bf16),
        blocks=pltpu.VMEM((n_b, 4, rows, half // 2), bf16),
        mixed=pltpu.VMEM((4, 4, rows, half // 2), bf16),
        mixer=pltpu.VMEM((seqs, seqs), f32),
        mix_p=pltpu.VMEM((3, seqs, seqs), bf16),
        to_outer=pltpu.VMEM((seqs, seqs), bf16),
        gather=pltpu.VMEM((n_r - 1, seqs, half), bf16),
        spread=pltpu.VMEM((n_r - 1, half, seqs), bf16),
        f_x=pltpu.VMEM((rows, seqs), f32),
        f_y=pltpu.VMEM((rows, seqs), f32),
        grad=pltpu.VMEM((4, rows, half // 2), f32),
        work=pltpu.VMEM((rows, half // 2), f32),
        early=pltpu.VMEM((4, rows, half // 2), f32),
        lent=pltpu.VMEM((4, rows, rows), bf16),
        lent_t=pltpu.VMEM((2, 2, rows, rows), bf16),
        sum_out=pltpu.VMEM((6, 4, rows + 16, half // 2), i16),
        sum_in=pltpu.VMEM((6, 4, rows + 16, half // 2), i16),
        row_q=pltpu.VMEM((n_r, 4, part + 16, half // 2), i16),
        row_in=pltpu.VMEM((n_r, 4, part + 16, half // 2), i16),
        rows_f=pltpu.VMEM((n_r, 2, part, half), f32),
        share=pltpu.VMEM((n_r, 2, part, half), f32),
        back_q=pltpu.VMEM((n_r, 2, part, half), i16),
        back_in=pltpu.VMEM((n_r, 2, part, half), i16),
        sq_mine=pltpu.VMEM((8, 128), f32),
        sq_all=pltpu.VMEM((n_r * n_b, 1, 128), f32),
        load_sem=dma((3,)),
        out_sem=dma((2, n_r)),
        turn_send=dma((pairs,)),
        turn_recv=dma((pairs,)),
        ag_send=dma((3, n_r)),
        ag_recv=dma((n_b, n_r)),
        line_send=dma((n_b, n_r)),
        pass_send=dma((n_b, 4)),
        mx_send=dma((n_r,)),
        mx_recv=dma((2, n_r)),
        sum_send=dma((6, 4)),
        sum_recv=dma((6, 4)),
        lend_send=dma((8,)),
        lend_recv=dma((8,)),
        swap_send=dma((2,)),
        swap_recv=dma((2,)),
        raw_send=dma((4,)),
        raw_recv=dma((2, 4)),
        row_send=dma((n_r, 3)),
        row_recv=dma((n_r, 3)),
        back_send=dma((n_r, 2)),
        back_recv=dma((n_r, 2)),
        sq_send=dma((n_r * n_b,)),
        sq_recv=dma((n_r * n_b,)),
    )
    names = ["x_hbm", "y_hbm", "pay_hbm", "col_ref", "coef_ref", "pred_ref", "x_out", "y_out"]
    names += list(scratch)
    found = pl.pallas_call(
        functools.partial(line_kernel, names, n_r, n_b),
        out_shape=[jax.ShapeDtypeStruct(x_start.shape, f32)] * 2,
        in_specs=[hbm, hbm, hbm, smem, vmem, vmem],
        out_specs=[hbm, hbm],
        scratch_shapes=list(scratch.values()),
        compiler_params=pltpu.CompilerParams(
            collective_id=0, has_side_effects=True, vmem_limit_bytes=60 * 1024 * 1024
        ),
    )(
        x_start,
        y_start,
        bucket_payoff,
        jnp.transpose(column_blocks, (2, 0, 1)),
        public_coef,
        predecessor_sequences,
    )
    block = pl.BlockSpec((1, rows // 2, seqs), lambda i: (0, i, 0))
    return pl.pallas_call(
        place_kernel,
        grid=(2,),
        out_shape=[jax.ShapeDtypeStruct(x_start.shape, f32)] * 2,
        in_specs=[block, block],
        out_specs=[block, block],
    )(*found)


def plain_kernel(
    n_r,
    n_b,
    x_ref,
    y_ref,
    pay_ref,
    col_ref,
    coef_ref,
    pred_ref,
    xo_ref,
    yo_ref,
    xs,
    ys,
    mixer,
    gather,
    pay_t,
    blocks,
    mixed,
    grad,
    sib_out,
    sib_in,
    far_out,
    far_in,
    sq_b,
    sq_r,
    rows_in,
    score,
    norm,
    mass,
    back_in,
    far_q,
    far_s,
    far_q_in,
    far_s_in,
    row_q,
    row_s,
    row_q_in,
    row_s_in,
    back_q,
    back_s,
    back_q_in,
    back_s_in,
    ag_send,
    ag_recv,
    fw_send,
    line_send,
    sib_send,
    sib_recv,
    far_send,
    far_recv,
    sqb_send,
    sqb_recv,
    sqr_send,
    sqr_recv,
    row_send,
    row_recv,
    back_send,
    back_recv,
    far_s_send,
    far_s_recv,
    row_s_send,
    row_s_recv,
    back_s_send,
    back_s_recv,
):
    rows, seqs = xs.shape
    half = seqs // 2
    part = rows // n_r
    pairs = n_b // 2
    me_r = lax.axis_index("round")
    me_b = lax.axis_index("bucket")
    pair = me_b // 2
    core = me_b % 2
    sibling = pair * 2 + 1 - core
    total_count = n_r * n_b * rows * seqs

    def remote(src, dst, send, recv, **where):
        return pltpu.make_async_remote_copy(
            src_ref=src,
            dst_ref=dst,
            send_sem=send,
            recv_sem=recv,
            device_id=where,
            device_id_type=pl.DeviceIdType.MESH,
        )

    barrier = pltpu.get_barrier_semaphore()
    for d in range(1, n_b):
        pl.semaphore_signal(
            barrier,
            inc=1,
            device_id={"bucket": (me_b + d) % n_b},
            device_id_type=pl.DeviceIdType.MESH,
        )
    for d in range(1, n_r):
        pl.semaphore_signal(
            barrier,
            inc=1,
            device_id={"round": (me_r + d) % n_r},
            device_id_type=pl.DeviceIdType.MESH,
        )
    pl.semaphore_wait(barrier, n_b + n_r - 2)

    def order(i):
        return jnp.where(i < half, 2 * i, 2 * (i - half) + 1)

    down = lax.broadcasted_iota(jnp.int32, (seqs, seqs), 0)
    across = lax.broadcasted_iota(jnp.int32, (seqs, seqs), 1)
    to_inner = (down == order(across)).astype(jnp.float32)
    to_outer = (order(down) == across).astype(jnp.float32)

    tiles, per_row, tile, _ = coef_ref.shape[1:]
    for m in range(tiles):
        for c in range(tiles):
            value = jnp.zeros((tile, tile), jnp.float32)
            for t in range(per_row):
                value = value + jnp.where(col_ref[0, m, t] == c, coef_ref[0, m, t], 0.0)
            mixer[m * tile : (m + 1) * tile, c * tile : (c + 1) * tile] = value
    mixer[...] = exact(to_outer, exact(mixer[...], to_inner))
    ys[...] = exact(y_ref[0], to_inner)
    for r in range(n_r - 1):
        place = order(lax.broadcasted_iota(jnp.int32, (seqs, half), 0))
        gather[r] = (place == pred_ref[r : r + 1, :]).astype(jnp.float32)

    def columns(j):
        return pl.ds(pl.multiple_of(j * rows, rows), rows)

    def coded(value, code_ref, scale_ref):
        top = jnp.max(jnp.abs(value), axis=0, keepdims=True)
        unit = jnp.maximum(top, 1e-30) / 32767.0
        code = jnp.floor(value * (1.0 / unit) + 0.5)
        code_ref[...] = code.astype(jnp.int32).astype(jnp.int16)
        scale_ref[...] = jnp.broadcast_to(unit, scale_ref.shape)

    def decoded(code_ref, scale_ref):
        return code_ref[...].astype(jnp.int32).astype(jnp.float32) * scale_ref[0:1, :]

    def prox(state, sign, factor, weight, short):
        def row_copy(d):
            s = (me_r + d) % n_r
            here = grad.at[pl.ds(pl.multiple_of(s * part, part), part)]
            if not short:
                return [
                    remote(here, rows_in.at[me_r], row_send.at[s], row_recv.at[me_r], round=s)
                ]
            return [
                remote(
                    row_q.at[s], row_q_in.at[me_r], row_send.at[s], row_recv.at[me_r], round=s
                ),
                remote(
                    row_s.at[s], row_s_in.at[me_r], row_s_send.at[s], row_s_recv.at[me_r], round=s
                ),
            ]

        def row_arrival(d):
            s = (me_r + d) % n_r
            if not short:
                return [
                    remote(rows_in.at[s], rows_in.at[s], row_send.at[s], row_recv.at[s], round=s)
                ]
            return [
                remote(row_q_in.at[s], row_q_in.at[s], row_send.at[s], row_recv.at[s], round=s),
                remote(
                    row_s_in.at[s], row_s_in.at[s], row_s_send.at[s], row_s_recv.at[s], round=s
                ),
            ]

        for d in range(1, n_r):
            if short:
                s = (me_r + d) % n_r
                here = pl.ds(pl.multiple_of(s * part, part), part)
                coded(grad[here, :], row_q.at[s], row_s.at[s])
            for copy in row_copy(d):
                copy.start()
        squares = grad[...]
        squares = jnp.sum((squares * squares).reshape(rows // 8, 8, seqs), axis=0)
        squares = sum(squares[:, i * 128 : (i + 1) * 128] for i in range(seqs // 128))
        sq_b[me_b] = squares

        def sqb_copy(d):
            s = (me_b + d) % n_b
            return remote(
                sq_b.at[me_b], sq_b.at[me_b], sqb_send.at[d], sqb_recv.at[me_b], bucket=s
            )

        def sqb_arrival(d):
            s = (me_b + d) % n_b
            return remote(sq_b.at[s], sq_b.at[s], sqb_send.at[d], sqb_recv.at[s], bucket=s)

        for d in range(1, n_b):
            sqb_copy(d).start()
        rows_in[me_r] = grad[pl.ds(pl.multiple_of(me_r * part, part), part), :]
        for d in range(1, n_b):
            sqb_arrival(d).wait_recv()
        sq_r[me_r] = jnp.sum(sq_b[...], axis=0)

        def sqr_copy(d):
            s = (me_r + d) % n_r
            return remote(sq_r.at[me_r], sq_r.at[me_r], sqr_send.at[d], sqr_recv.at[me_r], round=s)

        def sqr_arrival(d):
            s = (me_r + d) % n_r
            return remote(sq_r.at[s], sq_r.at[s], sqr_send.at[d], sqr_recv.at[s], round=s)

        for d in range(1, n_r):
            sqr_copy(d).start()
        for d in range(1, n_r):
            sqr_arrival(d).wait_recv()
        squares = jnp.sum(jnp.sum(sq_r[...], axis=0), axis=0, keepdims=True)
        squares = jnp.sum(squares, axis=1, keepdims=True)
        scale = sign / (factor * jnp.sqrt(squares / total_count + epsilon))
        for d in range(1, n_r):
            for copy in row_arrival(d):
                copy.wait_recv()
            if short:
                s = (me_r + d) % n_r
                rows_in[s] = decoded(row_q_in.at[s], row_s_in.at[s])

        for r in reversed(range(n_r)):
            values = rows_in[r] * scale
            if r < n_r - 1:
                values = values + exact(norm[r + 1], gather[r], nt)
            score[r] = values
            even, odd = values[:, :half], values[:, half:]
            larger = jnp.maximum(even, odd)
            norm[r] = larger + jnp.log(jnp.exp(even - larger) + jnp.exp(odd - larger))

        def back_copy(r):
            if not short:
                return [
                    remote(
                        mass.at[r], back_in.at[me_r], back_send.at[r], back_recv.at[me_r], round=r
                    )
                ]
            return [
                remote(
                    back_q.at[r], back_q_in.at[me_r], back_send.at[r], back_recv.at[me_r], round=r
                ),
                remote(
                    back_s.at[r],
                    back_s_in.at[me_r],
                    back_s_send.at[r],
                    back_s_recv.at[me_r],
                    round=r,
                ),
            ]

        def back_arrival(s):
            if not short:
                return [
                    remote(
                        back_in.at[s], back_in.at[s], back_send.at[s], back_recv.at[s], round=s
                    )
                ]
            return [
                remote(
                    back_q_in.at[s], back_q_in.at[s], back_send.at[s], back_recv.at[s], round=s
                ),
                remote(
                    back_s_in.at[s], back_s_in.at[s], back_s_send.at[s], back_s_recv.at[s], round=s
                ),
            ]

        for r in range(n_r):
            even = jnp.exp(score[r, :, :half] - norm[r])
            odd = jnp.exp(score[r, :, half:] - norm[r])
            if r > 0:
                parent = exact(mass[r - 1], gather[r - 1])
                even = parent * even
                odd = parent * odd
            mass[r, :, :half] = even
            mass[r, :, half:] = odd

            @pl.when(me_r != r)
            def _():
                if short:
                    coded(mass[r], back_q.at[r], back_s.at[r])
                for copy in back_copy(r):
                    copy.start()

        def update(s, best):
            here = pl.ds(pl.multiple_of(s * part, part), part)
            state[here, :] = (1.0 - weight) * state[here, :] + weight * best

        update(me_r, mass[me_r])
        for d in range(1, n_r):
            s = (me_r + d) % n_r
            for copy in back_arrival(s):
                copy.wait_recv()
            if short:
                update(s, decoded(back_q_in.at[s], back_s_in.at[s]))
            else:
                update(s, back_in[s])
        for d in range(1, n_r):
            for copy in row_copy(d) + back_copy((me_r + d) % n_r):
                copy.wait_send()
            sqr_copy(d).wait_send()
        for d in range(1, n_b):
            sqb_copy(d).wait_send()

    def step(index, _):
        weight = 2.0 / (index.astype(jnp.float32) + 3.0)
        short = False

        blocks[me_b] = exact(ys[...], mixer[...], nt).astype(jnp.bfloat16)

        def own_copy(kind):
            target = (sibling, me_b + 2, me_b - 2)[kind]
            return remote(
                blocks.at[me_b], blocks.at[me_b], ag_send.at[kind], ag_recv.at[me_b], bucket=target
            )

        def go_on(b, d, step):
            return remote(
                blocks.at[b], blocks.at[b], line_send.at[d], ag_recv.at[b], bucket=me_b + step
            )

        def pass_on(b, d):
            return remote(blocks.at[b], blocks.at[b], fw_send.at[d], ag_recv.at[b], bucket=sibling)

        def arrival(b):
            return remote(
                blocks.at[b], blocks.at[b], ag_send.at[0], ag_recv.at[b], bucket=sibling
            )

        def product(b):
            return jnp.dot(
                pay_ref[0, :, columns(b)], blocks[b], preferred_element_type=jnp.float32
            )

        @pl.when(pair < pairs - 1)
        def _():
            own_copy(1).start()

        @pl.when(pair > 0)
        def _():
            own_copy(2).start()

        own_copy(0).start()
        @pl.when(index == 0)
        def _():
            xs[...] = exact(x_ref[0], to_inner)

            def turn(j, _):
                pay_t[columns(j), :] = pay_ref[0, :, columns(j)].T
                return 0

            lax.fori_loop(0, n_b, turn, 0)
        grad[...] = product(me_b)
        arrival(sibling).wait_recv()
        grad[...] += product(sibling)

        def take(d, _):
            left = me_b - 2 * d
            right = me_b + 2 * d

            @pl.when(pair >= d)
            def _():
                arrival(left).wait_recv()

                @pl.when(pair < pairs - 1)
                def _():
                    go_on(left, d, 2).start()

                pass_on(left, d).start()

            @pl.when(pair + d < pairs)
            def _():
                arrival(right).wait_recv()

                @pl.when(pair > 0)
                def _():
                    go_on(right, pairs + d, -2).start()

                pass_on(right, pairs + d).start()

            def use(b, other):
                grad[...] += product(b)
                arrival(other).wait_recv()
                grad[...] += product(other)

            @pl.when(pair >= d)
            def _():
                use(left, sibling - 2 * d)

            @pl.when(pair + d < pairs)
            def _():
                use(right, sibling + 2 * d)

            return 0

        lax.fori_loop(1, pairs, take, 0)

        def drain(d, _):
            left = me_b - 2 * d
            right = me_b + 2 * d

            @pl.when(pair >= d)
            def _():
                pass_on(left, d).wait_send()

                @pl.when(pair < pairs - 1)
                def _():
                    go_on(left, d, 2).wait_send()

            @pl.when(pair + d < pairs)
            def _():
                pass_on(right, pairs + d).wait_send()

                @pl.when(pair > 0)
                def _():
                    go_on(right, pairs + d, -2).wait_send()

            return 0

        lax.fori_loop(1, pairs, drain, 0)
        own_copy(0).wait_send()

        @pl.when(pair < pairs - 1)
        def _():
            own_copy(1).wait_send()

        @pl.when(pair > 0)
        def _():
            own_copy(2).wait_send()

        prox(xs, -1.0, smooth_x, weight, short)

        mixed[...] = exact(xs[...], mixer[...]).astype(jnp.bfloat16)

        def partial(b):
            return jnp.dot(pay_t[columns(b), :], mixed[...], preferred_element_type=jnp.float32)

        def sib_copy(q):
            return remote(
                sib_out.at[q], sib_in.at[q], sib_send.at[q], sib_recv.at[q], bucket=sibling
            )

        def far_copy(q, step, target):
            slot = q if step > 0 else pairs + q
            if not short:
                return [
                    remote(
                        far_out.at[q],
                        far_in.at[slot],
                        far_send.at[q],
                        far_recv.at[slot],
                        bucket=target,
                    )
                ]
            return [
                remote(
                    far_q.at[q],
                    far_q_in.at[slot],
                    far_send.at[q],
                    far_recv.at[slot],
                    bucket=target,
                ),
                remote(
                    far_s.at[q],
                    far_s_in.at[slot],
                    far_s_send.at[q],
                    far_s_recv.at[slot],
                    bucket=target,
                ),
            ]

        def far_value(q, step):
            slot = q if step > 0 else pairs + q
            for copy in far_copy(q, step, sibling):
                copy.wait_recv()
            if short:
                return decoded(far_q_in.at[slot], far_s_in.at[slot])
            return far_in[slot]

        def to_sibling(q):
            sib_out[q] = partial(q * 2 + 1 - core)
            sib_copy(q).start()

        def move(q, step):
            far_out[q] = partial(q * 2 + core)
            sib_copy(q).wait_recv()
            far_out[q] += sib_in[q]

            @pl.when(pair > 0 if step > 0 else pair < pairs - 1)
            def _():
                far_out[q] += far_value(q, step)

            if short:
                coded(far_out[q], far_q.at[q], far_s.at[q])
            for copy in far_copy(q, step, me_b + step):
                copy.start()

        def outward(right, left):
            def one(i, _):
                @pl.when(pair < pairs - 1 - i)
                def _():
                    right(pairs - 1 - i)

                @pl.when(pair > i)
                def _():
                    left(i)

                return 0

            lax.fori_loop(0, pairs - 1, one, 0)

        def far_done(q, step):
            for copy in far_copy(q, step, me_b + step):
                copy.wait_send()

        outward(to_sibling, to_sibling)
        outward(lambda q: move(q, 2), lambda q: move(q, -2))
        to_sibling(pair)
        grad[...] = partial(me_b)
        sib_copy(pair).wait_recv()
        grad[...] += sib_in[pair]

        @pl.when(pair > 0)
        def _():
            grad[...] += far_value(pair, 2)

        @pl.when(pair < pairs - 1)
        def _():
            grad[...] += far_value(pair, -2)

        outward(lambda q: far_done(q, 2), lambda q: far_done(q, -2))
        for q in range(pairs):
            sib_copy(q).wait_send()
        prox(ys, 1.0, smooth_y, weight, short)
        return 0

    lax.fori_loop(0, 2, step, 0)
    down = lax.broadcasted_iota(jnp.int32, (seqs, seqs), 0)
    across = lax.broadcasted_iota(jnp.int32, (seqs, seqs), 1)
    to_outer = (order(down) == across).astype(jnp.float32)
    xo_ref[0] = exact(xs[...], to_outer)
    yo_ref[0] = exact(ys[...], to_outer)


def plain_body(x_start, y_start, bucket_payoff, column_blocks, public_coef, predecessor_sequences):
    n_r = lax.axis_size("round")
    n_b = lax.axis_size("bucket")
    _, rows, seqs = x_start.shape
    part = rows // n_r
    pairs = n_b // 2
    f32, bf16 = jnp.float32, jnp.bfloat16
    vmem = pl.BlockSpec(memory_space=pltpu.VMEM)
    smem = pl.BlockSpec(memory_space=pltpu.SMEM)
    dma = pltpu.SemaphoreType.DMA
    return pl.pallas_call(
        functools.partial(plain_kernel, n_r, n_b),
        out_shape=[jax.ShapeDtypeStruct(x_start.shape, f32)] * 2,
        in_specs=[vmem, vmem, vmem, smem, vmem, vmem],
        out_specs=[vmem, vmem],
        scratch_shapes=[
            pltpu.VMEM((rows, seqs), f32),
            pltpu.VMEM((rows, seqs), f32),
            pltpu.VMEM((seqs, seqs), f32),
            pltpu.VMEM((n_r - 1, seqs, seqs // 2), f32),
            pltpu.VMEM((n_b * rows, rows), bf16),
            pltpu.VMEM((n_b, rows, seqs), bf16),
            pltpu.VMEM((rows, seqs), bf16),
            pltpu.VMEM((rows, seqs), f32),
            pltpu.VMEM((pairs, rows, seqs), f32),
            pltpu.VMEM((pairs, rows, seqs), f32),
            pltpu.VMEM((pairs, rows, seqs), f32),
            pltpu.VMEM((2 * pairs, rows, seqs), f32),
            pltpu.VMEM((n_b, 8, 128), f32),
            pltpu.VMEM((n_r, 8, 128), f32),
            pltpu.VMEM((n_r, part, seqs), f32),
            pltpu.VMEM((n_r, part, seqs), f32),
            pltpu.VMEM((n_r, part, seqs // 2), f32),
            pltpu.VMEM((n_r, part, seqs), f32),
            pltpu.VMEM((n_r, part, seqs), f32),
            pltpu.VMEM((16, 128), jnp.int16),
            pltpu.VMEM((pairs, 8, seqs), f32),
            pltpu.VMEM((16, 128), jnp.int16),
            pltpu.VMEM((2 * pairs, 8, seqs), f32),
            pltpu.VMEM((16, 128), jnp.int16),
            pltpu.VMEM((n_r, 8, seqs), f32),
            pltpu.VMEM((16, 128), jnp.int16),
            pltpu.VMEM((n_r, 8, seqs), f32),
            pltpu.VMEM((16, 128), jnp.int16),
            pltpu.VMEM((n_r, 8, seqs), f32),
            pltpu.VMEM((16, 128), jnp.int16),
            pltpu.VMEM((n_r, 8, seqs), f32),
            dma((3,)),
            dma((n_b,)),
            dma((2 * pairs,)),
            dma((2 * pairs,)),
            dma((pairs,)),
            dma((pairs,)),
            dma((pairs,)),
            dma((2 * pairs,)),
            dma((n_b,)),
            dma((n_b,)),
            dma((n_r,)),
            dma((n_r,)),
            dma((n_r,)),
            dma((n_r,)),
            dma((n_r,)),
            dma((n_r,)),
            dma((pairs,)),
            dma((2 * pairs,)),
            dma((n_r,)),
            dma((n_r,)),
            dma((n_r,)),
            dma((n_r,)),
        ],
        compiler_params=pltpu.CompilerParams(
            collective_id=0, has_side_effects=True, vmem_limit_bytes=60 * 1024 * 1024
        ),
    )(x_start, y_start, bucket_payoff, column_blocks, public_coef, predecessor_sequences)


def solution(mesh):
    in_specs = (
        P("round", "bucket", None),
        P("round", "bucket", None),
        P("round", "bucket", None),
        P("round", None, None),
        P("round", None, None, None, None),
        P(),
    )
    out_specs = (P("round", "bucket", None), P("round", "bucket", None))

    line = mesh.shape["round"] == 4 and mesh.shape["bucket"] == 8

    def run(*arrays):
        return tuple(
            jax.shard_map(
                line_body if line else plain_body, mesh=mesh, in_specs=in_specs, out_specs=out_specs, check_vma=False
            )(*arrays)
        )

    return run
```

```python
import functools
import types

import jax
import jax.numpy as jnp
from jax import lax
from jax.experimental import pallas as pl
from jax.experimental.pallas import tpu as pltpu
from jax.sharding import PartitionSpec as P

smooth_x = 0.1
smooth_y = 0.1
epsilon = 1e-06
highest = lax.Precision.HIGHEST
nn = (((1,), (0,)), ((), ()))
nt = (((1,), (1,)), ((), ()))


def exact(a, b, dims=nn):
    return lax.dot_general(a, b, dims, precision=highest, preferred_element_type=jnp.float32)


weights = (2.0 / 3.0, 2.0 / 4.0)
top_code = 65535.0
shift_code = 32768


def split3(value):
    hi = value.astype(jnp.bfloat16)
    left = value - hi.astype(jnp.float32)
    mid = left.astype(jnp.bfloat16)
    lo = (left - mid.astype(jnp.float32)).astype(jnp.bfloat16)
    return [hi, mid, lo]


def dot(a, b, dims=nn):
    return lax.dot_general(a, b, dims, preferred_element_type=jnp.float32)


def picked(parts, one_hot, dims=nn):
    size = parts[0].shape[0]
    out = dot(jnp.concatenate(parts, axis=0), one_hot, dims)
    return sum(out[i * size : (i + 1) * size] for i in range(len(parts)))


def mix(parts, factors, dims):
    size = parts[0].shape[0]
    total = None
    for i, factor in reversed(list(enumerate(factors))):
        count = min(len(parts), 3 - i)
        out = dot(jnp.concatenate(parts[:count], axis=0), factor, dims)
        for j in reversed(range(count)):
            term = out[j * size : (j + 1) * size]
            total = term if total is None else total + term
    return total


def encode(value, code_ref):
    if len(code_ref.shape) == 3:
        wide = code_ref.shape[2]
        for i in range(code_ref.shape[0]):
            encode(value[:, i * wide : (i + 1) * wide], code_ref.at[i])
        return
    rows = value.shape[0]
    top = jnp.maximum(jnp.max(jnp.abs(value), axis=0, keepdims=True), 1e-30)
    power = jnp.floor(256.0 * jnp.log2(top * (1.0 / 32767.0))) + 1.0
    code = jnp.floor(value * jnp.exp2(power * (-1.0 / 256.0)) + 0.5)
    code_ref[:rows, :] = code.astype(jnp.int32).astype(jnp.int16)
    power = jnp.broadcast_to(power, (16, value.shape[1]))
    code_ref[rows:, :] = power.astype(jnp.int32).astype(jnp.int16)


def decode(code_ref):
    if len(code_ref.shape) == 3:
        return jnp.concatenate([decode(code_ref.at[i]) for i in range(code_ref.shape[0])], axis=1)
    rows = code_ref.shape[0] - 16
    power = code_ref[rows:, :].astype(jnp.int32).astype(jnp.float32)[0:1, :]
    unit = jnp.exp2(power * (1.0 / 256.0))
    return code_ref[:rows, :].astype(jnp.int32).astype(jnp.float32) * unit


def line_kernel(names, n_r, n_b, *refs):
    k = types.SimpleNamespace(**dict(zip(names, refs)))
    f32, bf16 = jnp.float32, jnp.bfloat16
    _, rows, seqs = k.x_hbm.shape
    half = seqs // 2
    wide = half // 2
    part = rows // n_r
    pairs = n_b // 2
    me_r = lax.axis_index("round")
    me_b = lax.axis_index("bucket")
    pair = me_b // 2
    core = me_b % 2
    sibling = pair * 2 + 1 - core
    spans = ((0, slice(0, half)), (1, slice(0, wide)), (1, slice(wide, half)))
    quarters = (slice(0, 2), slice(2, 3), slice(3, 4))
    members = ((0, 1), (2,), (3,))
    outward = jnp.where(pair < pairs // 2, -2, 2)
    end_chip = jnp.where(pair < pairs // 2, 0, pairs - 1)
    facing = pair - outward // 2
    far_end = pairs - 1 - end_chip
    inner = (pair > 0) & (pair < pairs - 1)
    total_count = n_r * n_b * rows * seqs

    def remote(src, dst, send, recv, **where):
        return pltpu.make_async_remote_copy(
            src_ref=src,
            dst_ref=dst,
            send_sem=send,
            recv_sem=recv,
            device_id=where,
            device_id_type=pl.DeviceIdType.MESH,
        )

    load_y = pltpu.make_async_copy(k.y_hbm, k.yv, k.load_sem.at[0])
    load_pay = pltpu.make_async_copy(k.pay_hbm, k.pay, k.load_sem.at[1])
    load_x = pltpu.make_async_copy(k.x_hbm, k.xv, k.load_sem.at[2])
    load_y.start()
    load_pay.start()
    load_x.start()

    barrier = pltpu.get_barrier_semaphore()
    for dr in range(n_r):
        for db in range(n_b):
            if dr or db:
                pl.semaphore_signal(
                    barrier,
                    inc=1,
                    device_id={"round": (me_r + dr) % n_r, "bucket": (me_b + db) % n_b},
                    device_id_type=pl.DeviceIdType.MESH,
                )

    def order(i):
        return 2 * (i // half * wide + i % wide) + (i % half) // wide

    down = lax.broadcasted_iota(jnp.int32, (seqs, seqs), 0)
    across = lax.broadcasted_iota(jnp.int32, (seqs, seqs), 1)
    k.to_outer[...] = (order(down) == across).astype(f32).astype(bf16)

    tiles, per_row, tile, _ = k.coef_ref.shape[1:]
    for m in range(tiles):
        for c in range(tiles):
            value = jnp.zeros((tile, tile), f32)
            for t in range(per_row):
                value = value + jnp.where(k.col_ref[t, 0, m] == c, k.coef_ref[0, m, t], 0.0)
            k.mixer[m * tile : (m + 1) * tile, c * tile : (c + 1) * tile] = value
    for i, piece in enumerate(split3(k.mixer[...])):
        k.mix_p[i] = dot(k.to_outer[...], piece).astype(bf16)

    def rows_of(s):
        return pl.ds(pl.multiple_of(s * part, part), part)

    def columns(j):
        return pl.ds(pl.multiple_of(j * rows, rows), rows)

    away = jnp.where(pair < pairs // 2, pairs // 2, 0)

    def lent_place(o):
        return (far_end - away, 1 - (far_end - away))[o]

    def lend(turn):
        o, i, p = turn // 4, turn // 2 % 2, turn % 2
        here = pl.ds(p * (rows // 2), rows // 2)
        b = 2 * lent_place(o) + i
        return remote(
            k.pay.at[0, here, columns(2 * away + b)],
            k.lent.at[b, here],
            k.lend_send.at[turn],
            k.lend_recv.at[turn],
            bucket=me_b - outward,
        )

    def lend_start(turns):
        @pl.when(jnp.logical_not(inner))
        def _():
            for turn in turns:
                lend(turn).start()

    def lent_swap(j, o):
        return remote(
            k.pay_out.at[j],
            k.lent_t.at[j, core],
            k.swap_send.at[o],
            k.swap_recv.at[o],
            bucket=sibling,
        )

    def wait_lent(o):
        j = lent_place(o)
        for i in range(2):
            for p in range(2):
                here = k.lent.at[2 * j + i, pl.ds(p * (rows // 2), rows // 2)]
                turn = 4 * o + 2 * i + p
                remote(
                    here, here, k.lend_send.at[turn], k.lend_recv.at[turn], bucket=sibling
                ).wait_recv()

    def turn_lent(o):
        j = lent_place(o)
        k.pay_out[j] = k.lent[2 * j + 1 - core].T
        lent_swap(j, o).start()
        k.lent_t[j, core] = k.lent[2 * j + core].T
        lent_swap(j, o).wait()


    def own_copy(kind, s):
        target = (sibling, me_b + 2, me_b - 2)[kind]
        here = k.blocks.at[me_b, :, rows_of(s), :]
        return remote(here, here, k.ag_send.at[kind, s], k.ag_recv.at[me_b, s], bucket=target)

    def own_start(s):
        @pl.when(pair < pairs - 1)
        def _():
            own_copy(1, s).start()

        @pl.when(pair > 0)
        def _():
            own_copy(2, s).start()

        own_copy(0, s).start()

    def own_drain(s):
        @pl.when(pair < pairs - 1)
        def _():
            own_copy(1, s).wait_send()

        @pl.when(pair > 0)
        def _():
            own_copy(2, s).wait_send()

        own_copy(0, s).wait_send()

    def set_own(s, value):
        value = value.astype(bf16)
        for c in range(4):
            k.blocks[me_b, c, rows_of(s), :] = value[:, c * wide : (c + 1) * wide]

    pl.semaphore_wait(barrier, n_b * n_r - 1)
    load_y.wait()
    load_pay.wait()
    lend_start(range(1))
    for s in range(n_r):
        value = mix(split3(k.yv[0, rows_of(s), :]), [k.mix_p[i] for i in range(3)], nt)
        k.f_y[rows_of(s), :] = value
        set_own(s, value)
        own_start(s)

    def part_of(b, s):
        return k.blocks.at[b, :, rows_of(s), :]

    def unit_of(b, c):
        return k.blocks.at[b, c]

    def block(b, u):
        return jnp.concatenate([k.blocks[b, c] for c in members[u]], axis=1)

    def by_parts(b):
        for s in range(n_r):
            arrived(part_of(b, s), b, s)

    def by_whole(b):
        arrived(k.blocks.at[b], b, 0)

    def by_unit(b, c):
        arrived(unit_of(b, c), b, c)

    def arrived(here, b, i):
        remote(here, here, k.ag_send.at[0, 0], k.ag_recv.at[b, i], bucket=sibling).wait_recv()

    def go_on(here, b, i, step):
        return remote(here, here, k.line_send.at[b, i], k.ag_recv.at[b, i], bucket=me_b + step)

    def pass_on(here, b, i):
        return remote(here, here, k.pass_send.at[b, i], k.ag_recv.at[b, i], bucket=sibling)

    def add_product(b, u):
        value = dot(k.pay[0, :, columns(b)], block(b, u))
        for i, c in enumerate(members[u]):
            k.grad[c] += value[:, i * wide : (i + 1) * wide]

    def lent_product(b, c):
        return dot(k.lent[b - 2 * away], k.blocks[b, c])

    def setup():
        lend_start(range(1, 5))


        def turn(q, _):
            k.pay_out[q] = k.pay[0, :, columns(q * 2 + 1 - core)].T
            turned(q).start()
            k.pay_t[q, core] = k.pay[0, :, columns(q * 2 + core)].T
            return 0

        lax.fori_loop(0, pairs, turn, 0)
        for r in range(n_r - 1):
            place = order(lax.broadcasted_iota(jnp.int32, (seqs, half), 0))
            one_hot = (place == k.pred_ref[r : r + 1, :]).astype(f32).astype(bf16)
            k.gather[r] = one_hot
            k.spread[r] = one_hot.T

        @pl.when(me_r == 0)
        def _():
            for s in range(n_r):
                k.back_in[s, 1] = jnp.full((part, half), 65535 - shift_code, jnp.int32).astype(
                    jnp.int16
                )

        load_x.wait()
        value = picked(split3(exact(k.xv[0], k.mixer[...])), k.to_outer[...], nt)
        k.f_x[...] = value
        for i in range(3):
            k.mix_p[i] = dot(k.mix_p[i], k.to_outer[...], nt).astype(bf16)

    def turned(q):
        return remote(
            k.pay_out.at[q],
            k.pay_t.at[q, core],
            k.turn_send.at[q],
            k.turn_recv.at[q],
            bucket=sibling,
        )


    def row_copy(d, u):
        s = (me_r + d) % n_r
        return remote(
            k.row_q.at[s, quarters[u]],
            k.row_in.at[me_r, quarters[u]],
            k.row_send.at[s, u],
            k.row_recv.at[me_r, u],
            round=s,
        )

    def row_arrival(d, u):
        s = (me_r + d) % n_r
        h, lanes = spans[u]
        here = k.row_in.at[s, quarters[u]]
        remote(here, here, k.row_send.at[s, u], k.row_recv.at[s, u], round=s).wait_recv()
        k.rows_f[s, h, :, lanes] = decode(here)

    def finish(u):
        for c in members[u]:
            squares = k.grad[c]
            squares = jnp.sum((squares * squares).reshape(rows // 8, 8, wide), axis=0)
            if c == 0:
                k.sq_mine[...] = squares
            else:
                k.sq_mine[...] += squares
        if u == 2:
            k.sq_all[me] = jnp.sum(k.sq_mine[...], axis=0, keepdims=True)
            for dr, db in others:
                square_copy(dr, db).start()
        for d in range(1, n_r):
            s = (me_r + d) % n_r
            for c in members[u]:
                encode(k.grad[c, rows_of(s), :], k.row_q.at[s, c])
            row_copy(d, u).start()
        for c in members[u]:
            h, lanes = c // 2, slice(c % 2 * wide, c % 2 * wide + wide)
            k.rows_f[me_r, h, :, lanes] = k.grad[c, rows_of(me_r), :]

    me = me_r * n_b + me_b

    def square_copy(dr, db):
        here = k.sq_all.at[me]
        return remote(
            here,
            here,
            k.sq_send.at[dr * n_b + db],
            k.sq_recv.at[me],
            round=(me_r + dr) % n_r,
            bucket=(me_b + db) % n_b,
        )

    def square_arrival(dr, db):
        s = (me_r + dr) % n_r * n_b + (me_b + db) % n_b
        here = k.sq_all.at[s]
        return remote(here, here, k.sq_send.at[0], k.sq_recv.at[s], bucket=sibling)

    others = [(dr, db) for dr in range(n_r) for db in range(n_b) if dr or db]

    def back_copy(r, i):
        return remote(
            k.back_q.at[r, i],
            k.back_in.at[me_r, i],
            k.back_send.at[r, i],
            k.back_recv.at[me_r, i],
            round=r,
        )

    def back_arrival(s):
        for i in range(2):

            def wait():
                here = k.back_in.at[s, i]
                remote(
                    here, here, k.back_send.at[s, i], k.back_recv.at[s, i], round=s
                ).wait_recv()

            if i == 0:
                wait()
            else:
                pl.when(me_r > 0)(wait)

    def back_drain(s):
        back_copy(s, 0).wait_send()

        @pl.when(s > 0)
        def _():
            back_copy(s, 1).wait_send()

    def give_back(r, i, value):
        code = jnp.floor(value * top_code + 0.5).astype(jnp.int32) - shift_code
        k.back_q[r, i] = code.astype(jnp.int16)

        @pl.when(me_r != r)
        def _():
            back_copy(r, i).start()

        @pl.when(me_r == r)
        def _():
            k.back_in[me_r, i] = k.back_q[r, i]

    def prox(sign, factor, after_scale=None):
        for u in range(2):
            for d in range(1, n_r):
                row_arrival(d, u)
        for d in range(1, n_r):
            row_arrival(d, 2)
        for dr, db in others:
            square_arrival(dr, db).wait_recv()
        squares = jnp.sum(k.sq_all[...], axis=0)
        squares = jnp.sum(squares, axis=1, keepdims=True)
        scale = sign / (factor * jnp.sqrt(squares / total_count + epsilon))

        if after_scale is not None:
            after_scale()
        carried = None
        for r in reversed(range(n_r)):
            norms = []
            evens = []
            for h in range(2):
                values = k.rows_f[r, h] * scale
                if carried is not None:
                    values = values + carried[:, h * half : (h + 1) * half]
                even, odd = values[:, :wide], values[:, wide:]
                small = jnp.exp(-jnp.abs(even - odd))
                larger = 1.0 / (1.0 + small)
                smaller = small * larger
                ahead = even >= odd
                evens.append(jnp.where(ahead, larger, smaller))
                k.share[r, h, :, :wide] = evens[h]
                k.share[r, h, :, wide:] = jnp.where(ahead, smaller, larger)
                norms.append(jnp.maximum(even, odd) + jnp.log(1.0 + small))
            give_back(r, 0, jnp.concatenate(evens, axis=1))
            if r > 0:
                norm = jnp.concatenate(norms, axis=1)
                carried = picked(split3(norm), k.spread[r - 1])

        mass = jnp.concatenate([k.share[0, 0], k.share[0, 1]], axis=1)
        for r in range(1, n_r):
            parent = picked(split3(mass), k.gather[r - 1])
            give_back(r, 1, parent)
            above = [parent[:, h * wide : (h + 1) * wide] for h in (0, 0, 1, 1)]
            shares = jnp.concatenate([k.share[r, 0], k.share[r, 1]], axis=1)
            mass = shares * jnp.concatenate(above, axis=1)

    def prox_drain():
        for d in range(1, n_r):
            for u in range(3):
                row_copy(d, u).wait_send()
            back_drain((me_r + d) % n_r)
        for dr, db in others:
            square_copy(dr, db).wait_send()

    def pieces(s):
        share, parent = [
            (k.back_in[s, i].astype(jnp.int32) + shift_code).astype(f32) * (1.0 / top_code)
            for i in range(2)
        ]
        even = parent * share
        odd = parent - even
        both = (even[:, :wide], odd[:, :wide], even[:, wide:], odd[:, wide:])
        whole = jnp.concatenate(both, axis=1)
        return split3(whole)[:2]

    def mixed_part(s, state, weight, dims):
        value = mix(pieces(s), [k.mix_p[i] for i in range(3)], dims)
        value = (1.0 - weight) * state[rows_of(s), :] + weight * value
        state[rows_of(s), :] = value
        return value

    def add_best(out, s, share):
        best = picked(pieces(s), k.to_outer[...])
        out[0, rows_of(s), :] += share * best


    def mixed_copy(s):
        here = k.mixed.at[core, :, rows_of(s), :]
        return remote(here, here, k.mx_send.at[s], k.mx_recv.at[core, s], bucket=sibling)

    def mixed_arrival(s):
        here = k.mixed.at[1 - core, :, rows_of(s), :]
        return remote(here, here, k.mx_send.at[s], k.mx_recv.at[1 - core, s], bucket=sibling)

    def raw_copy(n):
        return remote(
            k.mixed.at[core, n],
            k.mixed.at[2 + core, n],
            k.raw_send.at[n],
            k.raw_recv.at[core, n],
            bucket=me_b - outward,
        )

    def raw_pass(n):
        here = k.mixed.at[2 + core, n]
        return remote(here, here, k.raw_send.at[n], k.raw_recv.at[core, n], bucket=sibling)

    def raw_arrival(source, n):
        here = k.mixed.at[2 + source, n]
        remote(
            here, here, k.raw_send.at[n], k.raw_recv.at[source, n], bucket=sibling
        ).wait_recv()

    def partial(q, n):
        return dot(k.pay_t[q, 0], k.mixed[0, n]) + dot(k.pay_t[q, 1], k.mixed[1, n])

    def lent_partial(j, n):
        return dot(k.lent_t[j, 0], k.mixed[2, n]) + dot(k.lent_t[j, 1], k.mixed[3, n])

    def sum_copy(kind, n, step):
        return remote(
            k.sum_out.at[kind, n],
            k.sum_in.at[kind, n],
            k.sum_send.at[kind, n],
            k.sum_recv.at[kind, n],
            bucket=me_b + step,
        )

    def sum_arrival(kind, n):
        here = k.sum_in.at[kind, n]
        remote(
            here, here, k.sum_send.at[kind, n], k.sum_recv.at[kind, n], bucket=sibling
        ).wait_recv()
        return decode(here)

    def sums_of_end(index):
        def lend_sum(n, _):
            k.work[...] = partial(facing - outward // 2, n)
            encode(k.work[...], k.sum_out.at[4, n])
            sum_copy(4, n, -outward).start()
            return 0

        @pl.when(index == 0)
        def _():
            lax.fori_loop(0, 4, lend_sum, 0)

        def give(n, _):
            k.work[...] = partial(facing, n)
            encode(k.work[...], k.sum_out.at[3, n])
            sum_copy(3, n, -outward).start()
            return 0

        lax.fori_loop(0, 4, give, 0)

    def sums_of_inner(index):
        def give(i, _):
            n = i % 4

            @pl.when(i < 4)
            def _():
                raw_arrival(core, n)
                raw_pass(n).start()

            q = jnp.where(i < 4, far_end, facing)
            k.work[...] = partial(q, n)

            @pl.when(i < 4)
            def _():
                raw_arrival(1 - core, n)

            @pl.when((i < 4) | (index == 1))
            def _():
                k.work[...] += lent_partial(q - away, n)

            @pl.when((i >= 4) & (index == 0))
            def _():
                k.work[...] += sum_arrival(4, n)

            encode(k.work[...], k.sum_out.at[i // 4, n])
            sum_copy(i // 4, n, -outward).start()

            @pl.when((i >= 2) & (i < 6))
            def _():
                k.work[...] = partial(end_chip, i - 2)
                k.work[...] += sum_arrival(0, i - 2)
                encode(k.work[...], k.sum_out.at[2, i - 2])
                sum_copy(2, i - 2, outward).start()

            return 0

        lax.fori_loop(0, 8, give, 0)

    def sums_drain(index):
        @pl.when(inner)
        def _():
            for n in range(4):
                raw_pass(n).wait_send()
                sum_copy(0, n, -outward).wait_send()
                sum_copy(1, n, -outward).wait_send()
                sum_copy(2, n, outward).wait_send()

        @pl.when(jnp.logical_not(inner))
        def _():
            for n in range(4):
                raw_copy(n).wait_send()
                sum_copy(3, n, -outward).wait_send()

                @pl.when(index == 0)
                def _():
                    sum_copy(4, n, -outward).wait_send()

    def out_copy(i, s):
        here, there = ((k.xo_ref, k.x_out), (k.yo_ref, k.y_out))[i]
        return pltpu.make_async_copy(
            here.at[:, rows_of(s)], there.at[:, rows_of(s)], k.out_sem.at[i, s]
        )

    def step(index, _):
        weight = 2.0 / (index.astype(f32) + 3.0)

        @pl.when(index == 0)
        def _():
            setup()

        first = -outward
        second = jnp.where(inner, outward, -2 * outward)
        far = jnp.where(inner, -2 * outward, -3 * outward)

        for u in range(3):
            value = dot(k.pay[0, :, columns(me_b)], block(me_b, u))
            for i, c in enumerate(members[u]):
                k.grad[c] = value[:, i * wide : (i + 1) * wide]
        by_parts(sibling)
        for u in range(2 + 1):
            add_product(sibling, u)

        @pl.when(index == 0)
        def _():
            for q in range(pairs):
                turned(q).wait()
            k.xo_ref[...] = (1.0 - weights[0]) * (1.0 - weights[1]) * k.xv[...]
            k.yo_ref[...] = (1.0 - weights[0]) * (1.0 - weights[1]) * k.yv[...]

        @pl.when(index == 1)
        def _():
            for s in range(n_r):
                add_best(k.yo_ref, s, weights[0] * (1.0 - weights[1]))

        def both(offset):
            for u in range(3):
                add_product(me_b + offset, u)
            by_whole(sibling + offset)
            for u in range(3):
                add_product(sibling + offset, u)

        plain = index == 0
        b = me_b + first
        for s in range(n_r):
            arrived(part_of(b, s), b, s)

            @pl.when(inner & plain)
            def _():
                go_on(part_of(b, s), b, s, outward).start()

        pass_on(k.blocks.at[b], b, 0).start()
        b2 = me_b + second

        @pl.when(inner)
        def _():
            by_parts(b2)
            for c in range(4):
                go_on(unit_of(b2, c), b2, c, -outward).start()
            pass_on(k.blocks.at[b2], b2, 0).start()

        both(first)

        @pl.when(inner & jnp.logical_not(plain))
        def _():
            wait_lent(1)
            for c in range(4):
                k.early[c] = lent_product(b, c) + lent_product(sibling + first, c)

        @pl.when(jnp.logical_not(inner) & plain)
        def _():
            by_parts(b2)
            pass_on(k.blocks.at[b2], b2, 0).start()

        @pl.when(inner | plain)
        def _():
            both(second)

        b3 = me_b + far
        for c in range(4):

            @pl.when(inner | plain)
            def _():
                by_unit(b3, c)

                @pl.when(inner & plain)
                def _():
                    go_on(unit_of(b3, c), b3, c, outward).start()

                pass_on(unit_of(b3, c), b3, c).start()

                @pl.when(plain)
                def _():
                    k.grad[c] += dot(k.pay[0, :, columns(b3)], k.blocks[b3, c])

                by_unit(sibling + far, c)

                @pl.when(jnp.logical_not(plain))
                def _():
                    k.early[c] += lent_product(b3, c) + lent_product(sibling + far, c)
                    encode(k.early[c], k.sum_out.at[5, c])
                    sum_copy(5, c, outward).start()
                    k.grad[c] += dot(k.pay[0, :, columns(b3)], k.blocks[b3, c])

                k.grad[c] += dot(k.pay[0, :, columns(sibling + far)], k.blocks[sibling + far, c])

            @pl.when(jnp.logical_not(inner | plain))
            def _():
                k.grad[c] += sum_arrival(5, c)

            if c > 0:
                finish(c - 1)

        @pl.when(inner & jnp.logical_not(plain))
        def _():
            turn_lent(1)

        @pl.when(inner & plain)
        def _():
            for c in range(4):
                go_on(part_of(b, c), b, c, outward).wait_send()
                go_on(unit_of(b3, c), b3, c, outward).wait_send()

        @pl.when(inner)
        def _():
            for c in range(4):
                go_on(unit_of(b2, c), b2, c, -outward).wait_send()

        pass_on(k.blocks.at[b], b, 0).wait_send()

        @pl.when(inner | plain)
        def _():
            pass_on(k.blocks.at[b2], b2, 0).wait_send()
            for c in range(4):
                pass_on(unit_of(b3, c), b3, c).wait_send()

        @pl.when(inner & jnp.logical_not(plain))
        def _():
            for c in range(4):
                sum_copy(5, c, outward).wait_send()

        @pl.when(jnp.logical_not(inner | plain))
        def _():
            for turn in range(8):
                lend(turn).wait_send()

        for s in range(n_r):
            own_drain(s)

        def lend_more(turns):
            @pl.when(index == 0)
            def _():
                lend_start(turns)

        prox(-1.0, smooth_x, functools.partial(lend_more, range(5, 7)))
        for d in range(n_r):
            s = (me_r + d) % n_r
            if d > 0:
                back_arrival(s)
            value = mixed_part(s, k.f_x, weight, nn).astype(bf16)
            for c in range(4):
                k.mixed[core, c, rows_of(s), :] = value[:, c * wide : (c + 1) * wide]
            mixed_copy(s).start()

        @pl.when(jnp.logical_not(inner))
        def _():
            for n in range(4):
                raw_copy(n).start()

        for d in range(n_r):
            mixed_arrival((me_r + d) % n_r).wait_recv()

        @pl.when(inner)
        def _():
            @pl.when(index == 0)
            def _():
                wait_lent(0)
                turn_lent(0)

            sums_of_inner(index)

        @pl.when(jnp.logical_not(inner))
        def _():
            sums_of_end(index)

        prox_drain()
        for s in range(n_r):
            mixed_copy(s).wait_send()
        share = jnp.where(index == 0, weights[0] * (1.0 - weights[1]), weights[1])
        for s in range(n_r):
            add_best(k.xo_ref, s, share)

            @pl.when(index == 1)
            def _():
                out_copy(0, s).start()

        for n in range(4):
            k.grad[n] = partial(pair, n)
        for u in range(3):
            for n in members[u]:

                @pl.when(inner)
                def _():
                    k.grad[n] += sum_arrival(3, n)
                    k.grad[n] += sum_arrival(1, n)

                @pl.when(jnp.logical_not(inner))
                def _():
                    k.grad[n] += sum_arrival(2, n)

            finish(u)
        sums_drain(index)

        prox(1.0, smooth_y, functools.partial(lend_more, range(7, 8)))
        for d in range(n_r):
            s = (me_r + d) % n_r
            if d > 0:
                back_arrival(s)

            @pl.when(index == 0)
            def _():
                set_own(s, mixed_part(s, k.f_y, weight, nt))
                own_start(s)

            @pl.when(index == 1)
            def _():
                add_best(k.yo_ref, s, weights[1])
                out_copy(1, s).start()

        prox_drain()
        return 0

    lax.fori_loop(0, 2, step, 0)
    for i in range(2):
        for s in range(n_r):
            out_copy(i, s).wait()


def place_kernel(x_in, y_in, x_out, y_out):
    x_out[...] = x_in[...]
    y_out[...] = y_in[...]


def line_body(x_start, y_start, bucket_payoff, column_blocks, public_coef, predecessor_sequences):
    n_r = lax.axis_size("round")
    n_b = lax.axis_size("bucket")
    _, rows, seqs = x_start.shape
    half = seqs // 2
    part = rows // n_r
    pairs = n_b // 2
    f32, bf16, i16 = jnp.float32, jnp.bfloat16, jnp.int16
    vmem = pl.BlockSpec(memory_space=pltpu.VMEM)
    smem = pl.BlockSpec(memory_space=pltpu.SMEM)
    hbm = pl.BlockSpec(memory_space=pl.ANY)
    dma = pltpu.SemaphoreType.DMA
    scratch = dict(
        xv=pltpu.VMEM((1, rows, seqs), f32),
        yv=pltpu.VMEM((1, rows, seqs), f32),
        xo_ref=pltpu.VMEM((1, rows, seqs), f32),
        yo_ref=pltpu.VMEM((1, rows, seqs), f32),
        pay=pltpu.VMEM((1, rows, n_b * rows), bf16),
        pay_t=pltpu.VMEM((pairs, 2, rows, rows), bf16),
        pay_out=pltpu.VMEM((pairs, rows, rows), bf16),
        blocks=pltpu.VMEM((n_b, 4, rows, half // 2), bf16),
        mixed=pltpu.VMEM((4, 4, rows, half // 2), bf16),
        mixer=pltpu.VMEM((seqs, seqs), f32),
        mix_p=pltpu.VMEM((3, seqs, seqs), bf16),
        to_outer=pltpu.VMEM((seqs, seqs), bf16),
        gather=pltpu.VMEM((n_r - 1, seqs, half), bf16),
        spread=pltpu.VMEM((n_r - 1, half, seqs), bf16),
        f_x=pltpu.VMEM((rows, seqs), f32),
        f_y=pltpu.VMEM((rows, seqs), f32),
        grad=pltpu.VMEM((4, rows, half // 2), f32),
        work=pltpu.VMEM((rows, half // 2), f32),
        early=pltpu.VMEM((4, rows, half // 2), f32),
        lent=pltpu.VMEM((4, rows, rows), bf16),
        lent_t=pltpu.VMEM((2, 2, rows, rows), bf16),
        sum_out=pltpu.VMEM((6, 4, rows + 16, half // 2), i16),
        sum_in=pltpu.VMEM((6, 4, rows + 16, half // 2), i16),
        row_q=pltpu.VMEM((n_r, 4, part + 16, half // 2), i16),
        row_in=pltpu.VMEM((n_r, 4, part + 16, half // 2), i16),
        rows_f=pltpu.VMEM((n_r, 2, part, half), f32),
        share=pltpu.VMEM((n_r, 2, part, half), f32),
        back_q=pltpu.VMEM((n_r, 2, part, half), i16),
        back_in=pltpu.VMEM((n_r, 2, part, half), i16),
        sq_mine=pltpu.VMEM((8, 128), f32),
        sq_all=pltpu.VMEM((n_r * n_b, 1, 128), f32),
        load_sem=dma((3,)),
        out_sem=dma((2, n_r)),
        turn_send=dma((pairs,)),
        turn_recv=dma((pairs,)),
        ag_send=dma((3, n_r)),
        ag_recv=dma((n_b, n_r)),
        line_send=dma((n_b, n_r)),
        pass_send=dma((n_b, 4)),
        mx_send=dma((n_r,)),
        mx_recv=dma((2, n_r)),
        sum_send=dma((6, 4)),
        sum_recv=dma((6, 4)),
        lend_send=dma((8,)),
        lend_recv=dma((8,)),
        swap_send=dma((2,)),
        swap_recv=dma((2,)),
        raw_send=dma((4,)),
        raw_recv=dma((2, 4)),
        row_send=dma((n_r, 3)),
        row_recv=dma((n_r, 3)),
        back_send=dma((n_r, 2)),
        back_recv=dma((n_r, 2)),
        sq_send=dma((n_r * n_b,)),
        sq_recv=dma((n_r * n_b,)),
    )
    names = ["x_hbm", "y_hbm", "pay_hbm", "col_ref", "coef_ref", "pred_ref", "x_out", "y_out"]
    names += list(scratch)
    found = pl.pallas_call(
        functools.partial(line_kernel, names, n_r, n_b),
        out_shape=[jax.ShapeDtypeStruct(x_start.shape, f32)] * 2,
        in_specs=[hbm, hbm, hbm, smem, vmem, vmem],
        out_specs=[hbm, hbm],
        scratch_shapes=list(scratch.values()),
        compiler_params=pltpu.CompilerParams(
            collective_id=0, has_side_effects=True, vmem_limit_bytes=60 * 1024 * 1024
        ),
    )(
        x_start,
        y_start,
        bucket_payoff,
        jnp.transpose(column_blocks, (2, 0, 1)),
        public_coef,
        predecessor_sequences,
    )
    block = pl.BlockSpec((1, rows // 2, seqs), lambda i: (0, i, 0))
    return pl.pallas_call(
        place_kernel,
        grid=(2,),
        out_shape=[jax.ShapeDtypeStruct(x_start.shape, f32)] * 2,
        in_specs=[block, block],
        out_specs=[block, block],
    )(*found)


def plain_kernel(
    n_r,
    n_b,
    x_ref,
    y_ref,
    pay_ref,
    col_ref,
    coef_ref,
    pred_ref,
    xo_ref,
    yo_ref,
    xs,
    ys,
    mixer,
    gather,
    pay_t,
    blocks,
    mixed,
    grad,
    sib_out,
    sib_in,
    far_out,
    far_in,
    sq_b,
    sq_r,
    rows_in,
    score,
    norm,
    mass,
    back_in,
    far_q,
    far_s,
    far_q_in,
    far_s_in,
    row_q,
    row_s,
    row_q_in,
    row_s_in,
    back_q,
    back_s,
    back_q_in,
    back_s_in,
    ag_send,
    ag_recv,
    fw_send,
    line_send,
    sib_send,
    sib_recv,
    far_send,
    far_recv,
    sqb_send,
    sqb_recv,
    sqr_send,
    sqr_recv,
    row_send,
    row_recv,
    back_send,
    back_recv,
    far_s_send,
    far_s_recv,
    row_s_send,
    row_s_recv,
    back_s_send,
    back_s_recv,
):
    rows, seqs = xs.shape
    half = seqs // 2
    part = rows // n_r
    pairs = n_b // 2
    me_r = lax.axis_index("round")
    me_b = lax.axis_index("bucket")
    pair = me_b // 2
    core = me_b % 2
    sibling = pair * 2 + 1 - core
    total_count = n_r * n_b * rows * seqs

    def remote(src, dst, send, recv, **where):
        return pltpu.make_async_remote_copy(
            src_ref=src,
            dst_ref=dst,
            send_sem=send,
            recv_sem=recv,
            device_id=where,
            device_id_type=pl.DeviceIdType.MESH,
        )

    barrier = pltpu.get_barrier_semaphore()
    for d in range(1, n_b):
        pl.semaphore_signal(
            barrier,
            inc=1,
            device_id={"bucket": (me_b + d) % n_b},
            device_id_type=pl.DeviceIdType.MESH,
        )
    for d in range(1, n_r):
        pl.semaphore_signal(
            barrier,
            inc=1,
            device_id={"round": (me_r + d) % n_r},
            device_id_type=pl.DeviceIdType.MESH,
        )
    pl.semaphore_wait(barrier, n_b + n_r - 2)

    def order(i):
        return jnp.where(i < half, 2 * i, 2 * (i - half) + 1)

    down = lax.broadcasted_iota(jnp.int32, (seqs, seqs), 0)
    across = lax.broadcasted_iota(jnp.int32, (seqs, seqs), 1)
    to_inner = (down == order(across)).astype(jnp.float32)
    to_outer = (order(down) == across).astype(jnp.float32)

    tiles, per_row, tile, _ = coef_ref.shape[1:]
    for m in range(tiles):
        for c in range(tiles):
            value = jnp.zeros((tile, tile), jnp.float32)
            for t in range(per_row):
                value = value + jnp.where(col_ref[0, m, t] == c, coef_ref[0, m, t], 0.0)
            mixer[m * tile : (m + 1) * tile, c * tile : (c + 1) * tile] = value
    mixer[...] = exact(to_outer, exact(mixer[...], to_inner))
    ys[...] = exact(y_ref[0], to_inner)
    for r in range(n_r - 1):
        place = order(lax.broadcasted_iota(jnp.int32, (seqs, half), 0))
        gather[r] = (place == pred_ref[r : r + 1, :]).astype(jnp.float32)

    def columns(j):
        return pl.ds(pl.multiple_of(j * rows, rows), rows)

    def coded(value, code_ref, scale_ref):
        top = jnp.max(jnp.abs(value), axis=0, keepdims=True)
        unit = jnp.maximum(top, 1e-30) / 32767.0
        code = jnp.floor(value * (1.0 / unit) + 0.5)
        code_ref[...] = code.astype(jnp.int32).astype(jnp.int16)
        scale_ref[...] = jnp.broadcast_to(unit, scale_ref.shape)

    def decoded(code_ref, scale_ref):
        return code_ref[...].astype(jnp.int32).astype(jnp.float32) * scale_ref[0:1, :]

    def prox(state, sign, factor, weight, short):
        def row_copy(d):
            s = (me_r + d) % n_r
            here = grad.at[pl.ds(pl.multiple_of(s * part, part), part)]
            if not short:
                return [
                    remote(here, rows_in.at[me_r], row_send.at[s], row_recv.at[me_r], round=s)
                ]
            return [
                remote(
                    row_q.at[s], row_q_in.at[me_r], row_send.at[s], row_recv.at[me_r], round=s
                ),
                remote(
                    row_s.at[s], row_s_in.at[me_r], row_s_send.at[s], row_s_recv.at[me_r], round=s
                ),
            ]

        def row_arrival(d):
            s = (me_r + d) % n_r
            if not short:
                return [
                    remote(rows_in.at[s], rows_in.at[s], row_send.at[s], row_recv.at[s], round=s)
                ]
            return [
                remote(row_q_in.at[s], row_q_in.at[s], row_send.at[s], row_recv.at[s], round=s),
                remote(
                    row_s_in.at[s], row_s_in.at[s], row_s_send.at[s], row_s_recv.at[s], round=s
                ),
            ]

        for d in range(1, n_r):
            if short:
                s = (me_r + d) % n_r
                here = pl.ds(pl.multiple_of(s * part, part), part)
                coded(grad[here, :], row_q.at[s], row_s.at[s])
            for copy in row_copy(d):
                copy.start()
        squares = grad[...]
        squares = jnp.sum((squares * squares).reshape(rows // 8, 8, seqs), axis=0)
        squares = sum(squares[:, i * 128 : (i + 1) * 128] for i in range(seqs // 128))
        sq_b[me_b] = squares

        def sqb_copy(d):
            s = (me_b + d) % n_b
            return remote(
                sq_b.at[me_b], sq_b.at[me_b], sqb_send.at[d], sqb_recv.at[me_b], bucket=s
            )

        def sqb_arrival(d):
            s = (me_b + d) % n_b
            return remote(sq_b.at[s], sq_b.at[s], sqb_send.at[d], sqb_recv.at[s], bucket=s)

        for d in range(1, n_b):
            sqb_copy(d).start()
        rows_in[me_r] = grad[pl.ds(pl.multiple_of(me_r * part, part), part), :]
        for d in range(1, n_b):
            sqb_arrival(d).wait_recv()
        sq_r[me_r] = jnp.sum(sq_b[...], axis=0)

        def sqr_copy(d):
            s = (me_r + d) % n_r
            return remote(sq_r.at[me_r], sq_r.at[me_r], sqr_send.at[d], sqr_recv.at[me_r], round=s)

        def sqr_arrival(d):
            s = (me_r + d) % n_r
            return remote(sq_r.at[s], sq_r.at[s], sqr_send.at[d], sqr_recv.at[s], round=s)

        for d in range(1, n_r):
            sqr_copy(d).start()
        for d in range(1, n_r):
            sqr_arrival(d).wait_recv()
        squares = jnp.sum(jnp.sum(sq_r[...], axis=0), axis=0, keepdims=True)
        squares = jnp.sum(squares, axis=1, keepdims=True)
        scale = sign / (factor * jnp.sqrt(squares / total_count + epsilon))
        for d in range(1, n_r):
            for copy in row_arrival(d):
                copy.wait_recv()
            if short:
                s = (me_r + d) % n_r
                rows_in[s] = decoded(row_q_in.at[s], row_s_in.at[s])

        for r in reversed(range(n_r)):
            values = rows_in[r] * scale
            if r < n_r - 1:
                values = values + exact(norm[r + 1], gather[r], nt)
            score[r] = values
            even, odd = values[:, :half], values[:, half:]
            larger = jnp.maximum(even, odd)
            norm[r] = larger + jnp.log(jnp.exp(even - larger) + jnp.exp(odd - larger))

        def back_copy(r):
            if not short:
                return [
                    remote(
                        mass.at[r], back_in.at[me_r], back_send.at[r], back_recv.at[me_r], round=r
                    )
                ]
            return [
                remote(
                    back_q.at[r], back_q_in.at[me_r], back_send.at[r], back_recv.at[me_r], round=r
                ),
                remote(
                    back_s.at[r],
                    back_s_in.at[me_r],
                    back_s_send.at[r],
                    back_s_recv.at[me_r],
                    round=r,
                ),
            ]

        def back_arrival(s):
            if not short:
                return [
                    remote(
                        back_in.at[s], back_in.at[s], back_send.at[s], back_recv.at[s], round=s
                    )
                ]
            return [
                remote(
                    back_q_in.at[s], back_q_in.at[s], back_send.at[s], back_recv.at[s], round=s
                ),
                remote(
                    back_s_in.at[s], back_s_in.at[s], back_s_send.at[s], back_s_recv.at[s], round=s
                ),
            ]

        for r in range(n_r):
            even = jnp.exp(score[r, :, :half] - norm[r])
            odd = jnp.exp(score[r, :, half:] - norm[r])
            if r > 0:
                parent = exact(mass[r - 1], gather[r - 1])
                even = parent * even
                odd = parent * odd
            mass[r, :, :half] = even
            mass[r, :, half:] = odd

            @pl.when(me_r != r)
            def _():
                if short:
                    coded(mass[r], back_q.at[r], back_s.at[r])
                for copy in back_copy(r):
                    copy.start()

        def update(s, best):
            here = pl.ds(pl.multiple_of(s * part, part), part)
            state[here, :] = (1.0 - weight) * state[here, :] + weight * best

        update(me_r, mass[me_r])
        for d in range(1, n_r):
            s = (me_r + d) % n_r
            for copy in back_arrival(s):
                copy.wait_recv()
            if short:
                update(s, decoded(back_q_in.at[s], back_s_in.at[s]))
            else:
                update(s, back_in[s])
        for d in range(1, n_r):
            for copy in row_copy(d) + back_copy((me_r + d) % n_r):
                copy.wait_send()
            sqr_copy(d).wait_send()
        for d in range(1, n_b):
            sqb_copy(d).wait_send()

    def step(index, _):
        weight = 2.0 / (index.astype(jnp.float32) + 3.0)
        short = False

        blocks[me_b] = exact(ys[...], mixer[...], nt).astype(jnp.bfloat16)

        def own_copy(kind):
            target = (sibling, me_b + 2, me_b - 2)[kind]
            return remote(
                blocks.at[me_b], blocks.at[me_b], ag_send.at[kind], ag_recv.at[me_b], bucket=target
            )

        def go_on(b, d, step):
            return remote(
                blocks.at[b], blocks.at[b], line_send.at[d], ag_recv.at[b], bucket=me_b + step
            )

        def pass_on(b, d):
            return remote(blocks.at[b], blocks.at[b], fw_send.at[d], ag_recv.at[b], bucket=sibling)

        def arrival(b):
            return remote(
                blocks.at[b], blocks.at[b], ag_send.at[0], ag_recv.at[b], bucket=sibling
            )

        def product(b):
            return jnp.dot(
                pay_ref[0, :, columns(b)], blocks[b], preferred_element_type=jnp.float32
            )

        @pl.when(pair < pairs - 1)
        def _():
            own_copy(1).start()

        @pl.when(pair > 0)
        def _():
            own_copy(2).start()

        own_copy(0).start()
        @pl.when(index == 0)
        def _():
            xs[...] = exact(x_ref[0], to_inner)

            def turn(j, _):
                pay_t[columns(j), :] = pay_ref[0, :, columns(j)].T
                return 0

            lax.fori_loop(0, n_b, turn, 0)
        grad[...] = product(me_b)
        arrival(sibling).wait_recv()
        grad[...] += product(sibling)

        def take(d, _):
            left = me_b - 2 * d
            right = me_b + 2 * d

            @pl.when(pair >= d)
            def _():
                arrival(left).wait_recv()

                @pl.when(pair < pairs - 1)
                def _():
                    go_on(left, d, 2).start()

                pass_on(left, d).start()

            @pl.when(pair + d < pairs)
            def _():
                arrival(right).wait_recv()

                @pl.when(pair > 0)
                def _():
                    go_on(right, pairs + d, -2).start()

                pass_on(right, pairs + d).start()

            def use(b, other):
                grad[...] += product(b)
                arrival(other).wait_recv()
                grad[...] += product(other)

            @pl.when(pair >= d)
            def _():
                use(left, sibling - 2 * d)

            @pl.when(pair + d < pairs)
            def _():
                use(right, sibling + 2 * d)

            return 0

        lax.fori_loop(1, pairs, take, 0)

        def drain(d, _):
            left = me_b - 2 * d
            right = me_b + 2 * d

            @pl.when(pair >= d)
            def _():
                pass_on(left, d).wait_send()

                @pl.when(pair < pairs - 1)
                def _():
                    go_on(left, d, 2).wait_send()

            @pl.when(pair + d < pairs)
            def _():
                pass_on(right, pairs + d).wait_send()

                @pl.when(pair > 0)
                def _():
                    go_on(right, pairs + d, -2).wait_send()

            return 0

        lax.fori_loop(1, pairs, drain, 0)
        own_copy(0).wait_send()

        @pl.when(pair < pairs - 1)
        def _():
            own_copy(1).wait_send()

        @pl.when(pair > 0)
        def _():
            own_copy(2).wait_send()

        prox(xs, -1.0, smooth_x, weight, short)

        mixed[...] = exact(xs[...], mixer[...]).astype(jnp.bfloat16)

        def partial(b):
            return jnp.dot(pay_t[columns(b), :], mixed[...], preferred_element_type=jnp.float32)

        def sib_copy(q):
            return remote(
                sib_out.at[q], sib_in.at[q], sib_send.at[q], sib_recv.at[q], bucket=sibling
            )

        def far_copy(q, step, target):
            slot = q if step > 0 else pairs + q
            if not short:
                return [
                    remote(
                        far_out.at[q],
                        far_in.at[slot],
                        far_send.at[q],
                        far_recv.at[slot],
                        bucket=target,
                    )
                ]
            return [
                remote(
                    far_q.at[q],
                    far_q_in.at[slot],
                    far_send.at[q],
                    far_recv.at[slot],
                    bucket=target,
                ),
                remote(
                    far_s.at[q],
                    far_s_in.at[slot],
                    far_s_send.at[q],
                    far_s_recv.at[slot],
                    bucket=target,
                ),
            ]

        def far_value(q, step):
            slot = q if step > 0 else pairs + q
            for copy in far_copy(q, step, sibling):
                copy.wait_recv()
            if short:
                return decoded(far_q_in.at[slot], far_s_in.at[slot])
            return far_in[slot]

        def to_sibling(q):
            sib_out[q] = partial(q * 2 + 1 - core)
            sib_copy(q).start()

        def move(q, step):
            far_out[q] = partial(q * 2 + core)
            sib_copy(q).wait_recv()
            far_out[q] += sib_in[q]

            @pl.when(pair > 0 if step > 0 else pair < pairs - 1)
            def _():
                far_out[q] += far_value(q, step)

            if short:
                coded(far_out[q], far_q.at[q], far_s.at[q])
            for copy in far_copy(q, step, me_b + step):
                copy.start()

        def outward(right, left):
            def one(i, _):
                @pl.when(pair < pairs - 1 - i)
                def _():
                    right(pairs - 1 - i)

                @pl.when(pair > i)
                def _():
                    left(i)

                return 0

            lax.fori_loop(0, pairs - 1, one, 0)

        def far_done(q, step):
            for copy in far_copy(q, step, me_b + step):
                copy.wait_send()

        outward(to_sibling, to_sibling)
        outward(lambda q: move(q, 2), lambda q: move(q, -2))
        to_sibling(pair)
        grad[...] = partial(me_b)
        sib_copy(pair).wait_recv()
        grad[...] += sib_in[pair]

        @pl.when(pair > 0)
        def _():
            grad[...] += far_value(pair, 2)

        @pl.when(pair < pairs - 1)
        def _():
            grad[...] += far_value(pair, -2)

        outward(lambda q: far_done(q, 2), lambda q: far_done(q, -2))
        for q in range(pairs):
            sib_copy(q).wait_send()
        prox(ys, 1.0, smooth_y, weight, short)
        return 0

    lax.fori_loop(0, 2, step, 0)
    down = lax.broadcasted_iota(jnp.int32, (seqs, seqs), 0)
    across = lax.broadcasted_iota(jnp.int32, (seqs, seqs), 1)
    to_outer = (order(down) == across).astype(jnp.float32)
    xo_ref[0] = exact(xs[...], to_outer)
    yo_ref[0] = exact(ys[...], to_outer)


def plain_body(x_start, y_start, bucket_payoff, column_blocks, public_coef, predecessor_sequences):
    n_r = lax.axis_size("round")
    n_b = lax.axis_size("bucket")
    _, rows, seqs = x_start.shape
    part = rows // n_r
    pairs = n_b // 2
    f32, bf16 = jnp.float32, jnp.bfloat16
    vmem = pl.BlockSpec(memory_space=pltpu.VMEM)
    smem = pl.BlockSpec(memory_space=pltpu.SMEM)
    dma = pltpu.SemaphoreType.DMA
    return pl.pallas_call(
        functools.partial(plain_kernel, n_r, n_b),
        out_shape=[jax.ShapeDtypeStruct(x_start.shape, f32)] * 2,
        in_specs=[vmem, vmem, vmem, smem, vmem, vmem],
        out_specs=[vmem, vmem],
        scratch_shapes=[
            pltpu.VMEM((rows, seqs), f32),
            pltpu.VMEM((rows, seqs), f32),
            pltpu.VMEM((seqs, seqs), f32),
            pltpu.VMEM((n_r - 1, seqs, seqs // 2), f32),
            pltpu.VMEM((n_b * rows, rows), bf16),
            pltpu.VMEM((n_b, rows, seqs), bf16),
            pltpu.VMEM((rows, seqs), bf16),
            pltpu.VMEM((rows, seqs), f32),
            pltpu.VMEM((pairs, rows, seqs), f32),
            pltpu.VMEM((pairs, rows, seqs), f32),
            pltpu.VMEM((pairs, rows, seqs), f32),
            pltpu.VMEM((2 * pairs, rows, seqs), f32),
            pltpu.VMEM((n_b, 8, 128), f32),
            pltpu.VMEM((n_r, 8, 128), f32),
            pltpu.VMEM((n_r, part, seqs), f32),
            pltpu.VMEM((n_r, part, seqs), f32),
            pltpu.VMEM((n_r, part, seqs // 2), f32),
            pltpu.VMEM((n_r, part, seqs), f32),
            pltpu.VMEM((n_r, part, seqs), f32),
            pltpu.VMEM((16, 128), jnp.int16),
            pltpu.VMEM((pairs, 8, seqs), f32),
            pltpu.VMEM((16, 128), jnp.int16),
            pltpu.VMEM((2 * pairs, 8, seqs), f32),
            pltpu.VMEM((16, 128), jnp.int16),
            pltpu.VMEM((n_r, 8, seqs), f32),
            pltpu.VMEM((16, 128), jnp.int16),
            pltpu.VMEM((n_r, 8, seqs), f32),
            pltpu.VMEM((16, 128), jnp.int16),
            pltpu.VMEM((n_r, 8, seqs), f32),
            pltpu.VMEM((16, 128), jnp.int16),
            pltpu.VMEM((n_r, 8, seqs), f32),
            dma((3,)),
            dma((n_b,)),
            dma((2 * pairs,)),
            dma((2 * pairs,)),
            dma((pairs,)),
            dma((pairs,)),
            dma((pairs,)),
            dma((2 * pairs,)),
            dma((n_b,)),
            dma((n_b,)),
            dma((n_r,)),
            dma((n_r,)),
            dma((n_r,)),
            dma((n_r,)),
            dma((n_r,)),
            dma((n_r,)),
            dma((pairs,)),
            dma((2 * pairs,)),
            dma((n_r,)),
            dma((n_r,)),
            dma((n_r,)),
            dma((n_r,)),
        ],
        compiler_params=pltpu.CompilerParams(
            collective_id=0, has_side_effects=True, vmem_limit_bytes=60 * 1024 * 1024
        ),
    )(x_start, y_start, bucket_payoff, column_blocks, public_coef, predecessor_sequences)


def solution(mesh):
    in_specs = (
        P("round", "bucket", None),
        P("round", "bucket", None),
        P("round", "bucket", None),
        P("round", None, None),
        P("round", None, None, None, None),
        P(),
    )
    out_specs = (P("round", "bucket", None), P("round", "bucket", None))

    line = mesh.shape["round"] == 4 and mesh.shape["bucket"] == 8

    def run(*arrays):
        return tuple(
            jax.shard_map(
                line_body if line else plain_body, mesh=mesh, in_specs=in_specs, out_specs=out_specs, check_vma=False
            )(*arrays)
        )

    return run
```

```python
import functools
import types

import jax
import jax.numpy as jnp
from jax import lax
from jax.experimental import pallas as pl
from jax.experimental.pallas import tpu as pltpu
from jax.sharding import PartitionSpec as P

smooth_x = 0.1
smooth_y = 0.1
epsilon = 1e-06
highest = lax.Precision.HIGHEST
nn = (((1,), (0,)), ((), ()))
nt = (((1,), (1,)), ((), ()))


def exact(a, b, dims=nn):
    return lax.dot_general(a, b, dims, precision=highest, preferred_element_type=jnp.float32)


weights = (2.0 / 3.0, 2.0 / 4.0)
top_code = 65535.0
shift_code = 32768


def split3(value):
    hi = value.astype(jnp.bfloat16)
    left = value - hi.astype(jnp.float32)
    mid = left.astype(jnp.bfloat16)
    lo = (left - mid.astype(jnp.float32)).astype(jnp.bfloat16)
    return [hi, mid, lo]


def dot(a, b, dims=nn):
    return lax.dot_general(a, b, dims, preferred_element_type=jnp.float32)


def picked(parts, one_hot, dims=nn):
    size = parts[0].shape[0]
    out = dot(jnp.concatenate(parts, axis=0), one_hot, dims)
    return sum(out[i * size : (i + 1) * size] for i in range(len(parts)))


def mix(parts, factors, dims):
    size = parts[0].shape[0]
    total = None
    for i, factor in reversed(list(enumerate(factors))):
        count = min(len(parts), 3 - i)
        out = dot(jnp.concatenate(parts[:count], axis=0), factor, dims)
        for j in reversed(range(count)):
            term = out[j * size : (j + 1) * size]
            total = term if total is None else total + term
    return total


def encode(value, code_ref):
    if len(code_ref.shape) == 3:
        wide = code_ref.shape[2]
        for i in range(code_ref.shape[0]):
            encode(value[:, i * wide : (i + 1) * wide], code_ref.at[i])
        return
    rows = value.shape[0]
    top = jnp.maximum(jnp.max(jnp.abs(value), axis=0, keepdims=True), 1e-30)
    power = jnp.floor(256.0 * jnp.log2(top * (1.0 / 32767.0))) + 1.0
    code = jnp.floor(value * jnp.exp2(power * (-1.0 / 256.0)) + 0.5)
    code_ref[:rows, :] = code.astype(jnp.int32).astype(jnp.int16)
    power = jnp.broadcast_to(power, (16, value.shape[1]))
    code_ref[rows:, :] = power.astype(jnp.int32).astype(jnp.int16)


def decode(code_ref):
    if len(code_ref.shape) == 3:
        return jnp.concatenate([decode(code_ref.at[i]) for i in range(code_ref.shape[0])], axis=1)
    rows = code_ref.shape[0] - 16
    power = code_ref[rows:, :].astype(jnp.int32).astype(jnp.float32)[0:1, :]
    unit = jnp.exp2(power * (1.0 / 256.0))
    return code_ref[:rows, :].astype(jnp.int32).astype(jnp.float32) * unit


def line_kernel(names, n_r, n_b, *refs):
    k = types.SimpleNamespace(**dict(zip(names, refs)))
    f32, bf16 = jnp.float32, jnp.bfloat16
    _, rows, seqs = k.x_hbm.shape
    half = seqs // 2
    wide = half // 2
    part = rows // n_r
    pairs = n_b // 2
    me_r = lax.axis_index("round")
    me_b = lax.axis_index("bucket")
    pair = me_b // 2
    core = me_b % 2
    sibling = pair * 2 + 1 - core
    spans = ((0, slice(0, half)), (1, slice(0, wide)), (1, slice(wide, half)))
    quarters = (slice(0, 2), slice(2, 3), slice(3, 4))
    members = ((0, 1), (2,), (3,))
    outward = jnp.where(pair < pairs // 2, -2, 2)
    end_chip = jnp.where(pair < pairs // 2, 0, pairs - 1)
    facing = pair - outward // 2
    far_end = pairs - 1 - end_chip
    inner = (pair > 0) & (pair < pairs - 1)
    total_count = n_r * n_b * rows * seqs

    def remote(src, dst, send, recv, **where):
        return pltpu.make_async_remote_copy(
            src_ref=src,
            dst_ref=dst,
            send_sem=send,
            recv_sem=recv,
            device_id=where,
            device_id_type=pl.DeviceIdType.MESH,
        )

    load_y = pltpu.make_async_copy(k.y_hbm, k.yv, k.load_sem.at[0])
    load_pay = pltpu.make_async_copy(k.pay_hbm, k.pay, k.load_sem.at[1])
    load_x = pltpu.make_async_copy(k.x_hbm, k.xv, k.load_sem.at[2])
    load_y.start()
    load_pay.start()
    load_x.start()

    barrier = pltpu.get_barrier_semaphore()
    for dr in range(n_r):
        for db in range(n_b):
            if dr or db:
                pl.semaphore_signal(
                    barrier,
                    inc=1,
                    device_id={"round": (me_r + dr) % n_r, "bucket": (me_b + db) % n_b},
                    device_id_type=pl.DeviceIdType.MESH,
                )

    def order(i):
        return 2 * (i // half * wide + i % wide) + (i % half) // wide

    down = lax.broadcasted_iota(jnp.int32, (seqs, seqs), 0)
    across = lax.broadcasted_iota(jnp.int32, (seqs, seqs), 1)
    k.to_outer[...] = (order(down) == across).astype(f32).astype(bf16)

    tiles, per_row, tile, _ = k.coef_ref.shape[1:]
    for m in range(tiles):
        for c in range(tiles):
            value = jnp.zeros((tile, tile), f32)
            for t in range(per_row):
                value = value + jnp.where(k.col_ref[t, 0, m] == c, k.coef_ref[0, m, t], 0.0)
            k.mixer[m * tile : (m + 1) * tile, c * tile : (c + 1) * tile] = value
    for i, piece in enumerate(split3(k.mixer[...])):
        k.mix_p[i] = dot(k.to_outer[...], piece).astype(bf16)

    def rows_of(s):
        return pl.ds(pl.multiple_of(s * part, part), part)

    def columns(j):
        return pl.ds(pl.multiple_of(j * rows, rows), rows)

    away = jnp.where(pair < pairs // 2, pairs // 2, 0)

    def lent_place(o):
        return (far_end - away, 1 - (far_end - away))[o]

    def lend(turn):
        o, i, p = turn // 4, turn // 2 % 2, turn % 2
        here = pl.ds(p * (rows // 2), rows // 2)
        b = 2 * lent_place(o) + i
        return remote(
            k.pay.at[0, here, columns(2 * away + b)],
            k.lent.at[b, here],
            k.lend_send.at[turn],
            k.lend_recv.at[turn],
            bucket=me_b - outward,
        )

    def lend_start(turns):
        @pl.when(jnp.logical_not(inner))
        def _():
            for turn in turns:
                lend(turn).start()

    def lent_swap(j, o):
        return remote(
            k.pay_out.at[j],
            k.lent_t.at[j, core],
            k.swap_send.at[o],
            k.swap_recv.at[o],
            bucket=sibling,
        )

    def wait_lent(o):
        j = lent_place(o)
        for i in range(2):
            for p in range(2):
                here = k.lent.at[2 * j + i, pl.ds(p * (rows // 2), rows // 2)]
                turn = 4 * o + 2 * i + p
                remote(
                    here, here, k.lend_send.at[turn], k.lend_recv.at[turn], bucket=sibling
                ).wait_recv()

    def turn_lent(o):
        j = lent_place(o)
        k.pay_out[j] = k.lent[2 * j + 1 - core].T
        lent_swap(j, o).start()
        k.lent_t[j, core] = k.lent[2 * j + core].T
        lent_swap(j, o).wait()


    def own_copy(kind, s):
        target = (sibling, me_b + 2, me_b - 2)[kind]
        here = k.blocks.at[me_b, :, rows_of(s), :]
        return remote(here, here, k.ag_send.at[kind, s], k.ag_recv.at[me_b, s], bucket=target)

    def own_start(s):
        @pl.when(pair < pairs - 1)
        def _():
            own_copy(1, s).start()

        @pl.when(pair > 0)
        def _():
            own_copy(2, s).start()

        own_copy(0, s).start()

    def own_drain(s):
        @pl.when(pair < pairs - 1)
        def _():
            own_copy(1, s).wait_send()

        @pl.when(pair > 0)
        def _():
            own_copy(2, s).wait_send()

        own_copy(0, s).wait_send()

    def set_own(s, value):
        value = value.astype(bf16)
        for c in range(4):
            k.blocks[me_b, c, rows_of(s), :] = value[:, c * wide : (c + 1) * wide]

    pl.semaphore_wait(barrier, n_b * n_r - 1)
    load_y.wait()
    load_pay.wait()
    lend_start(range(1))
    for s in range(n_r):
        value = mix(split3(k.yv[0, rows_of(s), :]), [k.mix_p[i] for i in range(3)], nt)
        k.f_y[rows_of(s), :] = value
        set_own(s, value)
        own_start(s)

    def part_of(b, s):
        return k.blocks.at[b, :, rows_of(s), :]

    def unit_of(b, c):
        return k.blocks.at[b, c]

    def block(b, u):
        return jnp.concatenate([k.blocks[b, c] for c in members[u]], axis=1)

    def by_parts(b):
        for s in range(n_r):
            arrived(part_of(b, s), b, s)

    def by_whole(b):
        arrived(k.blocks.at[b], b, 0)

    def by_unit(b, c):
        arrived(unit_of(b, c), b, c)

    def arrived(here, b, i):
        remote(here, here, k.ag_send.at[0, 0], k.ag_recv.at[b, i], bucket=sibling).wait_recv()

    def go_on(here, b, i, step):
        return remote(here, here, k.line_send.at[b, i], k.ag_recv.at[b, i], bucket=me_b + step)

    def pass_on(here, b, i):
        return remote(here, here, k.pass_send.at[b, i], k.ag_recv.at[b, i], bucket=sibling)

    def add_product(b, u):
        value = dot(k.pay[0, :, columns(b)], block(b, u))
        for i, c in enumerate(members[u]):
            k.grad[c] += value[:, i * wide : (i + 1) * wide]

    def lent_product(b, c):
        return dot(k.lent[b - 2 * away], k.blocks[b, c])

    def setup():
        lend_start(range(1, 5))


        def turn(q, _):
            k.pay_out[q] = k.pay[0, :, columns(q * 2 + 1 - core)].T
            turned(q).start()
            k.pay_t[q, core] = k.pay[0, :, columns(q * 2 + core)].T
            return 0

        lax.fori_loop(0, pairs, turn, 0)
        for r in range(n_r - 1):
            place = order(lax.broadcasted_iota(jnp.int32, (seqs, half), 0))
            one_hot = (place == k.pred_ref[r : r + 1, :]).astype(f32).astype(bf16)
            k.gather[r] = one_hot
            k.spread[r] = one_hot.T

        @pl.when(me_r == 0)
        def _():
            for s in range(n_r):
                k.back_in[s, 1] = jnp.full((part, half), 65535 - shift_code, jnp.int32).astype(
                    jnp.int16
                )

        load_x.wait()
        value = picked(split3(exact(k.xv[0], k.mixer[...])), k.to_outer[...], nt)
        k.f_x[...] = value
        for i in range(3):
            k.mix_p[i] = dot(k.mix_p[i], k.to_outer[...], nt).astype(bf16)

    def turned(q):
        return remote(
            k.pay_out.at[q],
            k.pay_t.at[q, core],
            k.turn_send.at[q],
            k.turn_recv.at[q],
            bucket=sibling,
        )


    def row_copy(d, u):
        s = (me_r + d) % n_r
        return remote(
            k.row_q.at[s, quarters[u]],
            k.row_in.at[me_r, quarters[u]],
            k.row_send.at[s, u],
            k.row_recv.at[me_r, u],
            round=s,
        )

    def row_arrival(d, u):
        s = (me_r + d) % n_r
        h, lanes = spans[u]
        here = k.row_in.at[s, quarters[u]]
        remote(here, here, k.row_send.at[s, u], k.row_recv.at[s, u], round=s).wait_recv()
        k.rows_f[s, h, :, lanes] = decode(here)

    def finish(u):
        for c in members[u]:
            squares = k.grad[c]
            squares = jnp.sum((squares * squares).reshape(rows // 8, 8, wide), axis=0)
            if c == 0:
                k.sq_mine[...] = squares
            else:
                k.sq_mine[...] += squares
        if u == 2:
            k.sq_all[me] = jnp.sum(k.sq_mine[...], axis=0, keepdims=True)
            for dr, db in others:
                square_copy(dr, db).start()
        for d in range(1, n_r):
            s = (me_r + d) % n_r
            for c in members[u]:
                encode(k.grad[c, rows_of(s), :], k.row_q.at[s, c])
            row_copy(d, u).start()
        for c in members[u]:
            h, lanes = c // 2, slice(c % 2 * wide, c % 2 * wide + wide)
            k.rows_f[me_r, h, :, lanes] = k.grad[c, rows_of(me_r), :]

    me = me_r * n_b + me_b

    def square_copy(dr, db):
        here = k.sq_all.at[me]
        return remote(
            here,
            here,
            k.sq_send.at[dr * n_b + db],
            k.sq_recv.at[me],
            round=(me_r + dr) % n_r,
            bucket=(me_b + db) % n_b,
        )

    def square_arrival(dr, db):
        s = (me_r + dr) % n_r * n_b + (me_b + db) % n_b
        here = k.sq_all.at[s]
        return remote(here, here, k.sq_send.at[0], k.sq_recv.at[s], bucket=sibling)

    others = [(dr, db) for dr in range(n_r) for db in range(n_b) if dr or db]
    others.sort(key=lambda o: -min(o[1], n_b - o[1]))

    def back_copy(r, i):
        return remote(
            k.back_q.at[r, i],
            k.back_in.at[me_r, i],
            k.back_send.at[r, i],
            k.back_recv.at[me_r, i],
            round=r,
        )

    def back_arrival(s):
        for i in range(2):

            def wait():
                here = k.back_in.at[s, i]
                remote(
                    here, here, k.back_send.at[s, i], k.back_recv.at[s, i], round=s
                ).wait_recv()

            if i == 0:
                wait()
            else:
                pl.when(me_r > 0)(wait)

    def back_drain(s):
        back_copy(s, 0).wait_send()

        @pl.when(s > 0)
        def _():
            back_copy(s, 1).wait_send()

    def give_back(r, i, value):
        code = jnp.floor(value * top_code + 0.5).astype(jnp.int32) - shift_code
        k.back_q[r, i] = code.astype(jnp.int16)

        @pl.when(me_r != r)
        def _():
            back_copy(r, i).start()

        @pl.when(me_r == r)
        def _():
            k.back_in[me_r, i] = k.back_q[r, i]

    def prox(sign, factor, after_scale=None):
        for u in range(2):
            for d in range(1, n_r):
                row_arrival(d, u)
        for d in range(1, n_r):
            row_arrival(d, 2)
        for dr, db in others:
            square_arrival(dr, db).wait_recv()
        squares = jnp.sum(k.sq_all[...], axis=0)
        squares = jnp.sum(squares, axis=1, keepdims=True)
        scale = sign / (factor * jnp.sqrt(squares / total_count + epsilon))

        if after_scale is not None:
            after_scale()
        carried = None
        for r in reversed(range(n_r)):
            norms = []
            evens = []
            for h in range(2):
                values = k.rows_f[r, h] * scale
                if carried is not None:
                    values = values + carried[:, h * half : (h + 1) * half]
                even, odd = values[:, :wide], values[:, wide:]
                small = jnp.exp(-jnp.abs(even - odd))
                larger = 1.0 / (1.0 + small)
                smaller = small * larger
                ahead = even >= odd
                evens.append(jnp.where(ahead, larger, smaller))
                k.share[r, h, :, :wide] = evens[h]
                k.share[r, h, :, wide:] = jnp.where(ahead, smaller, larger)
                norms.append(jnp.maximum(even, odd) + jnp.log(1.0 + small))
            give_back(r, 0, jnp.concatenate(evens, axis=1))
            if r > 0:
                norm = jnp.concatenate(norms, axis=1)
                carried = picked(split3(norm), k.spread[r - 1])

        mass = jnp.concatenate([k.share[0, 0], k.share[0, 1]], axis=1)
        for r in range(1, n_r):
            parent = picked(split3(mass), k.gather[r - 1])
            give_back(r, 1, parent)
            above = [parent[:, h * wide : (h + 1) * wide] for h in (0, 0, 1, 1)]
            shares = jnp.concatenate([k.share[r, 0], k.share[r, 1]], axis=1)
            mass = shares * jnp.concatenate(above, axis=1)

    def prox_drain():
        for d in range(1, n_r):
            for u in range(3):
                row_copy(d, u).wait_send()
            back_drain((me_r + d) % n_r)
        for dr, db in others:
            square_copy(dr, db).wait_send()

    def pieces(s):
        share, parent = [
            (k.back_in[s, i].astype(jnp.int32) + shift_code).astype(f32) * (1.0 / top_code)
            for i in range(2)
        ]
        even = parent * share
        odd = parent - even
        both = (even[:, :wide], odd[:, :wide], even[:, wide:], odd[:, wide:])
        whole = jnp.concatenate(both, axis=1)
        return split3(whole)[:2]

    def mixed_part(s, state, weight, dims):
        value = mix(pieces(s), [k.mix_p[i] for i in range(3)], dims)
        value = (1.0 - weight) * state[rows_of(s), :] + weight * value
        state[rows_of(s), :] = value
        return value

    def add_best(out, s, share):
        best = picked(pieces(s), k.to_outer[...])
        out[0, rows_of(s), :] += share * best


    def mixed_copy(s):
        here = k.mixed.at[core, :, rows_of(s), :]
        return remote(here, here, k.mx_send.at[s], k.mx_recv.at[core, s], bucket=sibling)

    def mixed_arrival(s):
        here = k.mixed.at[1 - core, :, rows_of(s), :]
        return remote(here, here, k.mx_send.at[s], k.mx_recv.at[1 - core, s], bucket=sibling)

    def raw_copy(n):
        return remote(
            k.mixed.at[core, n],
            k.mixed.at[2 + core, n],
            k.raw_send.at[n],
            k.raw_recv.at[core, n],
            bucket=me_b - outward,
        )

    def raw_pass(n):
        here = k.mixed.at[2 + core, n]
        return remote(here, here, k.raw_send.at[n], k.raw_recv.at[core, n], bucket=sibling)

    def raw_arrival(source, n):
        here = k.mixed.at[2 + source, n]
        remote(
            here, here, k.raw_send.at[n], k.raw_recv.at[source, n], bucket=sibling
        ).wait_recv()

    def partial(q, n):
        return dot(k.pay_t[q, 0], k.mixed[0, n]) + dot(k.pay_t[q, 1], k.mixed[1, n])

    def lent_partial(j, n):
        return dot(k.lent_t[j, 0], k.mixed[2, n]) + dot(k.lent_t[j, 1], k.mixed[3, n])

    def sum_copy(kind, n, step):
        return remote(
            k.sum_out.at[kind, n],
            k.sum_in.at[kind, n],
            k.sum_send.at[kind, n],
            k.sum_recv.at[kind, n],
            bucket=me_b + step,
        )

    def sum_arrival(kind, n):
        here = k.sum_in.at[kind, n]
        remote(
            here, here, k.sum_send.at[kind, n], k.sum_recv.at[kind, n], bucket=sibling
        ).wait_recv()
        return decode(here)

    def sums_of_end(index):
        def lend_sum(n, _):
            k.work[...] = partial(facing - outward // 2, n)
            encode(k.work[...], k.sum_out.at[4, n])
            sum_copy(4, n, -outward).start()
            return 0

        @pl.when(index == 0)
        def _():
            lax.fori_loop(0, 4, lend_sum, 0)

        def give(n, _):
            k.work[...] = partial(facing, n)
            encode(k.work[...], k.sum_out.at[3, n])
            sum_copy(3, n, -outward).start()
            return 0

        lax.fori_loop(0, 4, give, 0)

    def sums_of_inner(index):
        def give(i, _):
            n = i % 4

            @pl.when(i < 4)
            def _():
                raw_arrival(core, n)
                raw_pass(n).start()

            q = jnp.where(i < 4, far_end, facing)
            k.work[...] = partial(q, n)

            @pl.when(i < 4)
            def _():
                raw_arrival(1 - core, n)

            @pl.when((i < 4) | (index == 1))
            def _():
                k.work[...] += lent_partial(q - away, n)

            @pl.when((i >= 4) & (index == 0))
            def _():
                k.work[...] += sum_arrival(4, n)

            encode(k.work[...], k.sum_out.at[i // 4, n])
            sum_copy(i // 4, n, -outward).start()

            @pl.when((i >= 2) & (i < 6))
            def _():
                k.work[...] = partial(end_chip, i - 2)
                k.work[...] += sum_arrival(0, i - 2)
                encode(k.work[...], k.sum_out.at[2, i - 2])
                sum_copy(2, i - 2, outward).start()

            return 0

        lax.fori_loop(0, 8, give, 0)

    def sums_drain(index):
        @pl.when(inner)
        def _():
            for n in range(4):
                raw_pass(n).wait_send()
                sum_copy(0, n, -outward).wait_send()
                sum_copy(1, n, -outward).wait_send()
                sum_copy(2, n, outward).wait_send()

        @pl.when(jnp.logical_not(inner))
        def _():
            for n in range(4):
                raw_copy(n).wait_send()
                sum_copy(3, n, -outward).wait_send()

                @pl.when(index == 0)
                def _():
                    sum_copy(4, n, -outward).wait_send()

    def out_copy(i, s):
        here, there = ((k.xo_ref, k.x_out), (k.yo_ref, k.y_out))[i]
        return pltpu.make_async_copy(
            here.at[:, rows_of(s)], there.at[:, rows_of(s)], k.out_sem.at[i, s]
        )

    def step(index, _):
        weight = 2.0 / (index.astype(f32) + 3.0)

        @pl.when(index == 0)
        def _():
            setup()

        first = -outward
        second = jnp.where(inner, outward, -2 * outward)
        far = jnp.where(inner, -2 * outward, -3 * outward)

        for u in range(3):
            value = dot(k.pay[0, :, columns(me_b)], block(me_b, u))
            for i, c in enumerate(members[u]):
                k.grad[c] = value[:, i * wide : (i + 1) * wide]
        by_parts(sibling)
        for u in range(2 + 1):
            add_product(sibling, u)

        @pl.when(index == 0)
        def _():
            for q in range(pairs):
                turned(q).wait()
            k.xo_ref[...] = (1.0 - weights[0]) * (1.0 - weights[1]) * k.xv[...]
            k.yo_ref[...] = (1.0 - weights[0]) * (1.0 - weights[1]) * k.yv[...]

        @pl.when(index == 1)
        def _():
            for s in range(n_r):
                add_best(k.yo_ref, s, weights[0] * (1.0 - weights[1]))

        def both(offset):
            for u in range(3):
                add_product(me_b + offset, u)
            by_whole(sibling + offset)
            for u in range(3):
                add_product(sibling + offset, u)

        plain = index == 0
        b = me_b + first
        for s in range(n_r):
            arrived(part_of(b, s), b, s)

            @pl.when(inner & plain)
            def _():
                go_on(part_of(b, s), b, s, outward).start()

        pass_on(k.blocks.at[b], b, 0).start()
        b2 = me_b + second

        @pl.when(inner)
        def _():
            by_parts(b2)
            for c in range(4):
                go_on(unit_of(b2, c), b2, c, -outward).start()
            pass_on(k.blocks.at[b2], b2, 0).start()

        both(first)

        @pl.when(inner & jnp.logical_not(plain))
        def _():
            wait_lent(1)
            for c in range(4):
                k.early[c] = lent_product(b, c) + lent_product(sibling + first, c)

        @pl.when(jnp.logical_not(inner) & plain)
        def _():
            by_parts(b2)
            pass_on(k.blocks.at[b2], b2, 0).start()

        @pl.when(inner | plain)
        def _():
            both(second)

        b3 = me_b + far
        for c in range(4):

            @pl.when(inner | plain)
            def _():
                by_unit(b3, c)

                @pl.when(inner & plain)
                def _():
                    go_on(unit_of(b3, c), b3, c, outward).start()

                pass_on(unit_of(b3, c), b3, c).start()

                @pl.when(plain)
                def _():
                    k.grad[c] += dot(k.pay[0, :, columns(b3)], k.blocks[b3, c])

                by_unit(sibling + far, c)

                @pl.when(jnp.logical_not(plain))
                def _():
                    k.early[c] += lent_product(b3, c) + lent_product(sibling + far, c)
                    encode(k.early[c], k.sum_out.at[5, c])
                    sum_copy(5, c, outward).start()
                    k.grad[c] += dot(k.pay[0, :, columns(b3)], k.blocks[b3, c])

                k.grad[c] += dot(k.pay[0, :, columns(sibling + far)], k.blocks[sibling + far, c])

            @pl.when(jnp.logical_not(inner | plain))
            def _():
                k.grad[c] += sum_arrival(5, c)

            if c > 0:
                finish(c - 1)

        @pl.when(inner & jnp.logical_not(plain))
        def _():
            turn_lent(1)

        @pl.when(inner & plain)
        def _():
            for c in range(4):
                go_on(part_of(b, c), b, c, outward).wait_send()
                go_on(unit_of(b3, c), b3, c, outward).wait_send()

        @pl.when(inner)
        def _():
            for c in range(4):
                go_on(unit_of(b2, c), b2, c, -outward).wait_send()

        pass_on(k.blocks.at[b], b, 0).wait_send()

        @pl.when(inner | plain)
        def _():
            pass_on(k.blocks.at[b2], b2, 0).wait_send()
            for c in range(4):
                pass_on(unit_of(b3, c), b3, c).wait_send()

        @pl.when(inner & jnp.logical_not(plain))
        def _():
            for c in range(4):
                sum_copy(5, c, outward).wait_send()

        @pl.when(jnp.logical_not(inner | plain))
        def _():
            for turn in range(8):
                lend(turn).wait_send()

        for s in range(n_r):
            own_drain(s)

        def lend_more(turns):
            @pl.when(index == 0)
            def _():
                lend_start(turns)

        prox(-1.0, smooth_x, functools.partial(lend_more, range(5, 7)))
        for d in range(n_r):
            s = (me_r + d) % n_r
            if d > 0:
                back_arrival(s)
            value = mixed_part(s, k.f_x, weight, nn).astype(bf16)
            for c in range(4):
                k.mixed[core, c, rows_of(s), :] = value[:, c * wide : (c + 1) * wide]
            mixed_copy(s).start()

        @pl.when(jnp.logical_not(inner))
        def _():
            for n in range(4):
                raw_copy(n).start()

        for d in range(n_r):
            mixed_arrival((me_r + d) % n_r).wait_recv()

        @pl.when(inner)
        def _():
            @pl.when(index == 0)
            def _():
                wait_lent(0)
                turn_lent(0)

            sums_of_inner(index)

        @pl.when(jnp.logical_not(inner))
        def _():
            sums_of_end(index)

        prox_drain()
        for s in range(n_r):
            mixed_copy(s).wait_send()
        share = jnp.where(index == 0, weights[0] * (1.0 - weights[1]), weights[1])
        for s in range(n_r):
            add_best(k.xo_ref, s, share)

            @pl.when(index == 1)
            def _():
                out_copy(0, s).start()

        for n in range(4):
            k.grad[n] = partial(pair, n)
        for u in range(3):
            for n in members[u]:

                @pl.when(inner)
                def _():
                    k.grad[n] += sum_arrival(3, n)
                    k.grad[n] += sum_arrival(1, n)

                @pl.when(jnp.logical_not(inner))
                def _():
                    k.grad[n] += sum_arrival(2, n)

            finish(u)
        sums_drain(index)

        prox(1.0, smooth_y, functools.partial(lend_more, range(7, 8)))
        for d in range(n_r):
            s = (me_r + d) % n_r
            if d > 0:
                back_arrival(s)

            @pl.when(index == 0)
            def _():
                set_own(s, mixed_part(s, k.f_y, weight, nt))
                own_start(s)

            @pl.when(index == 1)
            def _():
                add_best(k.yo_ref, s, weights[1])
                out_copy(1, s).start()

        prox_drain()
        return 0

    lax.fori_loop(0, 2, step, 0)
    for i in range(2):
        for s in range(n_r):
            out_copy(i, s).wait()


def place_kernel(x_in, y_in, x_out, y_out):
    x_out[...] = x_in[...]
    y_out[...] = y_in[...]


def line_body(x_start, y_start, bucket_payoff, column_blocks, public_coef, predecessor_sequences):
    n_r = lax.axis_size("round")
    n_b = lax.axis_size("bucket")
    _, rows, seqs = x_start.shape
    half = seqs // 2
    part = rows // n_r
    pairs = n_b // 2
    f32, bf16, i16 = jnp.float32, jnp.bfloat16, jnp.int16
    vmem = pl.BlockSpec(memory_space=pltpu.VMEM)
    smem = pl.BlockSpec(memory_space=pltpu.SMEM)
    hbm = pl.BlockSpec(memory_space=pl.ANY)
    dma = pltpu.SemaphoreType.DMA
    scratch = dict(
        xv=pltpu.VMEM((1, rows, seqs), f32),
        yv=pltpu.VMEM((1, rows, seqs), f32),
        xo_ref=pltpu.VMEM((1, rows, seqs), f32),
        yo_ref=pltpu.VMEM((1, rows, seqs), f32),
        pay=pltpu.VMEM((1, rows, n_b * rows), bf16),
        pay_t=pltpu.VMEM((pairs, 2, rows, rows), bf16),
        pay_out=pltpu.VMEM((pairs, rows, rows), bf16),
        blocks=pltpu.VMEM((n_b, 4, rows, half // 2), bf16),
        mixed=pltpu.VMEM((4, 4, rows, half // 2), bf16),
        mixer=pltpu.VMEM((seqs, seqs), f32),
        mix_p=pltpu.VMEM((3, seqs, seqs), bf16),
        to_outer=pltpu.VMEM((seqs, seqs), bf16),
        gather=pltpu.VMEM((n_r - 1, seqs, half), bf16),
        spread=pltpu.VMEM((n_r - 1, half, seqs), bf16),
        f_x=pltpu.VMEM((rows, seqs), f32),
        f_y=pltpu.VMEM((rows, seqs), f32),
        grad=pltpu.VMEM((4, rows, half // 2), f32),
        work=pltpu.VMEM((rows, half // 2), f32),
        early=pltpu.VMEM((4, rows, half // 2), f32),
        lent=pltpu.VMEM((4, rows, rows), bf16),
        lent_t=pltpu.VMEM((2, 2, rows, rows), bf16),
        sum_out=pltpu.VMEM((6, 4, rows + 16, half // 2), i16),
        sum_in=pltpu.VMEM((6, 4, rows + 16, half // 2), i16),
        row_q=pltpu.VMEM((n_r, 4, part + 16, half // 2), i16),
        row_in=pltpu.VMEM((n_r, 4, part + 16, half // 2), i16),
        rows_f=pltpu.VMEM((n_r, 2, part, half), f32),
        share=pltpu.VMEM((n_r, 2, part, half), f32),
        back_q=pltpu.VMEM((n_r, 2, part, half), i16),
        back_in=pltpu.VMEM((n_r, 2, part, half), i16),
        sq_mine=pltpu.VMEM((8, 128), f32),
        sq_all=pltpu.VMEM((n_r * n_b, 1, 128), f32),
        load_sem=dma((3,)),
        out_sem=dma((2, n_r)),
        turn_send=dma((pairs,)),
        turn_recv=dma((pairs,)),
        ag_send=dma((3, n_r)),
        ag_recv=dma((n_b, n_r)),
        line_send=dma((n_b, n_r)),
        pass_send=dma((n_b, 4)),
        mx_send=dma((n_r,)),
        mx_recv=dma((2, n_r)),
        sum_send=dma((6, 4)),
        sum_recv=dma((6, 4)),
        lend_send=dma((8,)),
        lend_recv=dma((8,)),
        swap_send=dma((2,)),
        swap_recv=dma((2,)),
        raw_send=dma((4,)),
        raw_recv=dma((2, 4)),
        row_send=dma((n_r, 3)),
        row_recv=dma((n_r, 3)),
        back_send=dma((n_r, 2)),
        back_recv=dma((n_r, 2)),
        sq_send=dma((n_r * n_b,)),
        sq_recv=dma((n_r * n_b,)),
    )
    names = ["x_hbm", "y_hbm", "pay_hbm", "col_ref", "coef_ref", "pred_ref", "x_out", "y_out"]
    names += list(scratch)
    found = pl.pallas_call(
        functools.partial(line_kernel, names, n_r, n_b),
        out_shape=[jax.ShapeDtypeStruct(x_start.shape, f32)] * 2,
        in_specs=[hbm, hbm, hbm, smem, vmem, vmem],
        out_specs=[hbm, hbm],
        scratch_shapes=list(scratch.values()),
        compiler_params=pltpu.CompilerParams(
            collective_id=0, has_side_effects=True, vmem_limit_bytes=60 * 1024 * 1024
        ),
    )(
        x_start,
        y_start,
        bucket_payoff,
        jnp.transpose(column_blocks, (2, 0, 1)),
        public_coef,
        predecessor_sequences,
    )
    block = pl.BlockSpec((1, rows // 2, seqs), lambda i: (0, i, 0))
    return pl.pallas_call(
        place_kernel,
        grid=(2,),
        out_shape=[jax.ShapeDtypeStruct(x_start.shape, f32)] * 2,
        in_specs=[block, block],
        out_specs=[block, block],
    )(*found)


def plain_kernel(
    n_r,
    n_b,
    x_ref,
    y_ref,
    pay_ref,
    col_ref,
    coef_ref,
    pred_ref,
    xo_ref,
    yo_ref,
    xs,
    ys,
    mixer,
    gather,
    pay_t,
    blocks,
    mixed,
    grad,
    sib_out,
    sib_in,
    far_out,
    far_in,
    sq_b,
    sq_r,
    rows_in,
    score,
    norm,
    mass,
    back_in,
    far_q,
    far_s,
    far_q_in,
    far_s_in,
    row_q,
    row_s,
    row_q_in,
    row_s_in,
    back_q,
    back_s,
    back_q_in,
    back_s_in,
    ag_send,
    ag_recv,
    fw_send,
    line_send,
    sib_send,
    sib_recv,
    far_send,
    far_recv,
    sqb_send,
    sqb_recv,
    sqr_send,
    sqr_recv,
    row_send,
    row_recv,
    back_send,
    back_recv,
    far_s_send,
    far_s_recv,
    row_s_send,
    row_s_recv,
    back_s_send,
    back_s_recv,
):
    rows, seqs = xs.shape
    half = seqs // 2
    part = rows // n_r
    pairs = n_b // 2
    me_r = lax.axis_index("round")
    me_b = lax.axis_index("bucket")
    pair = me_b // 2
    core = me_b % 2
    sibling = pair * 2 + 1 - core
    total_count = n_r * n_b * rows * seqs

    def remote(src, dst, send, recv, **where):
        return pltpu.make_async_remote_copy(
            src_ref=src,
            dst_ref=dst,
            send_sem=send,
            recv_sem=recv,
            device_id=where,
            device_id_type=pl.DeviceIdType.MESH,
        )

    barrier = pltpu.get_barrier_semaphore()
    for d in range(1, n_b):
        pl.semaphore_signal(
            barrier,
            inc=1,
            device_id={"bucket": (me_b + d) % n_b},
            device_id_type=pl.DeviceIdType.MESH,
        )
    for d in range(1, n_r):
        pl.semaphore_signal(
            barrier,
            inc=1,
            device_id={"round": (me_r + d) % n_r},
            device_id_type=pl.DeviceIdType.MESH,
        )
    pl.semaphore_wait(barrier, n_b + n_r - 2)

    def order(i):
        return jnp.where(i < half, 2 * i, 2 * (i - half) + 1)

    down = lax.broadcasted_iota(jnp.int32, (seqs, seqs), 0)
    across = lax.broadcasted_iota(jnp.int32, (seqs, seqs), 1)
    to_inner = (down == order(across)).astype(jnp.float32)
    to_outer = (order(down) == across).astype(jnp.float32)

    tiles, per_row, tile, _ = coef_ref.shape[1:]
    for m in range(tiles):
        for c in range(tiles):
            value = jnp.zeros((tile, tile), jnp.float32)
            for t in range(per_row):
                value = value + jnp.where(col_ref[0, m, t] == c, coef_ref[0, m, t], 0.0)
            mixer[m * tile : (m + 1) * tile, c * tile : (c + 1) * tile] = value
    mixer[...] = exact(to_outer, exact(mixer[...], to_inner))
    ys[...] = exact(y_ref[0], to_inner)
    for r in range(n_r - 1):
        place = order(lax.broadcasted_iota(jnp.int32, (seqs, half), 0))
        gather[r] = (place == pred_ref[r : r + 1, :]).astype(jnp.float32)

    def columns(j):
        return pl.ds(pl.multiple_of(j * rows, rows), rows)

    def coded(value, code_ref, scale_ref):
        top = jnp.max(jnp.abs(value), axis=0, keepdims=True)
        unit = jnp.maximum(top, 1e-30) / 32767.0
        code = jnp.floor(value * (1.0 / unit) + 0.5)
        code_ref[...] = code.astype(jnp.int32).astype(jnp.int16)
        scale_ref[...] = jnp.broadcast_to(unit, scale_ref.shape)

    def decoded(code_ref, scale_ref):
        return code_ref[...].astype(jnp.int32).astype(jnp.float32) * scale_ref[0:1, :]

    def prox(state, sign, factor, weight, short):
        def row_copy(d):
            s = (me_r + d) % n_r
            here = grad.at[pl.ds(pl.multiple_of(s * part, part), part)]
            if not short:
                return [
                    remote(here, rows_in.at[me_r], row_send.at[s], row_recv.at[me_r], round=s)
                ]
            return [
                remote(
                    row_q.at[s], row_q_in.at[me_r], row_send.at[s], row_recv.at[me_r], round=s
                ),
                remote(
                    row_s.at[s], row_s_in.at[me_r], row_s_send.at[s], row_s_recv.at[me_r], round=s
                ),
            ]

        def row_arrival(d):
            s = (me_r + d) % n_r
            if not short:
                return [
                    remote(rows_in.at[s], rows_in.at[s], row_send.at[s], row_recv.at[s], round=s)
                ]
            return [
                remote(row_q_in.at[s], row_q_in.at[s], row_send.at[s], row_recv.at[s], round=s),
                remote(
                    row_s_in.at[s], row_s_in.at[s], row_s_send.at[s], row_s_recv.at[s], round=s
                ),
            ]

        for d in range(1, n_r):
            if short:
                s = (me_r + d) % n_r
                here = pl.ds(pl.multiple_of(s * part, part), part)
                coded(grad[here, :], row_q.at[s], row_s.at[s])
            for copy in row_copy(d):
                copy.start()
        squares = grad[...]
        squares = jnp.sum((squares * squares).reshape(rows // 8, 8, seqs), axis=0)
        squares = sum(squares[:, i * 128 : (i + 1) * 128] for i in range(seqs // 128))
        sq_b[me_b] = squares

        def sqb_copy(d):
            s = (me_b + d) % n_b
            return remote(
                sq_b.at[me_b], sq_b.at[me_b], sqb_send.at[d], sqb_recv.at[me_b], bucket=s
            )

        def sqb_arrival(d):
            s = (me_b + d) % n_b
            return remote(sq_b.at[s], sq_b.at[s], sqb_send.at[d], sqb_recv.at[s], bucket=s)

        for d in range(1, n_b):
            sqb_copy(d).start()
        rows_in[me_r] = grad[pl.ds(pl.multiple_of(me_r * part, part), part), :]
        for d in range(1, n_b):
            sqb_arrival(d).wait_recv()
        sq_r[me_r] = jnp.sum(sq_b[...], axis=0)

        def sqr_copy(d):
            s = (me_r + d) % n_r
            return remote(sq_r.at[me_r], sq_r.at[me_r], sqr_send.at[d], sqr_recv.at[me_r], round=s)

        def sqr_arrival(d):
            s = (me_r + d) % n_r
            return remote(sq_r.at[s], sq_r.at[s], sqr_send.at[d], sqr_recv.at[s], round=s)

        for d in range(1, n_r):
            sqr_copy(d).start()
        for d in range(1, n_r):
            sqr_arrival(d).wait_recv()
        squares = jnp.sum(jnp.sum(sq_r[...], axis=0), axis=0, keepdims=True)
        squares = jnp.sum(squares, axis=1, keepdims=True)
        scale = sign / (factor * jnp.sqrt(squares / total_count + epsilon))
        for d in range(1, n_r):
            for copy in row_arrival(d):
                copy.wait_recv()
            if short:
                s = (me_r + d) % n_r
                rows_in[s] = decoded(row_q_in.at[s], row_s_in.at[s])

        for r in reversed(range(n_r)):
            values = rows_in[r] * scale
            if r < n_r - 1:
                values = values + exact(norm[r + 1], gather[r], nt)
            score[r] = values
            even, odd = values[:, :half], values[:, half:]
            larger = jnp.maximum(even, odd)
            norm[r] = larger + jnp.log(jnp.exp(even - larger) + jnp.exp(odd - larger))

        def back_copy(r):
            if not short:
                return [
                    remote(
                        mass.at[r], back_in.at[me_r], back_send.at[r], back_recv.at[me_r], round=r
                    )
                ]
            return [
                remote(
                    back_q.at[r], back_q_in.at[me_r], back_send.at[r], back_recv.at[me_r], round=r
                ),
                remote(
                    back_s.at[r],
                    back_s_in.at[me_r],
                    back_s_send.at[r],
                    back_s_recv.at[me_r],
                    round=r,
                ),
            ]

        def back_arrival(s):
            if not short:
                return [
                    remote(
                        back_in.at[s], back_in.at[s], back_send.at[s], back_recv.at[s], round=s
                    )
                ]
            return [
                remote(
                    back_q_in.at[s], back_q_in.at[s], back_send.at[s], back_recv.at[s], round=s
                ),
                remote(
                    back_s_in.at[s], back_s_in.at[s], back_s_send.at[s], back_s_recv.at[s], round=s
                ),
            ]

        for r in range(n_r):
            even = jnp.exp(score[r, :, :half] - norm[r])
            odd = jnp.exp(score[r, :, half:] - norm[r])
            if r > 0:
                parent = exact(mass[r - 1], gather[r - 1])
                even = parent * even
                odd = parent * odd
            mass[r, :, :half] = even
            mass[r, :, half:] = odd

            @pl.when(me_r != r)
            def _():
                if short:
                    coded(mass[r], back_q.at[r], back_s.at[r])
                for copy in back_copy(r):
                    copy.start()

        def update(s, best):
            here = pl.ds(pl.multiple_of(s * part, part), part)
            state[here, :] = (1.0 - weight) * state[here, :] + weight * best

        update(me_r, mass[me_r])
        for d in range(1, n_r):
            s = (me_r + d) % n_r
            for copy in back_arrival(s):
                copy.wait_recv()
            if short:
                update(s, decoded(back_q_in.at[s], back_s_in.at[s]))
            else:
                update(s, back_in[s])
        for d in range(1, n_r):
            for copy in row_copy(d) + back_copy((me_r + d) % n_r):
                copy.wait_send()
            sqr_copy(d).wait_send()
        for d in range(1, n_b):
            sqb_copy(d).wait_send()

    def step(index, _):
        weight = 2.0 / (index.astype(jnp.float32) + 3.0)
        short = False

        blocks[me_b] = exact(ys[...], mixer[...], nt).astype(jnp.bfloat16)

        def own_copy(kind):
            target = (sibling, me_b + 2, me_b - 2)[kind]
            return remote(
                blocks.at[me_b], blocks.at[me_b], ag_send.at[kind], ag_recv.at[me_b], bucket=target
            )

        def go_on(b, d, step):
            return remote(
                blocks.at[b], blocks.at[b], line_send.at[d], ag_recv.at[b], bucket=me_b + step
            )

        def pass_on(b, d):
            return remote(blocks.at[b], blocks.at[b], fw_send.at[d], ag_recv.at[b], bucket=sibling)

        def arrival(b):
            return remote(
                blocks.at[b], blocks.at[b], ag_send.at[0], ag_recv.at[b], bucket=sibling
            )

        def product(b):
            return jnp.dot(
                pay_ref[0, :, columns(b)], blocks[b], preferred_element_type=jnp.float32
            )

        @pl.when(pair < pairs - 1)
        def _():
            own_copy(1).start()

        @pl.when(pair > 0)
        def _():
            own_copy(2).start()

        own_copy(0).start()
        @pl.when(index == 0)
        def _():
            xs[...] = exact(x_ref[0], to_inner)

            def turn(j, _):
                pay_t[columns(j), :] = pay_ref[0, :, columns(j)].T
                return 0

            lax.fori_loop(0, n_b, turn, 0)
        grad[...] = product(me_b)
        arrival(sibling).wait_recv()
        grad[...] += product(sibling)

        def take(d, _):
            left = me_b - 2 * d
            right = me_b + 2 * d

            @pl.when(pair >= d)
            def _():
                arrival(left).wait_recv()

                @pl.when(pair < pairs - 1)
                def _():
                    go_on(left, d, 2).start()

                pass_on(left, d).start()

            @pl.when(pair + d < pairs)
            def _():
                arrival(right).wait_recv()

                @pl.when(pair > 0)
                def _():
                    go_on(right, pairs + d, -2).start()

                pass_on(right, pairs + d).start()

            def use(b, other):
                grad[...] += product(b)
                arrival(other).wait_recv()
                grad[...] += product(other)

            @pl.when(pair >= d)
            def _():
                use(left, sibling - 2 * d)

            @pl.when(pair + d < pairs)
            def _():
                use(right, sibling + 2 * d)

            return 0

        lax.fori_loop(1, pairs, take, 0)

        def drain(d, _):
            left = me_b - 2 * d
            right = me_b + 2 * d

            @pl.when(pair >= d)
            def _():
                pass_on(left, d).wait_send()

                @pl.when(pair < pairs - 1)
                def _():
                    go_on(left, d, 2).wait_send()

            @pl.when(pair + d < pairs)
            def _():
                pass_on(right, pairs + d).wait_send()

                @pl.when(pair > 0)
                def _():
                    go_on(right, pairs + d, -2).wait_send()

            return 0

        lax.fori_loop(1, pairs, drain, 0)
        own_copy(0).wait_send()

        @pl.when(pair < pairs - 1)
        def _():
            own_copy(1).wait_send()

        @pl.when(pair > 0)
        def _():
            own_copy(2).wait_send()

        prox(xs, -1.0, smooth_x, weight, short)

        mixed[...] = exact(xs[...], mixer[...]).astype(jnp.bfloat16)

        def partial(b):
            return jnp.dot(pay_t[columns(b), :], mixed[...], preferred_element_type=jnp.float32)

        def sib_copy(q):
            return remote(
                sib_out.at[q], sib_in.at[q], sib_send.at[q], sib_recv.at[q], bucket=sibling
            )

        def far_copy(q, step, target):
            slot = q if step > 0 else pairs + q
            if not short:
                return [
                    remote(
                        far_out.at[q],
                        far_in.at[slot],
                        far_send.at[q],
                        far_recv.at[slot],
                        bucket=target,
                    )
                ]
            return [
                remote(
                    far_q.at[q],
                    far_q_in.at[slot],
                    far_send.at[q],
                    far_recv.at[slot],
                    bucket=target,
                ),
                remote(
                    far_s.at[q],
                    far_s_in.at[slot],
                    far_s_send.at[q],
                    far_s_recv.at[slot],
                    bucket=target,
                ),
            ]

        def far_value(q, step):
            slot = q if step > 0 else pairs + q
            for copy in far_copy(q, step, sibling):
                copy.wait_recv()
            if short:
                return decoded(far_q_in.at[slot], far_s_in.at[slot])
            return far_in[slot]

        def to_sibling(q):
            sib_out[q] = partial(q * 2 + 1 - core)
            sib_copy(q).start()

        def move(q, step):
            far_out[q] = partial(q * 2 + core)
            sib_copy(q).wait_recv()
            far_out[q] += sib_in[q]

            @pl.when(pair > 0 if step > 0 else pair < pairs - 1)
            def _():
                far_out[q] += far_value(q, step)

            if short:
                coded(far_out[q], far_q.at[q], far_s.at[q])
            for copy in far_copy(q, step, me_b + step):
                copy.start()

        def outward(right, left):
            def one(i, _):
                @pl.when(pair < pairs - 1 - i)
                def _():
                    right(pairs - 1 - i)

                @pl.when(pair > i)
                def _():
                    left(i)

                return 0

            lax.fori_loop(0, pairs - 1, one, 0)

        def far_done(q, step):
            for copy in far_copy(q, step, me_b + step):
                copy.wait_send()

        outward(to_sibling, to_sibling)
        outward(lambda q: move(q, 2), lambda q: move(q, -2))
        to_sibling(pair)
        grad[...] = partial(me_b)
        sib_copy(pair).wait_recv()
        grad[...] += sib_in[pair]

        @pl.when(pair > 0)
        def _():
            grad[...] += far_value(pair, 2)

        @pl.when(pair < pairs - 1)
        def _():
            grad[...] += far_value(pair, -2)

        outward(lambda q: far_done(q, 2), lambda q: far_done(q, -2))
        for q in range(pairs):
            sib_copy(q).wait_send()
        prox(ys, 1.0, smooth_y, weight, short)
        return 0

    lax.fori_loop(0, 2, step, 0)
    down = lax.broadcasted_iota(jnp.int32, (seqs, seqs), 0)
    across = lax.broadcasted_iota(jnp.int32, (seqs, seqs), 1)
    to_outer = (order(down) == across).astype(jnp.float32)
    xo_ref[0] = exact(xs[...], to_outer)
    yo_ref[0] = exact(ys[...], to_outer)


def plain_body(x_start, y_start, bucket_payoff, column_blocks, public_coef, predecessor_sequences):
    n_r = lax.axis_size("round")
    n_b = lax.axis_size("bucket")
    _, rows, seqs = x_start.shape
    part = rows // n_r
    pairs = n_b // 2
    f32, bf16 = jnp.float32, jnp.bfloat16
    vmem = pl.BlockSpec(memory_space=pltpu.VMEM)
    smem = pl.BlockSpec(memory_space=pltpu.SMEM)
    dma = pltpu.SemaphoreType.DMA
    return pl.pallas_call(
        functools.partial(plain_kernel, n_r, n_b),
        out_shape=[jax.ShapeDtypeStruct(x_start.shape, f32)] * 2,
        in_specs=[vmem, vmem, vmem, smem, vmem, vmem],
        out_specs=[vmem, vmem],
        scratch_shapes=[
            pltpu.VMEM((rows, seqs), f32),
            pltpu.VMEM((rows, seqs), f32),
            pltpu.VMEM((seqs, seqs), f32),
            pltpu.VMEM((n_r - 1, seqs, seqs // 2), f32),
            pltpu.VMEM((n_b * rows, rows), bf16),
            pltpu.VMEM((n_b, rows, seqs), bf16),
            pltpu.VMEM((rows, seqs), bf16),
            pltpu.VMEM((rows, seqs), f32),
            pltpu.VMEM((pairs, rows, seqs), f32),
            pltpu.VMEM((pairs, rows, seqs), f32),
            pltpu.VMEM((pairs, rows, seqs), f32),
            pltpu.VMEM((2 * pairs, rows, seqs), f32),
            pltpu.VMEM((n_b, 8, 128), f32),
            pltpu.VMEM((n_r, 8, 128), f32),
            pltpu.VMEM((n_r, part, seqs), f32),
            pltpu.VMEM((n_r, part, seqs), f32),
            pltpu.VMEM((n_r, part, seqs // 2), f32),
            pltpu.VMEM((n_r, part, seqs), f32),
            pltpu.VMEM((n_r, part, seqs), f32),
            pltpu.VMEM((16, 128), jnp.int16),
            pltpu.VMEM((pairs, 8, seqs), f32),
            pltpu.VMEM((16, 128), jnp.int16),
            pltpu.VMEM((2 * pairs, 8, seqs), f32),
            pltpu.VMEM((16, 128), jnp.int16),
            pltpu.VMEM((n_r, 8, seqs), f32),
            pltpu.VMEM((16, 128), jnp.int16),
            pltpu.VMEM((n_r, 8, seqs), f32),
            pltpu.VMEM((16, 128), jnp.int16),
            pltpu.VMEM((n_r, 8, seqs), f32),
            pltpu.VMEM((16, 128), jnp.int16),
            pltpu.VMEM((n_r, 8, seqs), f32),
            dma((3,)),
            dma((n_b,)),
            dma((2 * pairs,)),
            dma((2 * pairs,)),
            dma((pairs,)),
            dma((pairs,)),
            dma((pairs,)),
            dma((2 * pairs,)),
            dma((n_b,)),
            dma((n_b,)),
            dma((n_r,)),
            dma((n_r,)),
            dma((n_r,)),
            dma((n_r,)),
            dma((n_r,)),
            dma((n_r,)),
            dma((pairs,)),
            dma((2 * pairs,)),
            dma((n_r,)),
            dma((n_r,)),
            dma((n_r,)),
            dma((n_r,)),
        ],
        compiler_params=pltpu.CompilerParams(
            collective_id=0, has_side_effects=True, vmem_limit_bytes=60 * 1024 * 1024
        ),
    )(x_start, y_start, bucket_payoff, column_blocks, public_coef, predecessor_sequences)


def solution(mesh):
    in_specs = (
        P("round", "bucket", None),
        P("round", "bucket", None),
        P("round", "bucket", None),
        P("round", None, None),
        P("round", None, None, None, None),
        P(),
    )
    out_specs = (P("round", "bucket", None), P("round", "bucket", None))

    line = mesh.shape["round"] == 4 and mesh.shape["bucket"] == 8

    def run(*arrays):
        return tuple(
            jax.shard_map(
                line_body if line else plain_body, mesh=mesh, in_specs=in_specs, out_specs=out_specs, check_vma=False
            )(*arrays)
        )

    return run
```
